32 devices in a mesh: expert: 4 (over z), tensor: 4 (over y, x), rep: 2 (over core).
Axes of the slice: x: 2, y: 2, z: 4, core: 2. Of those that a mesh axis runs over, the one named last changes fastest.
Arguments:
- tokens: bfloat16 [8, 1024, 768], P(('expert', 'rep'), 'tensor'), may hold values from -16 to 16
- segments: int32 [8, 1024], P(('expert', 'rep')), may hold values from 0 to 2, as said below
- routes: int32 [8, 1024, 2], P(('expert', 'rep'), 'tensor'), may hold values from 0 to 63, all different within a row
- capacity: int32 [64], replicated, may hold values from 6 to 12, as said below
- cotangent: bfloat16 [8, 1024, 768], P(('expert', 'rep'), 'tensor'), may hold values from -6 to 6
- rel_table: bfloat16 [32, 12], P('expert', 'tensor'), may hold values from -4 to 4
- w_query: bfloat16 [768, 768], P('expert', 'tensor'), may hold values from -0.21875 to 0.21875
- w_key: bfloat16 [768, 768], P('expert', 'tensor'), may hold values from -0.21875 to 0.21875
- w_value: bfloat16 [768, 768], P('expert', 'tensor'), may hold values from -0.21875 to 0.21875
- w_attn_out: bfloat16 [768, 768], P('expert', 'tensor'), may hold values from -0.875 to 0.875
- gain_attn: bfloat16 [768], P('expert'), may hold values from 0.5 to 1.5
- gain_moe: bfloat16 [768], P('expert'), may hold values from 0.5 to 1.5
- w_router: bfloat16 [768, 64], P('expert'), may hold values from -0.15625 to 0.15625
- w_in: bfloat16 [64, 768, 3072], P('expert', None, 'tensor'), may hold values from -0.21875 to 0.21875
- w_out: bfloat16 [64, 3072, 768], P('expert', 'tensor'), may hold values from -0.109375 to 0.109375
Outputs:
- output: bfloat16 [8, 1024, 768], P(('expert', 'rep'), 'tensor')
- grad_tokens: float32 [8, 1024, 768], P(('expert', 'rep'), 'tensor')
- grad_table: float32 [32, 12], P('expert', 'tensor')
- grad_query: float32 [768, 768], P('expert', 'tensor')
- grad_key: float32 [768, 768], P('expert', 'tensor')
- grad_value: float32 [768, 768], P('expert', 'tensor')
- grad_attn_out: float32 [768, 768], P('expert', 'tensor')
- grad_gain_attn: float32 [768], P('expert')
- grad_gain_moe: float32 [768], P('expert')
- grad_router: float32 [768, 64], P('expert')
- grad_w_in: float32 [64, 768, 3072], P('expert', None, 'tensor')
- grad_w_out: float32 [64, 3072, 768], P('expert', 'tensor')
The draws below stay inside these ranges and needn't reach their ends.
Inputs may be any that keep to these rules, and one draw needn't show every extreme that they name: `segments`: segment numbers never fall along a sequence. Each sequence holds the tail of a document (fewer than 128 positions), one whole document that begins before position 128 and ends within the last 256 positions, and the head of another document. `routes`: the two experts of a token differ. `capacity`: some expert has all 12 slots.
All inputs are finite; a program needn't handle non-finite values.
Results may differ from the reference program's by a relative error of at most 0.025.
Values may be sent and summed in bfloat16 or wider, within the bound.
No kernel may reach another device: no remote copies, remote signals or barrier semaphores. Data moves between devices by JAX's collectives and lax.ppermute only.
A program may use at most 384 MiB of HBM per device.

```python
import jax
import jax.numpy as jnp
from jax import lax

D = 768
HEADS = 12
HEAD = 64
FF = 3072
EXPERTS = 64
BUCKETS = 32
TOK_DEV = 256
SEQ = 1024
SEQS = 8
CAP = 12


def draw_tokens(key, part):
    key = jax.random.fold_in(key, 37)
    base_key, size_key, channel_key, sign_key = jax.random.split(key, 4)
    base = jnp.clip(jax.random.normal(base_key, (SEQS, SEQ, D), jnp.float32), -4.0, 4.0)
    lower_end = 6.0
    magnitude = jax.random.uniform(size_key, (SEQS, SEQ, 1), jnp.float32, lower_end, 12.0)
    picked = jax.random.permutation(channel_key, D)[:2]
    signs = jnp.where(jax.random.randint(sign_key, (2,), 0, 2) == 0, -1.0, 1.0).astype(jnp.float32)
    columns = jnp.arange(D, dtype=jnp.int32)
    pattern = jnp.sum((columns[None, :] == picked[:, None]).astype(jnp.float32) * signs[:, None], axis=0)
    return (base + magnitude * pattern).astype(jnp.bfloat16)


def draw_segments(key, part):
    key = jax.random.fold_in(key, 11)
    first, second = jax.random.split(key, 2)
    half = max(TOK_DEV // 2, 2)
    start_big = jax.random.randint(first, (SEQS, 1), 1, half)
    start_last = jax.random.randint(second, (SEQS, 1), SEQ - TOK_DEV + 1, SEQ - half + 1)
    place = jnp.arange(SEQ, dtype=jnp.int32)[None, :]
    ids = (place >= start_big).astype(jnp.int32) + (place >= start_last).astype(jnp.int32)
    return ids.astype(jnp.int32)


def draw_capacity(key, part):
    key = jax.random.fold_in(key, 23)
    first, second = jax.random.split(key, 2)
    lowest = max(CAP // 2, 1)
    drawn = jax.random.randint(first, (EXPERTS,), lowest, CAP + 1)
    chosen = jax.random.randint(second, (), 0, EXPERTS)
    return jnp.where(jnp.arange(EXPERTS) == chosen, CAP, drawn).astype(jnp.int32)


def block_levels(own_key, dims, cuts, least, top_value):
    def one(dim, blocks):
        steps = jax.random.uniform(jax.random.fold_in(jax.random.fold_in(own_key, 6), dim), (blocks,), jnp.float32, least / len(cuts), top_value / len(cuts))
        return jnp.repeat(jnp.exp(steps), dims[dim] // blocks).reshape((-1,) + (1,) * (len(dims) - dim - 1))

    factor_of = one(*cuts[0])
    for cut in cuts[1:]:
        factor_of = factor_of * one(*cut)
    return factor_of


def distinct(own_key, rows, number_of, top, lift):
    order = jax.random.permutation(jax.random.fold_in(own_key, 1), number_of)
    pull = order
    for power in range(3):
        pull = pull * pull // number_of
    pull = pull * lift // number_of
    tickets = jax.random.randint(jax.random.fold_in(own_key, 2), (rows, number_of), 0, 4096) + pull
    fixed_rows = jax.random.permutation(jax.random.fold_in(own_key, 3), rows)[jnp.arange(number_of) % rows]
    tickets = jnp.where(jnp.arange(rows)[:, None] == fixed_rows[None, :], 1 << 14, tickets)
    merit = tickets * number_of + jnp.arange(number_of)
    return lax.top_k(merit.astype(jnp.int32), top)[1].astype(jnp.int32)


def bell_draw(rng, shape, deviation, bound, shards=(), kind=jnp.bfloat16):
    values = jax.random.normal(rng, shape, jnp.float32) * deviation
    if len(shards) > 0:
        values = block_levels(rng, shape, shards, -0.22, 0.18) * values
    return jnp.clip(values, min=-bound, max=bound).astype(kind)


def setup_inputs(seed: int = 0) -> dict:
    splits = jax.random.split(jax.random.key(seed), 16)
    return {
        "tokens": draw_tokens(jax.random.fold_in(splits[15], 71), 0),
        "segments": draw_segments(jax.random.fold_in(splits[15], 71), 0),
        "routes": distinct(splits[2], SEQS * SEQ, EXPERTS, 2, 256).reshape((SEQS, SEQ, 2)),
        "capacity": draw_capacity(jax.random.fold_in(splits[15], 71), 0),
        "cotangent": bell_draw(splits[4], (SEQS, SEQ, D), 1.0, 6.0, ((0, 8), (1, 4))),
        "rel_table": bell_draw(splits[5], (BUCKETS, HEADS), 1.0, 4.0, ((0, 4), (1, 4))),
        "w_query": bell_draw(splits[6], (D, HEADS * HEAD), D ** -0.5, 0.21875, ((0, 4), (1, 4))),
        "w_key": bell_draw(splits[7], (D, HEADS * HEAD), D ** -0.5, 0.21875, ((0, 4), (1, 4))),
        "w_value": bell_draw(splits[8], (D, HEADS * HEAD), D ** -0.5, 0.21875, ((0, 4), (1, 4))),
        "w_attn_out": bell_draw(splits[9], (D, HEADS * HEAD), (HEADS * HEAD // 16) ** -0.5, 0.875, ((0, 4), (1, 4))),
        "gain_attn": jnp.clip(1.0 + 0.1 * jax.random.normal(splits[10], (D,), jnp.float32), 0.5, 1.5).astype(jnp.bfloat16),
        "gain_moe": jnp.clip(1.0 + 0.1 * jax.random.normal(splits[11], (D,), jnp.float32), 0.5, 1.5).astype(jnp.bfloat16),
        "w_router": bell_draw(splits[12], (D, EXPERTS), (2 * D) ** -0.5, 0.15625, ((0, 4),)),
        "w_in": bell_draw(splits[13], (EXPERTS, D, FF), D ** -0.5, 0.21875, ((0, 4), (2, 4))),
        "w_out": bell_draw(splits[14], (EXPERTS, FF, D), FF ** -0.5, 0.109375, ((0, 4), (1, 4))),
    }


@jax.custom_vjp
def low(v):
    return lax.optimization_barrier(v.astype(jnp.bfloat16)).astype(jnp.float32)

@jax.custom_vjp
def low_back(v):
    return v

def low_keep(v):
    return (low(v), None)

def low_pass(kept, grad):
    return (grad,)

def back_keep(v):
    return (v, None)

def back_low(kept, grad):
    return (low(grad),)
low.defvjp(low_keep, low_pass)
low_back.defvjp(back_keep, back_low)
epsilon = 1e-06
score_scale = 0.125
masked_value = -1e+30
thresholds = (16, 19, 21, 24, 27, 31, 35, 40, 46, 52, 59, 67, 77, 87, 99, 113)
highest = lax.Precision.HIGHEST

def bucket_of(offset):
    total = jnp.clip(offset, 0, 15).astype(jnp.int32)
    for level in thresholds:
        total = total + (offset >= level).astype(jnp.int32)
    return total

def product(left, right):
    return jnp.dot(left, right, precision=highest, preferred_element_type=jnp.float32)

def sequence_layer(weights, capacity, rows, segment, route):
    table, w_query, w_key, w_value, w_attn, gain_attn, gain_moe, w_router, w_in, w_out = weights
    length = rows.shape[0]
    scale_one = lax.rsqrt(lax.optimization_barrier(jnp.mean(rows * rows, axis=-1, keepdims=True)) + epsilon)
    normed = low(rows * scale_one * gain_attn)
    query = low_back(low(product(normed, w_query))).reshape(length, HEADS, HEAD)
    keys = low_back(low(product(normed, w_key))).reshape(length, HEADS, HEAD)
    values = low_back(low(product(normed, w_value))).reshape(length, HEADS, HEAD)
    place = jnp.arange(length, dtype=jnp.int32)
    offset = place[:, None] - place[None, :]
    bias = jnp.transpose(table[bucket_of(offset)], (2, 0, 1))
    scores = jnp.einsum('qhd,khd->hqk', query, keys, precision=highest) * score_scale + bias
    scores = low_back(scores)
    allowed = (segment[:, None] == segment[None, :]) & (offset >= 0)
    scores = jnp.where(allowed[None], scores, masked_value)
    weights_low = low(jax.nn.softmax(scores, axis=-1))
    mixed = jnp.einsum('hqk,khd->qhd', weights_low, values, precision=highest).reshape(length, HEADS * HEAD)
    mixed = low_back(low(mixed))
    attention = low_back(product(mixed, w_attn.T))
    state = rows + attention
    scale_two = lax.rsqrt(lax.optimization_barrier(jnp.mean(state * state, axis=-1, keepdims=True)) + epsilon)
    normed_two = low(state * scale_two * gain_moe)
    logits = low_back(product(normed_two, w_router))
    chance = jax.nn.softmax(logits, axis=-1)
    expert_ids = jnp.arange(EXPERTS, dtype=jnp.int32)
    chosen = (route[:, :, None] == expert_ids).astype(jnp.float32)
    picked = lax.optimization_barrier(jnp.sum(chance[:, None, :] * chosen, axis=-1))
    gate = picked / lax.optimization_barrier(jnp.sum(picked, axis=-1, keepdims=True))
    blocks = length // TOK_DEV
    flat_route = route.reshape(blocks, 2 * TOK_DEV)
    member = (flat_route[:, :, None] == expert_ids).astype(jnp.int32)
    earlier = jnp.cumsum(member, axis=1) - member
    position = lax.optimization_barrier(jnp.sum(earlier * member, axis=-1))
    limit = lax.optimization_barrier(jnp.sum(member * capacity, axis=-1))
    slot = flat_route * CAP + position
    slot_ids = jnp.arange(EXPERTS * CAP, dtype=jnp.int32)
    dispatch = ((slot[:, :, None] == slot_ids) & (position < limit)[:, :, None]).astype(jnp.float32)
    per_token = lax.optimization_barrier(jnp.sum(dispatch.reshape(blocks, TOK_DEV, 2, EXPERTS * CAP), axis=2))
    slots = jnp.einsum('bts,btd->bsd', per_token, normed_two.reshape(blocks, TOK_DEV, D), precision=highest)
    slots = low_back(slots).reshape(blocks, EXPERTS, CAP, D)
    inner = low_back(jnp.einsum('becd,edf->becf', slots, w_in, precision=highest))
    active = low(jax.nn.gelu(inner))
    result = low_back(low(jnp.einsum('becf,efd->becd', active, w_out, precision=highest)))
    returned = jnp.einsum('bps,bsd->bpd', dispatch, result.reshape(blocks, EXPERTS * CAP, D), precision=highest)
    returned = returned.reshape(length, 2, D)
    mixture = lax.optimization_barrier(jnp.sum(gate[:, :, None] * returned, axis=1))
    return state + mixture

def reference(tokens, segments, routes, capacity, cotangent, rel_table, w_query, w_key, w_value, w_attn_out, gain_attn, gain_moe, w_router, w_in, w_out):
    floats = [a.astype(jnp.float32) for a in (rel_table, w_query, w_key, w_value, w_attn_out, gain_attn, gain_moe, w_router, w_in, w_out)]
    group = 4 if SEQS % 4 == 0 else 1
    count = SEQS // group

    def layer(rows, *weights):

        def one_group(inputs):
            return jax.vmap(lambda r, s, t: sequence_layer(weights, capacity, r, s, t))(*inputs)
        shaped = (rows.reshape(count, group, SEQ, D), segments.reshape(count, group, SEQ), routes.reshape(count, group, SEQ, 2))
        result = lax.map(jax.checkpoint(one_group), shaped)
        return result.reshape(SEQS, SEQ, D)
    output, pullback = jax.vjp(layer, tokens.astype(jnp.float32), *floats)
    grads = pullback(cotangent.astype(jnp.float32))
    return (output.astype(jnp.bfloat16), grads[0], grads[1], grads[2], grads[3], grads[4], grads[5], grads[6], grads[7], grads[8], grads[9], grads[10])
```

```python
import functools
import math

import jax
import jax.numpy as jnp
from jax import lax
from jax.experimental import pallas as pl
from jax.experimental.pallas import tpu as pltpu
from jax.sharding import PartitionSpec as P

HEAD = 64
CAP = 12
QB = 128
epsilon = 1e-06
masked_value = -1e30
thresholds = (16, 19, 21, 24, 27, 31, 35, 40, 46, 52, 59, 67, 77, 87, 99, 113)
lowest = tuple(range(16)) + thresholds
f32 = jnp.float32
bf16 = jnp.bfloat16
i32 = jnp.int32
NN = (((1,), (0,)), ((), ()))
NT = (((1,), (1,)), ((), ()))
TN = (((0,), (0,)), ((), ()))
VM = pl.BlockSpec(memory_space=pltpu.VMEM)
SM = pl.BlockSpec(memory_space=pltpu.SMEM)
sd = jax.ShapeDtypeStruct


def dot(a, b, dims=NN):
    return lax.dot_general(a, b, dims, preferred_element_type=f32)


def call(kernel, name, outs, operands, scratch=(), smem=0, flops=0, moved=4_000_000, alias=None):
    return pl.pallas_call(
        kernel,
        out_shape=tuple(outs),
        in_specs=[SM] * smem + [VM] * (len(operands) - smem),
        out_specs=tuple(VM for _ in outs),
        scratch_shapes=list(scratch),
        compiler_params=pltpu.CompilerParams(vmem_limit_bytes=56 << 20),
        cost_estimate=pl.CostEstimate(flops=flops, bytes_accessed=moved, transcendentals=0),
        name=name,
    )(*operands)


def to_tensor(a, flip):
    return lax.ppermute(a, "tensor", [(i, i ^ flip) for i in range(4)])


def to_expert(a, shift, size):
    return lax.ppermute(a, "expert", [(i, (i + shift) % size) for i in range(size)])


def to_core(a):
    return lax.ppermute(a, "rep", [(0, 1), (1, 0)])


def shifted(blocks):
    size = len(blocks)
    return [blocks[0]] + [to_expert(blocks[k], k, size) for k in range(1, size)]


def gather_pieces(own, half):
    px = to_tensor(own, 1)
    py = to_tensor(own, 2)
    d0 = to_tensor(px[:half], 2)
    d1 = to_tensor(py[half:], 1)
    return own, px, py, d0, d1


def scatter_pieces(pack_x, pack_y, x_late, y_late):
    got_x = to_tensor(pack_x, 1)
    got_y = to_tensor(pack_y, 2)
    late_x = to_tensor((x_late.astype(f32) + got_y[0].astype(f32)).astype(bf16), 1)
    late_y = to_tensor((y_late.astype(f32) + got_x[0].astype(f32)).astype(bf16), 2)
    return got_x, late_y, got_y, late_x


def add_parts(own, got_x, late_y, got_y, late_x):
    half = late_y.shape[0]
    first = own[0:half, :].astype(f32) + got_x[1].astype(f32) + late_y[...].astype(f32)
    second = own[half:, :].astype(f32) + got_y[1].astype(f32) + late_x[...].astype(f32)
    return first, second


def onehot(index, width):
    return lax.broadcasted_iota(i32, (index.shape[0], width), 1) == index


def as_bf16(mask):
    return jnp.where(mask, 1.0, 0.0).astype(bf16)


def prepare_kernel(size, chunks, me_ref, routes_ref, capacity_ref, cot_ref, idx_ref, *g_refs):
    count = routes_ref.shape[0]
    experts = capacity_ref.shape[1]
    local = experts // size
    part = local // chunks
    me = me_ref[0]
    first, second = routes_ref[:, 0:1], routes_ref[:, 1:2]
    both = as_bf16(onehot(first, experts)) + as_bf16(onehot(second, experts))
    rows = lax.broadcasted_iota(i32, (count, count), 0)
    cols = lax.broadcasted_iota(i32, (count, count), 1)
    before = dot(as_bf16(cols < rows), both)
    capacity = capacity_ref[...].astype(f32)
    shift = int(math.log2(local))
    columns = []
    for route in (first, second):
        mine = onehot(route, experts)
        position = jnp.sum(jnp.where(mine, before, 0.0), axis=1, keepdims=True)
        limit = jnp.sum(jnp.where(mine, jnp.broadcast_to(capacity, mine.shape), 0.0), axis=1, keepdims=True)
        keep = position < limit
        position = position.astype(i32)
        owner = lax.shift_right_logical(route, jnp.full_like(route, shift))
        inner = route & (local - 1)
        away = (owner - me + size) & (size - 1)
        chunk = lax.shift_right_logical(inner, jnp.full_like(route, int(math.log2(part))))
        slot = ((chunk * size + away) * part + (inner & (part - 1))) * CAP + position
        columns += [route, jnp.where(keep, slot, -1), jnp.where(keep, away * local + inner, -1), away * CAP + position]
    for n, column in enumerate(columns):
        idx_ref[:, n:n + 1] = column
    width = experts * CAP
    spread = as_bf16(onehot(columns[1], width)) + as_bf16(onehot(columns[5], width))
    slots = dot(spread, cot_ref[...], TN).astype(bf16)
    rows_of = part * CAP
    for k in range(size):
        for c in range(chunks):
            g_refs[k][c * rows_of:(c + 1) * rows_of, :] = slots[(c * size + k) * rows_of:(c * size + k + 1) * rows_of]


def order_matrix(size, part, block, extra, out_extra):
    rows = part * size * CAP
    m = [[0.0] * (size * block) for _ in range(rows + out_extra)]
    for e in range(part):
        for k in range(size):
            for c in range(CAP):
                m[(e * size + k) * CAP + c][k * block + e * CAP + c] = 1.0
    for r in range(extra):
        for k in range(size):
            m[rows + r][k * block + part * CAP + r] = 1.0
    return jnp.array(m, dtype=bf16)


def reorder_kernel(count, m_ref, *refs):
    blocks, out_ref = refs[:count], refs[count]
    out_ref[...] = dot(m_ref[...], jnp.concatenate([b[...] for b in blocks], axis=0)).astype(bf16)


def reorder(matrix, blocks, name):
    rows = matrix.shape[0]
    width = blocks[0].shape[1]
    return call(functools.partial(reorder_kernel, len(blocks)), name, [sd((rows, width), bf16)], (matrix, *blocks),
                flops=2 * matrix.size * width, moved=2 * rows * width * 2)[0]


def give_back_kernel(count, extra, m_ref, *refs):
    if extra:
        extra_ref, refs = refs[0], refs[1:]
    own, got_x, late_y, got_y, late_x = refs[:5]
    outs = refs[5:]
    first, second = add_parts(own, got_x, late_y, got_y, late_x)
    rows = jnp.concatenate([first.astype(bf16), second.astype(bf16)], axis=0)
    back = dot(m_ref[...], rows, TN).astype(bf16)
    block = back.shape[0] // count
    for k in range(count):
        outs[k][0:block, :] = back[k * block:(k + 1) * block]
        if extra:
            outs[k][block:, :] = extra_ref[...]


def plain_back_kernel(count, m_ref, rows_ref, *outs):
    back = dot(m_ref[...], rows_ref[...], TN).astype(bf16)
    block = back.shape[0] // count
    for k in range(count):
        outs[k][...] = back[k * block:(k + 1) * block]


def unpack_kernel(size, at_ref, *refs):
    mine, other = refs[:size], refs[size:2 * size]
    full, qkv_ref, wo_ref, router_ref, gains_ref, table_ref = refs[2 * size:]
    me, rep = at_ref[0], at_ref[1]
    half = mine[0].shape[0]
    for k in range(size):
        z = (me - k + size) & (size - 1)
        full[2 * z + rep] = mine[k][...].astype(f32)
        full[2 * z + 1 - rep] = other[k][...].astype(f32)
    full = jnp.concatenate([full[n] for n in range(2 * size)], axis=0)
    qkv_ref[...] = full[:, 0:576].astype(bf16)
    router_ref[...] = full[:, 576:640].astype(bf16)
    wo_ref[...] = full[:, 640:832].astype(bf16)
    tail = full[:, 768:896]
    turned = tail.T
    gains_ref[...] = turned[64:72, :]
    rows = table_ref.shape[0] // size
    for z in range(size):
        table_ref[z * rows:(z + 1) * rows, :] = tail[z * 2 * half: z * 2 * half + rows, :]


def unpack(at, mine, other, buckets):
    size = len(mine)
    half, cols = mine[0].shape
    width = 2 * half * size

    def kernel(at_ref, *refs):
        unpack_kernel(size, at_ref, *refs[:2 * size], refs[-1], *refs[2 * size:-1])

    outs = [sd((width, 576), bf16), sd((width, 192), bf16), sd((width, 64), bf16), sd((8, width), f32), sd((buckets, 128), f32)]
    return call(kernel, "unpack", outs, (at, *mine, *other), scratch=[pltpu.VMEM((2 * size, half, cols), f32)], smem=1)


def put_pieces(part, tok, own, pack_x, pack_y, x_late, y_late):
    half = tok // 2
    own[...] = part(0, 0, tok)
    pack_x[0] = part(3, 0, half)
    pack_x[1] = part(1, 0, half)
    pack_y[0] = part(3, half, half)
    pack_y[1] = part(2, half, half)
    x_late[...] = part(1, half, half)
    y_late[...] = part(2, 0, half)


def piece_shapes(rows, width):
    half = rows // 2
    return [sd((rows, width), bf16), sd((2, half, width), bf16), sd((2, half, width), bf16), sd((half, width), bf16), sd((half, width), bf16)]


def near_offset():
    rows = lax.broadcasted_iota(jnp.int32, (QB, 2 * QB), 0)
    cols = lax.broadcasted_iota(jnp.int32, (QB, 2 * QB), 1)
    return QB + rows - cols


def near_bias(table_ref, head, buckets):
    off = near_offset()
    bias = jnp.where(off < 0, masked_value, table_ref[0, head])
    for b in range(1, buckets):
        bias = jnp.where(off >= lowest[b], table_ref[b, head], bias)
    return bias


def scores_of(q, k_ref, head, i, near, far, seg_col, seg_row_ref):
    lo = max(i - 1, 0) * QB
    hi = (i + 1) * QB
    s = dot(q, k_ref[head, 0:hi], NT)
    bias = near[:, QB:] if i == 0 else near
    same_near = seg_col == seg_row_ref[:, lo:hi]
    s_near = jnp.where(same_near, s[:, lo:hi] + bias, masked_value)
    if lo == 0:
        return s_near
    same_far = seg_col == seg_row_ref[:, 0:lo]
    s_far = jnp.where(same_far, s[:, 0:lo] + far, masked_value)
    return jnp.concatenate([s_far, s_near], axis=1)


def attn_fwd_kernel(heads, at_ref, table_ref, own_ref, px_ref, py_ref, pd0_ref, pd1_ref, segc_ref, segr_ref, w_ref, wo_ref, gain_ref,
                    xn_ref, qkv_ref, o_ref, lse_ref, out_own, out_px, out_py, out_x, out_y, qs, ks, vs):
    pos = at_ref[2]
    tok = own_ref.shape[0]
    half = tok // 2
    buckets = table_ref.shape[0]
    gain = gain_ref[0:1, :]

    def norm(rows):
        x = rows.astype(f32)
        r = lax.rsqrt(jnp.mean(x * x, axis=-1, keepdims=True) + epsilon)
        return (x * r * gain).astype(bf16)

    def at(flip, start=0, size=tok):
        return pl.ds(pl.multiple_of((pos ^ flip) * tok + start, half), size)

    xn_ref[at(0), :] = norm(own_ref[...])
    xn_ref[at(1), :] = norm(px_ref[...])
    xn_ref[at(2), :] = norm(py_ref[...])
    xn_ref[at(3, 0, half), :] = norm(pd0_ref[...])
    xn_ref[at(3, half, half), :] = norm(pd1_ref[...])
    qkv = dot(xn_ref[...], w_ref[...]).astype(bf16)
    qkv_ref[...] = qkv
    width = heads * HEAD
    for h in range(heads):
        qs[h] = qkv[:, h * HEAD:(h + 1) * HEAD] * bf16(0.125)
        ks[h] = qkv[:, width + h * HEAD: width + (h + 1) * HEAD]
        vs[h] = qkv[:, 2 * width + h * HEAD: 2 * width + (h + 1) * HEAD]
    blocks = xn_ref.shape[0] // QB
    for h in range(heads):
        near = near_bias(table_ref, h, buckets)
        far = table_ref[buckets - 1, h]
        for i in range(blocks):
            rows = slice(i * QB, (i + 1) * QB)
            s = scores_of(qs[h, rows], ks, h, i, near, far, segc_ref[rows, :], segr_ref)
            top = jnp.max(s, axis=-1, keepdims=True)
            e = jnp.exp(s - top)
            total = jnp.sum(e, axis=-1, keepdims=True)
            p = (e * (1.0 / total)).astype(bf16)
            o_ref[rows, h * HEAD:(h + 1) * HEAD] = dot(p, vs[h, 0:(i + 1) * QB]).astype(bf16)
            lse_ref[rows, h:h + 1] = top + jnp.log(total)
    wo = wo_ref[...]
    put_pieces(lambda flip, start, size: dot(o_ref[at(flip, start, size), :], wo, NT).astype(bf16), tok, out_own, out_px, out_py, out_x, out_y)


def attn_bwd_kernel(heads, size, at_ref, table_ref, own_ref, px_ref, py_ref, pd0_ref, pd1_ref, segc_ref, segr_ref, w_ref, wo_ref,
                    xn_ref, qkv_ref, o_ref, lse_ref, keep_ref, send_ref, gain_ref, gtab_ref, out_own, out_px, out_py, out_x, out_y,
                    dh, qs, ks, vs, do, dk, dv, dqkv, acc, full):
    pos = at_ref[2]
    rep = at_ref[1]
    tok = own_ref.shape[0]
    half = tok // 2
    buckets = table_ref.shape[0]
    width = heads * HEAD

    def at(flip, start=0, size=tok):
        return pl.ds(pl.multiple_of((pos ^ flip) * tok + start, half), size)

    dh[at(0), :] = own_ref[...]
    dh[at(1), :] = px_ref[...]
    dh[at(2), :] = py_ref[...]
    dh[at(3, 0, half), :] = pd0_ref[...]
    dh[at(3, half, half), :] = pd1_ref[...]
    dall = dot(dh[...], wo_ref[...]).astype(bf16)
    for h in range(heads):
        do[h] = dall[:, h * HEAD:(h + 1) * HEAD]
        qs[h] = qkv_ref[:, h * HEAD:(h + 1) * HEAD] * bf16(0.125)
        ks[h] = qkv_ref[:, width + h * HEAD: width + (h + 1) * HEAD]
        vs[h] = qkv_ref[:, 2 * width + h * HEAD: 2 * width + (h + 1) * HEAD]
    blocks = xn_ref.shape[0] // QB
    off = near_offset()
    for h in range(heads):
        near = near_bias(table_ref, h, buckets)
        far = table_ref[buckets - 1, h]
        acc[...] = jnp.zeros_like(acc)
        dk[...] = jnp.zeros_like(dk)
        dv[...] = jnp.zeros_like(dv)
        far_sum = jnp.zeros((QB, 1), f32)
        for i in range(blocks):
            rows = slice(i * QB, (i + 1) * QB)
            lo = max(i - 1, 0) * QB
            hi = (i + 1) * QB
            q = qs[h, rows]
            s = scores_of(q, ks, h, i, near, far, segc_ref[rows, :], segr_ref)
            p = jnp.exp(s - lse_ref[rows, h:h + 1])
            g = do[h, rows]
            dv[0:hi] += dot(p.astype(bf16), g, TN)
            dp = dot(g, vs[h, 0:hi], NT)
            pd = p * dp
            ds = (pd - p * jnp.sum(pd, axis=-1, keepdims=True)).astype(bf16)
            dq = dot(ds, ks[h, 0:hi]) * 0.125
            dqkv[rows, h * HEAD:(h + 1) * HEAD] = dq.astype(bf16)
            dk[0:hi] += dot(ds, q, TN)
            dsf = ds.astype(f32)
            if i == 0:
                acc[:, QB:] += dsf
            else:
                acc[...] += dsf[:, lo:hi]
            if lo > 0:
                far_sum = far_sum + jnp.sum(dsf[:, 0:lo], axis=-1, keepdims=True)
        dqkv[:, width + h * HEAD: width + (h + 1) * HEAD] = dk[...].astype(bf16)
        dqkv[:, 2 * width + h * HEAD: 2 * width + (h + 1) * HEAD] = dv[...].astype(bf16)
        total = acc[...]
        rest = jnp.sum(far_sum, axis=0, keepdims=True)
        for b in range(buckets):
            if b == buckets - 1:
                inside = off >= lowest[b]
            else:
                inside = (off >= lowest[b]) & (off < lowest[b + 1])
            part = jnp.sum(jnp.where(inside, total, 0.0), axis=0, keepdims=True)
            one = jnp.sum(part, axis=1, keepdims=True)
            gtab_ref[b:b + 1, h:h + 1] = one + rest if b == buckets - 1 else one
    w = w_ref[...]
    def part(flip, start, size):
        return dot(dqkv[at(flip, start, size), :], w, NT).astype(bf16)

    put_pieces(part, tok, out_own, out_px, out_py, out_x, out_y)
    grad = dot(xn_ref[...], dqkv[...], TN)
    gain_sum = jnp.sum(grad * w.astype(f32), axis=1, keepdims=True)
    gain_ref[...] = jnp.broadcast_to(gain_sum, (gain_sum.shape[0], 128)).T[0:8, :]
    grad_out = dot(dh[...], o_ref[...], TN)
    part_rows = keep_ref.shape[1]
    for n in range(2 * size):
        full[n, :, 0:3 * width] = grad[n * part_rows:(n + 1) * part_rows].astype(bf16)
        full[n, :, 3 * width:] = grad_out[n * part_rows:(n + 1) * part_rows].astype(bf16)
    for z in range(size):
        keep_ref[z] = full[2 * z + rep]
        send_ref[z] = full[2 * z + 1 - rep]


def attn_fwd(at, table, pieces, segc, segr, w, wo, gains):
    tok, width = pieces[0].shape
    length = segc.shape[0]
    heads = wo.shape[1] // HEAD
    outs = [sd((length, width), bf16), sd((length, 3 * heads * HEAD), bf16), sd((length, heads * HEAD), bf16), sd((length, heads), f32)]
    return call(functools.partial(attn_fwd_kernel, heads), "attn_fwd", outs + piece_shapes(tok, width),
                (at, table, *pieces, segc, segr, w, wo, gains),
                scratch=[pltpu.VMEM((heads, length, HEAD), bf16)] * 3, smem=2, flops=8_000_000_000, moved=10_000_000)


def attn_bwd(at, size, table, pieces, segc, segr, w, wo, xn, qkv, o, lse):
    tok, width = pieces[0].shape
    length = segc.shape[0]
    heads = wo.shape[1] // HEAD
    outs = [sd((size, width // (2 * size), 4 * heads * HEAD), bf16)] * 2 + [sd((8, width), f32), sd((table.shape[0], heads), f32)]
    scratch = [pltpu.VMEM((length, width), bf16)] + [pltpu.VMEM((heads, length, HEAD), bf16)] * 4 + [pltpu.VMEM((length, HEAD), f32)] * 2
    scratch += [pltpu.VMEM((length, 3 * heads * HEAD), bf16), pltpu.VMEM((QB, 2 * QB), f32), pltpu.VMEM((2 * size, width // (2 * size), 4 * heads * HEAD), bf16)]
    return call(functools.partial(attn_bwd_kernel, heads, size), "attn_bwd", outs + piece_shapes(tok, width),
                (at, table, *pieces, segc, segr, w, wo, xn, qkv, o, lse), scratch=scratch, smem=2, flops=16_000_000_000, moved=12_000_000)


def route_kernel(size, chunks, idx_ref, tokens_ref, own, got_x, late_y, got_y, late_x, router_ref, gains_ref, h_ref, xn_ref, probs_ref, gate_ref, *blocks):
    count, width = tokens_ref.shape
    experts = router_ref.shape[1]
    local = experts // size
    rows_of = local // chunks * CAP
    lanes = lanes_of(size)
    first, second = add_parts(own, got_x, late_y, got_y, late_x)
    h = tokens_ref[...].astype(f32) + jnp.concatenate([first, second], axis=0)
    r = lax.rsqrt(jnp.mean(h * h, axis=-1, keepdims=True) + epsilon)
    xn = (h * r * gains_ref[1:2, :]).astype(bf16)
    h_ref[...] = h
    xn_ref[...] = xn
    logits = dot(xn, router_ref[...])
    e = jnp.exp(logits - jnp.max(logits, axis=-1, keepdims=True))
    probs = e / jnp.sum(e, axis=-1, keepdims=True)
    probs_ref[...] = probs
    picked = [jnp.sum(jnp.where(onehot(idx_ref[:, 4 * j:4 * j + 1], experts), probs, 0.0), axis=-1, keepdims=True) for j in (0, 1)]
    total = picked[0] + picked[1]
    gates = [p / total for p in picked]
    gate_ref[:, 0:1], gate_ref[:, 1:2], gate_ref[:, 2:3] = gates[0], gates[1], total
    spread = as_bf16(onehot(idx_ref[:, 1:2], experts * CAP)) + as_bf16(onehot(idx_ref[:, 5:6], experts * CAP))
    slots = dot(spread, xn, TN).astype(bf16)
    held = jnp.zeros((experts, lanes), f32)
    for j in (0, 1):
        to = as_bf16(onehot(idx_ref[:, 4 * j + 2:4 * j + 3], experts))
        at = jnp.where(onehot(idx_ref[:, 4 * j + 3:4 * j + 4], lanes), gates[j], 0.0).astype(bf16)
        held = held + dot(to, at, TN)
    for c in range(chunks):
        for k in range(size):
            ref = blocks[c * size + k]
            ref[0:rows_of, :] = slots[(c * size + k) * rows_of:(c * size + k + 1) * rows_of]
            if c == 0:
                ref[rows_of:, :] = jnp.zeros((16, width), bf16)
                ref[rows_of:rows_of + local, 0:lanes] = held[k * local:(k + 1) * local].astype(bf16)


def lanes_of(size):
    return -(-size * CAP // 128) * 128


def route(idx, tokens, parts, router, gains, size, chunks):
    count, width = tokens.shape
    experts = router.shape[1]
    rows_of = experts // size // chunks * CAP
    outs = [sd((count, width), f32), sd((count, width), bf16), sd((count, experts), f32), sd((count, 8), f32)]
    for c in range(chunks):
        outs += [sd((rows_of + (16 if c == 0 else 0), width), bf16)] * size
    return call(functools.partial(route_kernel, size, chunks), "route", outs, (idx, tokens, *parts, router, gains),
                flops=400_000_000, moved=5_000_000)


def moe_kernel(rows, part, offset, more, at_ref, own, px, py, d0, d1, e_own, e_px, e_py, e_d, g_ref, win_ref, wout_ref, *refs):
    if more:
        refs = refs[2:]
    o_own, o_px, o_py, o_x, o_y, y_ref, dg_ref, acts = refs
    pos = at_ref[2]
    e, j = pl.program_id(0), pl.program_id(1)
    early = e < part // 2
    wide = e_own.shape[1]

    pick = lax.broadcasted_iota(i32, (16, wide), 0) == e + offset
    square = lax.broadcasted_iota(i32, (rows, wide), 0) + j * rows == lax.broadcasted_iota(i32, (rows, wide), 1)

    def gate_of(ref):
        row = jnp.sum(jnp.where(pick, ref[...].astype(f32), 0.0), axis=0, keepdims=True)
        return jnp.sum(jnp.where(square, jnp.broadcast_to(row, square.shape), 0.0), axis=1, keepdims=True)

    gate = jnp.concatenate([gate_of(r) for r in (e_own, e_px, e_py, e_d)], axis=0)
    far = jnp.where(early, d0[...].astype(f32), d1[...].astype(f32)).astype(bf16)
    s = jnp.concatenate([own[...], px[...], py[...], far], axis=0)

    def keep(n, value):
        for flip in range(4):
            acts[n, 0, flip] = value[flip * rows:(flip + 1) * rows]

    keep(0, s)
    g = jnp.concatenate([g_ref[pos ^ flip] for flip in range(4)], axis=0).astype(f32)
    win, wout = win_ref[0], wout_ref[0]
    dy = (g * gate).astype(bf16)
    keep(1, dy)
    a = dot(s, win)
    dhid = dot(dy, wout, NT)
    c = math.sqrt(2.0 / math.pi)
    t = jnp.tanh(a * (c + (c * 0.044715) * (a * a)))
    up = 0.5 + 0.5 * t
    hid = (a * up).astype(bf16)
    slope = up + (0.5 * a) * (1.0 - t * t) * (c + (3 * c * 0.044715) * (a * a))
    da = (dhid * slope).astype(bf16)
    keep(2, hid)
    keep(3, da)
    y = dot(hid, wout)
    ones = jnp.ones((8, y.shape[1]), bf16)
    sums = dot(ones, (y * g).astype(bf16), NT)
    yb = y.astype(bf16)
    dg_ref[...] = jnp.zeros_like(dg_ref)
    for flip in range(4):
        y_ref[pos ^ flip] = yb[flip * rows:(flip + 1) * rows]
        dg_ref[0, flip:flip + 1, 0:rows] = sums[0:1, flip * rows:(flip + 1) * rows]
    ds = dot(da, win, NT).astype(bf16)
    o_own[...] = ds[0:rows]

    @pl.when(early)
    def _():
        o_px[0] = ds[3 * rows:]
        o_px[1] = ds[rows:2 * rows]
        o_y[...] = ds[2 * rows:3 * rows]

    @pl.when(jnp.logical_not(early))
    def _():
        o_py[0] = ds[3 * rows:]
        o_py[1] = ds[2 * rows:3 * rows]
        o_x[...] = ds[rows:2 * rows]


def moe(at, size, chunk, part, pieces, extras, g, w_in, w_out, before):
    all_rows = size * CAP
    rows = 128 if all_rows % 128 == 0 else all_rows
    steps = all_rows // rows
    local, width, hidden = w_in.shape
    half = part // 2
    lanes = -(-all_rows // 128) * 128
    lo = lambda e, j: jnp.where(e < half, e * steps + j, half * steps - 1)
    hi = lambda e, j: jnp.where(e < half, 0, (e - half) * steps + j)
    whole = lambda e, j: e * steps + j
    flat = lambda f: pl.BlockSpec((rows, width), lambda e, j: (f(e, j), 0))
    two = lambda f: pl.BlockSpec((2, rows, width), lambda e, j: (0, f(e, j), 0))
    first = chunk * part
    ext = lambda n: pl.BlockSpec((16, lanes), lambda e, j: (n // 16, 0))
    four = pl.BlockSpec((4, rows, width), lambda e, j: (0, (first + e) * steps + j, 0))
    in_specs = [SM, flat(whole), flat(whole), flat(whole), flat(lo), flat(hi)]
    in_specs += [ext(part * all_rows)] * 3 + [ext(half * all_rows), four]
    in_specs += [pl.BlockSpec((1, width, hidden), lambda e, j: (first + e, 0, 0)), pl.BlockSpec((1, hidden, width), lambda e, j: (first + e, 0, 0))]
    operands = [at, *pieces, *extras, g, w_in, w_out]
    alias = {}
    if before:
        alias = {len(operands): 5, len(operands) + 1: 6}
        operands += list(before)
        in_specs += [pl.BlockSpec(memory_space=pl.ANY)] * 2
    total, late = part * all_rows, half * all_rows
    outs = [sd((total, width), bf16), sd((2, late, width), bf16), sd((2, late, width), bf16), sd((late, width), bf16), sd((late, width), bf16),
            sd((4, local * all_rows, width), bf16), sd((local, 8, lanes), f32), sd((4, part, 4, all_rows, width), bf16)]
    out_specs = [flat(whole), two(lo), two(hi), flat(hi), flat(lo), four,
                 pl.BlockSpec((1, 8, lanes // steps), lambda e, j: (first + e, 0, j)),
                 pl.BlockSpec((4, 1, 4, rows, width), lambda e, j: (0, e, 0, j, 0))]
    return pl.pallas_call(
        functools.partial(moe_kernel, rows, part, first, bool(before)),
        grid=(part, steps),
        out_shape=tuple(outs), in_specs=in_specs, out_specs=tuple(out_specs),
        input_output_aliases=alias,
        compiler_params=pltpu.CompilerParams(vmem_limit_bytes=56 << 20),
        cost_estimate=pl.CostEstimate(flops=8 * part * 4 * all_rows * width * hidden, bytes_accessed=30_000_000, transcendentals=part * 4 * all_rows * hidden),
        name="moe",
    )(*operands)


def expert_grad_kernel(steps, at_ref, mine, other, *refs):
    gin, gout = refs[-2:]

    def put(a, b):
        both = [jnp.concatenate([r[n, 0, flip] for r in (a, b) for flip in range(4)], axis=0) for n in range(4)]
        for ref, left, right in ((gin, both[0], both[3]), (gout, both[2], both[1])):
            if steps == 1:
                ref[0] = dot(left, right, TN)
            else:
                part = dot(left, right, TN)
                ref[0] = jnp.where(pl.program_id(1) == 0, part, ref[0] + part)

    pl.when(at_ref[1] == 0)(lambda: put(mine, other))
    pl.when(at_ref[1] == 1)(lambda: put(other, mine))


def expert_grad(at, chunk, local, mine, other, before):
    part, four, all_rows, width = mine.shape[1:]
    rows = 128 if all_rows % 128 == 0 else all_rows
    steps = all_rows // rows
    spec = pl.BlockSpec((4, 1, 4, rows, width), lambda e, j: (0, e, 0, j, 0))
    in_specs = [SM, spec, spec]
    operands = [at, mine, other]
    alias = {}
    if before:
        alias = {3: 0, 4: 1}
        operands += list(before)
        in_specs += [pl.BlockSpec(memory_space=pl.ANY)] * 2
    out = pl.BlockSpec((1, width, width), lambda e, j: (chunk * part + e, 0, 0))
    return pl.pallas_call(
        functools.partial(expert_grad_kernel, steps),
        grid=(part, steps),
        out_shape=(sd((local, width, width), f32),) * 2, in_specs=in_specs, out_specs=(out, out),
        input_output_aliases=alias,
        compiler_params=pltpu.CompilerParams(vmem_limit_bytes=56 << 20),
        cost_estimate=pl.CostEstimate(flops=32 * part * all_rows * width * width,
                                      bytes_accessed=part * (64 * all_rows * width + 8 * width * width), transcendentals=0),
        name="expert_grad",
    )(*operands)


def back_kernel(size, chunks, idx_ref, cot_ref, h_ref, xn_ref, probs_ref, gate_ref, router_ref, gains_ref, *refs):
    blocks = refs[:chunks * size]
    dh_ref, dhb_ref, small_ref, ds = refs[chunks * size:]
    experts = router_ref.shape[1]
    local = experts // size
    rows_of = local // chunks * CAP
    lanes = lanes_of(size)
    for n, block in enumerate(blocks):
        ds[n * rows_of:(n + 1) * rows_of, :] = block[0:rows_of, :]
    last = blocks[(chunks - 1) * size:]
    held = jnp.concatenate([last[k][rows_of:rows_of + local, 0:lanes].astype(f32) for k in range(size)], axis=0).astype(bf16)
    spread = as_bf16(onehot(idx_ref[:, 1:2], experts * CAP)) + as_bf16(onehot(idx_ref[:, 5:6], experts * CAP))
    dxn = dot(spread, ds[...])
    probs = probs_ref[...]
    gates, dgates, chosen = [], [], []
    for j in (0, 1):
        got = dot(as_bf16(onehot(idx_ref[:, 4 * j + 2:4 * j + 3], experts)), held)
        dgates.append(jnp.sum(jnp.where(onehot(idx_ref[:, 4 * j + 3:4 * j + 4], lanes), got, 0.0), axis=-1, keepdims=True))
        gates.append(gate_ref[:, j:j + 1])
        chosen.append(onehot(idx_ref[:, 4 * j:4 * j + 1], experts))
    mean = gates[0] * dgates[0] + gates[1] * dgates[1]
    scale = 1.0 / gate_ref[:, 2:3]
    dprobs = jnp.where(chosen[0], (dgates[0] - mean) * scale, 0.0) + jnp.where(chosen[1], (dgates[1] - mean) * scale, 0.0)
    dlogits = (probs * (dprobs - jnp.sum(probs * dprobs, axis=-1, keepdims=True))).astype(bf16)
    small_ref[...] = jnp.zeros_like(small_ref)
    small_ref[:, 0:experts] = dot(xn_ref[...], dlogits, TN)
    dxn = dxn + dot(dlogits, router_ref[...], NT)
    h = h_ref[...]
    r = lax.rsqrt(jnp.mean(h * h, axis=-1, keepdims=True) + epsilon)
    gain_row = jnp.sum(dxn * h * r, axis=0, keepdims=True)
    small_ref[:, experts:experts + 1] = jnp.broadcast_to(gain_row, (8, gain_row.shape[1])).T[:, 0:1]
    scaled = dxn * gains_ref[1:2, :]
    dh = cot_ref[...].astype(f32) + r * scaled - h * (r * r * r) * jnp.mean(h * scaled, axis=-1, keepdims=True)
    dh_ref[...] = dh
    dhb_ref[...] = dh.astype(bf16)


def back(idx, cot, h, xn, probs, gate, router, gains, blocks, size, chunks):
    count, width = h.shape
    experts = router.shape[1]
    outs = [sd((count, width), f32), sd((count, width), bf16), sd((width, 128), f32)]
    return call(functools.partial(back_kernel, size, chunks), "back", outs, (idx, cot, h, xn, probs, gate, router, gains, *blocks),
                scratch=[pltpu.VMEM((experts * CAP, width), bf16)], flops=400_000_000, moved=6_000_000)


def mix_kernel(size, local, idx_ref, h_ref, gate_ref, *refs):
    blocks, out_ref, ys = refs[:size], refs[size], refs[size + 1]
    rows_of = local * CAP
    for k in range(size):
        ys[k * rows_of:(k + 1) * rows_of, :] = blocks[k][...]
    out = h_ref[...]
    for j in (0, 1):
        expert, lane = idx_ref[:, 4 * j + 2:4 * j + 3], idx_ref[:, 4 * j + 3:4 * j + 4]
        away = lax.shift_right_logical(expert, jnp.full_like(expert, int(math.log2(local))))
        slot = jnp.where(expert < 0, -1, expert * CAP + lane - away * CAP)
        out = out + gate_ref[:, j:j + 1] * dot(as_bf16(onehot(slot, rows_of * size)), ys[...])
    out_ref[...] = out.astype(bf16)


def mix(idx, h, gate, blocks, local):
    size = len(blocks)
    count, width = h.shape
    return call(functools.partial(mix_kernel, size, local), "mix", [sd((count, width), bf16)], (idx, h, gate, *blocks),
                scratch=[pltpu.VMEM((size * local * CAP, width), bf16)], flops=600_000_000, moved=3_000_000)[0]


def last_kernel(tokens_ref, dh_ref, own, got_x, late_y, got_y, late_x, gains_ref, out_ref):
    first, second = add_parts(own, got_x, late_y, got_y, late_x)
    x = tokens_ref[...].astype(f32)
    r = lax.rsqrt(jnp.mean(x * x, axis=-1, keepdims=True) + epsilon)
    scaled = jnp.concatenate([first, second], axis=0) * gains_ref[0:1, :]
    out_ref[...] = dh_ref[...] + r * scaled - x * (r * r * r) * jnp.mean(x * scaled, axis=-1, keepdims=True)


def total_kernel(*refs):
    out = refs[-1]
    out[...] = sum(r[...].astype(f32) for r in refs[:-1])


def finish_kernel(at_ref, mine_ref, other_ref, q_ref, k_ref, v_ref, o_ref, small_ref):
    half = mine_ref.shape[0]
    width = q_ref.shape[1]

    def put(first, second):
        for n, ref in enumerate((q_ref, k_ref, v_ref, o_ref)):
            ref[0:half, :] = first[:, n * width:(n + 1) * width]
            ref[half:, :] = second[:, n * width:(n + 1) * width]
        a, b = first[:, 4 * width:], second[:, 4 * width:]
        lane = lax.broadcasted_iota(i32, a.shape, 1)
        small_ref[0:half, :] = jnp.where(lane == 65, a + shift_lane(b), jnp.where(lane > 66, a + b, a))
        small_ref[half:, :] = jnp.where(lane == 65, b + shift_lane(a), b)

    def shift_lane(x):
        return jnp.broadcast_to(x[:, 66:67], x.shape)

    pl.when(at_ref[1] == 0)(lambda: put(mine_ref, other_ref))
    pl.when(at_ref[1] == 1)(lambda: put(other_ref, mine_ref))


def on_device(size, tokens, segments, routes, capacity, cotangent, rel_table, w_query, w_key, w_value, w_attn_out, gain_attn, gain_moe, w_router, w_in, w_out):
    z = lax.axis_index("expert").astype(i32)
    rep = lax.axis_index("rep").astype(i32)
    pos = lax.axis_index("tensor").astype(i32)
    at = jnp.stack([z, rep, pos])
    tok = tokens[0]
    cot = cotangent[0]
    count, width = tok.shape
    local = w_in.shape[0]
    experts = w_router.shape[1]
    chunks = 2 if local >= 4 else 1
    part = local // chunks
    rows_dev = w_query.shape[0]
    half = rows_dev // 2
    buckets = rel_table.shape[0] * size

    pieces = gather_pieces(tok, count // 2)
    table_rows = jnp.pad(rel_table, ((0, rows_dev - rel_table.shape[0]), (0, 59)))
    packed = jnp.concatenate([w_query, w_key, w_value, w_router, w_attn_out, gain_attn[:, None], gain_moe[:, None], table_rows], axis=1)
    mine = [lax.dynamic_slice_in_dim(packed, rep * half, half, axis=0)]
    mine += [to_expert(mine[0], k, size) for k in range(1, size)]
    other = [to_core(m) for m in mine]
    qkv_w, wo, router, gains, table_full = unpack(at, mine, other, buckets)
    table = table_full[:, 66:69]

    idx, *g_blocks = call(functools.partial(prepare_kernel, size, chunks), "prepare",
                          [sd((count, 8), i32)] + [sd((local * CAP, width), bf16)] * size,
                          (z[None], routes[0], capacity[None], cot), smem=1, flops=400_000_000)
    whole = order_matrix(size, local, local * CAP, 0, 0)
    g_own = reorder(whole, shifted(g_blocks), "order_g")
    g_all = lax.all_gather(g_own, "tensor", axis=0)

    segc, segr = segments[0][:, None], segments
    xn, qkv, o, lse, own, pack_x, pack_y, x_late, y_late = attn_fwd(at, table, pieces, segc, segr, qkv_w, wo, gains)
    parts = scatter_pieces(pack_x, pack_y, x_late, y_late)
    h, xn2, probs, gate, *blocks = route(idx, tok, (own, *parts), router, gains, size, chunks)

    extras = None
    before = ()
    acts, sums = [], []
    for c in range(chunks):
        extra = 16 if c == 0 else 0
        matrix = order_matrix(size, part, part * CAP + extra, extra, extra)
        ordered = reorder(matrix, shifted(blocks[c * size:(c + 1) * size]), "order")
        got = gather_pieces(ordered, part * CAP * size // 2)
        if c == 0:
            extras = (got[0], got[1], got[2], got[4])
        *scattered, y_full, dg_full, act = moe(at, size, c, part, got, extras, g_all, w_in, w_out, before)
        before = (y_full, dg_full)
        acts.append(act)
        sums.append((scattered[0], *scatter_pieces(*scattered[1:])))
    other_acts = [to_core(a) for a in acts]
    dg_x = to_tensor(dg_full, 1)
    dg_two = dg_full[:, 2] + dg_x[:, 3]
    dg = dg_full[:, 0] + dg_x[:, 1] + to_tensor(dg_two, 2)
    dg = jnp.pad(dg.astype(bf16), ((0, 16 - local), (0, width - dg.shape[1])))
    back_blocks = []
    for c in range(chunks):
        extra = c == chunks - 1
        matrix = order_matrix(size, part, part * CAP, 0, 0)
        outs = [sd((part * CAP + 16 * extra, width), bf16)] * size
        given = call(functools.partial(give_back_kernel, size, extra), "give_back", outs,
                     (matrix,) + ((dg,) if extra else ()) + sums[c], flops=300_000_000, moved=3_000_000)
        back_blocks += [given[0]] + [to_expert(given[k], size - k, size) for k in range(1, size)]
    dh, dhb, small = back(idx, cot, h, xn2, probs, gate, router, gains, back_blocks, size, chunks)

    y_own = lax.psum_scatter(y_full, "tensor", scatter_dimension=0)
    given = call(functools.partial(plain_back_kernel, size), "give_back_y", [sd((local * CAP, width), bf16)] * size,
                 (whole, y_own), flops=900_000_000, moved=3_000_000)
    y_blocks = [given[0]] + [to_expert(given[k], size - k, size) for k in range(1, size)]
    output = mix(idx, h, gate, y_blocks, local)

    grads = ()
    for c in range(chunks):
        grads = expert_grad(at, c, local, acts[c], other_acts[c], grads)

    dh_pieces = gather_pieces(dhb, count // 2)
    keep, send, gain_row, gtab, own, pack_x, pack_y, x_late, y_late = attn_bwd(at, size, table, dh_pieces, segc, segr, qkv_w, wo, xn, qkv, o, lse)
    parts = scatter_pieces(pack_x, pack_y, x_late, y_late)
    grad_tokens = call(last_kernel, "last", [sd((count, width), f32)], (tok, dh, own, *parts, gains), moved=3_000_000)[0]

    small = small + to_tensor(small, 1)
    small = small + to_tensor(small, 2)
    small = small + to_core(small)
    gain_row = gain_row + to_tensor(gain_row, 1)
    gain_row = gain_row + to_tensor(gain_row, 2)
    gain_col = gain_row[0].reshape(size, 2, half)
    got = to_core(send)
    out_blocks = []
    small_rows = small.reshape(size, 2, half, 128)
    gtab_rows = gtab.reshape(size, buckets // size, gtab.shape[1])
    for k in range(size):
        to = (z + k) & (size - 1)
        both = lax.dynamic_index_in_dim(keep, to, keepdims=False).astype(f32) + lax.dynamic_index_in_dim(got, to, keepdims=False).astype(f32)
        few = lax.dynamic_slice(small_rows, (to, rep, 0, 0), (1, 1, half, 128))[0, 0]
        gain_a = lax.dynamic_slice(gain_col, (to, rep, 0), (1, 1, half))[0, 0][:, None]
        gain_b = lax.dynamic_slice(gain_col, (to, 1 - rep, 0), (1, 1, half))[0, 0][:, None]
        rows = lax.dynamic_slice(gtab_rows, (to, 0, 0), (1, *gtab_rows.shape[1:]))[0]
        rows = jnp.pad(rows, ((0, half - rows.shape[0]), (0, 0)))
        tail = jnp.concatenate([few[:, :experts + 1], gain_a, gain_b, rows, few[:, experts + 6:]], axis=1)
        out_blocks.append(jnp.concatenate([both, tail], axis=1).astype(bf16))
    arrived = shifted(out_blocks)
    total = call(total_kernel, "total", [sd(out_blocks[0].shape, f32)], tuple(arrived))[0]
    swapped = to_core(total)
    lw = w_query.shape[1]
    grad_q, grad_k, grad_v, grad_o, few = call(finish_kernel, "finish", [sd((rows_dev, lw), f32)] * 4 + [sd((rows_dev, 128), f32)],
                                               (at, total, swapped), smem=1)
    grad_router = few[:, :experts]
    grad_gain_moe = few[:, experts]
    grad_gain_attn = few[:, experts + 1] / gain_attn.astype(f32)
    grad_table = few[:rel_table.shape[0], experts + 3:experts + 3 + rel_table.shape[1]]
    return (output[None], grad_tokens[None], grad_table, grad_q, grad_k, grad_v, grad_o, grad_gain_attn, grad_gain_moe, grad_router, grads[0], grads[1])


def solution(mesh):
    by_token = P(("expert", "rep"), "tensor", None)
    both = P("expert", "tensor")
    return jax.shard_map(
        functools.partial(on_device, mesh.shape["expert"]),
        mesh=mesh,
        in_specs=(by_token, P(("expert", "rep"), None), by_token, P(), by_token, both, both, both, both, both, P("expert"), P("expert"),
                  P("expert", None), P("expert", None, "tensor"), P("expert", "tensor", None)),
        out_specs=(by_token, by_token, both, both, both, both, both, P("expert"), P("expert"), P("expert", None),
                   P("expert", None, "tensor"), P("expert", "tensor", None)),
        check_vma=False,
    )
```

```python
import functools
import math

import jax
import jax.numpy as jnp
from jax import lax
from jax.experimental import pallas as pl
from jax.experimental.pallas import tpu as pltpu
from jax.sharding import PartitionSpec as P

HEAD = 64
CAP = 12
QB = 128
TABLE = 66
epsilon = 1e-06
masked_value = -1e30
thresholds = (16, 19, 21, 24, 27, 31, 35, 40, 46, 52, 59, 67, 77, 87, 99, 113)
lowest = tuple(range(16)) + thresholds
f32 = jnp.float32
bf16 = jnp.bfloat16
i32 = jnp.int32
NN = (((1,), (0,)), ((), ()))
NT = (((1,), (1,)), ((), ()))
TN = (((0,), (0,)), ((), ()))
VM = pl.BlockSpec(memory_space=pltpu.VMEM)
SM = pl.BlockSpec(memory_space=pltpu.SMEM)
sd = jax.ShapeDtypeStruct


def dot(a, b, dims=NN):
    return lax.dot_general(a, b, dims, preferred_element_type=f32)


ANY = pl.BlockSpec(memory_space=pl.ANY)
TIMES = {"attn_fwd": 13, "attn_bwd": 18, "attn_grad": 9, "project": 5, "moe": 300, "expert_grad": 30, "back": 5, "route": 4}


def cost(name):
    return pl.CostEstimate(flops=TIMES.get(name, 3) * 1_150_000_000, bytes_accessed=1000, transcendentals=0)


def call(kernel, name, outs, operands, scratch=(), smem=0, flops=0, moved=4_000_000, deps=()):
    given = len(operands)

    def body(*refs):
        kernel(*refs[:given], *refs[given + len(deps):])

    return pl.pallas_call(
        body,
        out_shape=tuple(outs),
        in_specs=[SM] * smem + [VM] * (given - smem) + [ANY] * len(deps),
        out_specs=tuple(VM for _ in outs),
        scratch_shapes=list(scratch),
        compiler_params=pltpu.CompilerParams(vmem_limit_bytes=56 << 20),
        cost_estimate=cost(name),
        name=name,
    )(*operands, *deps)


def after(value, *deps):
    return pl.pallas_call(
        lambda *refs: None,
        out_shape=sd(value.shape, value.dtype),
        in_specs=[ANY] * (1 + len(deps)),
        out_specs=ANY,
        input_output_aliases={0: 0},
        name="after",
    )(value, *deps)


def to_tensor(a, flip):
    return lax.ppermute(a, "tensor", [(i, i ^ flip) for i in range(4)])


def to_expert(a, shift, size):
    return lax.ppermute(a, "expert", [(i, (i + shift) % size) for i in range(size)])


def to_core(a):
    return lax.ppermute(a, "rep", [(0, 1), (1, 0)])


def shifted(blocks):
    size = len(blocks)
    return [blocks[0]] + [to_expert(blocks[k], k, size) for k in range(1, size)]


def gather_pieces(own, half):
    px = to_tensor(own, 1)
    py = to_tensor(own, 2)
    d0 = to_tensor(px[:half], 2)
    d1 = to_tensor(py[half:], 1)
    return own, px, py, d0, d1


def gather_direct(own):
    return (own, *[to_tensor(own, flip) for flip in (1, 2, 3)])


def late_kernel(x_late, y_late, got_x, got_y, sum_x, sum_y):
    sum_x[...] = (x_late[...].astype(f32) + got_y[0].astype(f32)).astype(bf16)
    sum_y[...] = (y_late[...].astype(f32) + got_x[0].astype(f32)).astype(bf16)


def scatter_end(got_x, got_y, x_late, y_late, deps):
    shape = sd(x_late.shape, bf16)
    sent = call(late_kernel, "late", [shape, shape], (x_late, y_late, got_x, got_y), deps=deps)
    return (got_x, to_tensor(sent[1], 2), got_y, to_tensor(sent[0], 1)), sent


def scatter_direct(own, *pieces):
    return (own, *[to_tensor(piece, flip) for flip, piece in zip((1, 2, 3), pieces)])


def add_terms(refs):
    return sum(r[...].astype(f32) for r in refs)


def onehot(index, width):
    return lax.broadcasted_iota(i32, (index.shape[0], width), 1) == index


def as_bf16(mask):
    return jnp.where(mask, 1.0, 0.0).astype(bf16)


def prepare_kernel(size, chunks, me_ref, routes_ref, capacity_ref, idx_ref):
    count = routes_ref.shape[1]
    experts = capacity_ref.shape[1]
    local = experts // size
    part = local // chunks
    me = me_ref[0]
    first, second = (jnp.broadcast_to(routes_ref[j:j + 1, :], (8, count)).T[:, 0:1] for j in (0, 1))
    both = as_bf16(onehot(first, experts)) + as_bf16(onehot(second, experts))
    rows = lax.broadcasted_iota(i32, (count, count), 0)
    cols = lax.broadcasted_iota(i32, (count, count), 1)
    before = dot(as_bf16(cols < rows), both)
    capacity = capacity_ref[...].astype(f32)
    shift = int(math.log2(local))
    columns = []
    for route in (first, second):
        mine = onehot(route, experts)
        position = jnp.sum(jnp.where(mine, before, 0.0), axis=1, keepdims=True)
        limit = jnp.sum(jnp.where(mine, jnp.broadcast_to(capacity, mine.shape), 0.0), axis=1, keepdims=True)
        keep = position < limit
        position = position.astype(i32)
        owner = lax.shift_right_logical(route, jnp.full_like(route, shift))
        inner = route & (local - 1)
        away = (owner - me + size) & (size - 1)
        chunk = lax.shift_right_logical(inner, jnp.full_like(route, int(math.log2(part))))
        slot = ((chunk * size + away) * part + (inner & (part - 1))) * CAP + position
        columns += [route, jnp.where(keep, slot, -1), jnp.where(keep, away * local + inner, -1), away * CAP + position]
    for n, column in enumerate(columns):
        idx_ref[:, n:n + 1] = column


def spread_kernel(first, idx_ref, rows_ref, *outs):
    block = outs[0].shape[0]
    width = block * len(outs)
    spread = as_bf16(onehot(idx_ref[:, 1:2] - first, width)) + as_bf16(onehot(idx_ref[:, 5:6] - first, width))
    slots = dot(spread, rows_ref[...], TN).astype(bf16)
    for n, ref in enumerate(outs):
        ref[...] = slots[n * block:(n + 1) * block]


def spread(idx, rows, chunk, blocks, block, deps, name):
    return call(functools.partial(spread_kernel, chunk * blocks * block), name, [sd((block, rows.shape[1]), bf16)] * blocks, (idx, rows),
                flops=400_000_000, moved=2_000_000, deps=deps)


def order_matrix(size, part, block, extra, out_extra):
    rows = part * size * CAP
    m = [[0.0] * (size * block) for _ in range(rows + out_extra)]
    for e in range(part):
        for k in range(size):
            for c in range(CAP):
                m[(e * size + k) * CAP + c][k * block + e * CAP + c] = 1.0
    for r in range(extra):
        for k in range(size):
            m[rows + r][k * block + part * CAP + r] = 1.0
    return jnp.array(m, dtype=bf16)


def reorder_kernel(count, m_ref, *refs):
    blocks, out_ref = refs[:count], refs[count]
    out_ref[...] = dot(m_ref[...], jnp.concatenate([b[...] for b in blocks], axis=0)).astype(bf16)


def reorder(matrix, blocks, name, deps=()):
    rows = matrix.shape[0]
    width = blocks[0].shape[1]
    return call(functools.partial(reorder_kernel, len(blocks)), name, [sd((rows, width), bf16)], (matrix, *blocks),
                flops=2 * matrix.size * width, moved=2 * rows * width * 2, deps=deps)[0]


def give_back_kernel(count, extra, m_ref, *refs):
    outs = refs[4:]
    total = add_terms(refs[:4]).astype(bf16)
    rows = m_ref.shape[0]
    back = dot(m_ref[...], total[0:rows], TN).astype(bf16)
    block = back.shape[0] // count
    for k in range(count):
        outs[k][0:block, :] = back[k * block:(k + 1) * block]
        if extra:
            outs[k][block:, :] = total[rows:]


def give_back_halves_kernel(count, m_ref, own_a, own_b, got_x, late_y, got_y, late_x, *outs):
    halves = (own_a[...].astype(f32) + got_x[1].astype(f32) + late_y[...].astype(f32), own_b[...].astype(f32) + got_y[1].astype(f32) + late_x[...].astype(f32))
    for n, total in enumerate(halves):
        back = dot(m_ref[...], total.astype(bf16), TN).astype(bf16)
        block = back.shape[0] // count
        for k in range(count):
            outs[k][n * block:(n + 1) * block, :] = back[k * block:(k + 1) * block]


def pack_kernel(at_ref, q_ref, k_ref, v_ref, r_ref, o_ref, ga_ref, gm_ref, t_ref, out_ref, full):
    rows, width = q_ref.shape
    full[...] = jnp.zeros_like(full)
    place = 0
    for ref in (q_ref, k_ref, v_ref, r_ref, o_ref):
        value = ref[...].astype(f32)
        value = value.T if ref is r_ref else value
        full[:, place:place + value.shape[1]] = value
        place += value.shape[1]
    for ref in (ga_ref, gm_ref):
        full[:, place:place + 1] = column_of(ref[...].astype(f32)[None, :])
        place += 1
    full[0:t_ref.shape[1], place:place + t_ref.shape[0]] = t_ref[...].astype(f32).T
    half = rows // 2
    for r in (0, 1):
        @pl.when(at_ref[1] == r)
        def _():
            out_ref[...] = full[r * half:(r + 1) * half, :].astype(bf16)


def join_kernel(*refs):
    rows = refs[0].shape[0]
    for n, ref in enumerate(refs[:-1]):
        refs[-1][n * rows:(n + 1) * rows, :] = ref[...]


def unpack_kernel(size, at_ref, *refs):
    mine, other = refs[:size], refs[size]
    full, qkv_ref, wo_ref, router_ref, gains_ref, table_ref = refs[size + 1:]
    me, rep = at_ref[0], at_ref[1]
    half = mine[0].shape[0]
    for k in range(size):
        z = (me - k + size) & (size - 1)
        full[2 * z + rep] = mine[k][...].astype(f32)
        full[2 * z + 1 - rep] = other[k * half:(k + 1) * half, :].astype(f32)
    full = jnp.concatenate([full[n] for n in range(2 * size)], axis=0)
    qkv_ref[...] = full[:, 0:576].astype(bf16)
    router_ref[...] = full[:, 576:640].astype(bf16)
    wo_ref[...] = full[:, 640:832].astype(bf16)
    tail = full[:, 768:896]
    turned = tail.T
    gains_ref[...] = turned[64:72, :]
    rows = table_ref.shape[0] // size
    for z in range(size):
        table_ref[z * rows:(z + 1) * rows, :] = tail[z * 2 * half: z * 2 * half + rows, :]


def unpack(at, mine, other, buckets):
    size = len(mine)
    half, cols = mine[0].shape
    width = 2 * half * size

    def kernel(at_ref, *refs):
        unpack_kernel(size, at_ref, *refs[:size + 1], refs[-1], *refs[size + 1:-1])

    outs = [sd((width, 576), bf16), sd((width, 192), bf16), sd((width, 64), bf16), sd((8, width), f32), sd((buckets, 128), f32)]
    return call(kernel, "unpack", outs, (at, *mine, other), scratch=[pltpu.VMEM((2 * size, half, cols), f32)], smem=1)


def piece_shapes(rows, width):
    return [sd((rows, width), bf16)] * 4


def near_offset():
    rows = lax.broadcasted_iota(jnp.int32, (QB, 2 * QB), 0)
    cols = lax.broadcasted_iota(jnp.int32, (QB, 2 * QB), 1)
    return QB + rows - cols


def near_bias(table_ref, head, buckets):
    off = near_offset()
    bias = jnp.where(off < 0, masked_value, table_ref[0, TABLE + head])
    for b in range(1, buckets):
        bias = jnp.where(off >= lowest[b], table_ref[b, TABLE + head], bias)
    return bias


def scores_of(q, k_ref, head, i, near, far, seg_col, seg_row_ref):
    lo = max(i - 1, 0) * QB
    hi = (i + 1) * QB
    s = dot(q, k_ref[head, 0:hi], NT)
    bias = near[:, QB:] if i == 0 else near
    same_near = seg_col == seg_row_ref[:, lo:hi]
    s_near = jnp.where(same_near, s[:, lo:hi] + bias, masked_value)
    if lo == 0:
        return s_near
    same_far = seg_col == seg_row_ref[:, 0:lo]
    s_far = jnp.where(same_far, s[:, 0:lo] + far, masked_value)
    return jnp.concatenate([s_far, s_near], axis=1)


def project_kernel(at_ref, own_ref, px_ref, py_ref, pd0_ref, pd1_ref, w_ref, gain_ref, xn_ref, qkv_ref):
    pos = at_ref[2]
    tok = own_ref.shape[0]
    half = tok // 2
    gain = gain_ref[0:1, :]

    def put(rows, flip, start=0):
        x = rows.astype(f32)
        r = lax.rsqrt(jnp.mean(x * x, axis=-1, keepdims=True) + epsilon)
        xn = (x * r * gain).astype(bf16)
        at = pl.ds(pl.multiple_of((pos ^ flip) * tok + start, half), rows.shape[0])
        xn_ref[at, :] = xn
        qkv_ref[at, :] = dot(xn, w_ref[...]).astype(bf16)

    put(own_ref[...], 0)
    put(px_ref[...], 1)
    put(py_ref[...], 2)
    put(pd0_ref[...], 3)
    put(pd1_ref[...], 3, half)


def column_of(row):
    return jnp.broadcast_to(row, (8, row.shape[1])).T[:, 0:1]


def attn_fwd_kernel(heads, at_ref, table_ref, qkv_ref, segr_ref, wo_ref, o_ref, lse_ref, out_own, out_x, out_y, out_d, qs, ks, vs, seg):
    pos = at_ref[2]
    tok = out_own.shape[0]
    half = tok // 2
    buckets = table_ref.shape[0]
    seg[...] = column_of(segr_ref[...])

    def at(flip, start=0, size=tok):
        return pl.ds(pl.multiple_of((pos ^ flip) * tok + start, half), size)

    width = heads * HEAD
    qkv = qkv_ref[...]
    for h in range(heads):
        qs[h] = qkv[:, h * HEAD:(h + 1) * HEAD] * bf16(0.125)
        ks[h] = qkv[:, width + h * HEAD: width + (h + 1) * HEAD]
        vs[h] = qkv[:, 2 * width + h * HEAD: 2 * width + (h + 1) * HEAD]
    blocks = qkv_ref.shape[0] // QB
    for h in range(heads):
        near = near_bias(table_ref, h, buckets)
        far = table_ref[buckets - 1, TABLE + h]
        for i in range(blocks):
            rows = slice(i * QB, (i + 1) * QB)
            s = scores_of(qs[h, rows], ks, h, i, near, far, seg[rows, :], segr_ref)
            top = jnp.max(s, axis=-1, keepdims=True)
            e = jnp.exp(s - top)
            total = jnp.sum(e, axis=-1, keepdims=True)
            p = (e * (1.0 / total)).astype(bf16)
            o_ref[rows, h * HEAD:(h + 1) * HEAD] = dot(p, vs[h, 0:(i + 1) * QB]).astype(bf16)
            lse_ref[rows, h:h + 1] = top + jnp.log(total)
    wo = wo_ref[...]
    for flip, ref in enumerate((out_own, out_x, out_y, out_d)):
        ref[...] = dot(o_ref[at(flip), :], wo, NT).astype(bf16)


def attn_bwd_kernel(heads, size, at_ref, table_ref, own_ref, px_ref, py_ref, pd_ref, segr_ref, wo_ref, qkv_ref, lse_ref,
                    gtab_ref, dqkv, dh, qs, ks, vs, do, dk, dv, acc, seg):
    pos = at_ref[2]
    tok = own_ref.shape[0]
    half = tok // 2
    buckets = table_ref.shape[0]
    width = heads * HEAD

    def at(flip, start=0, size=tok):
        return pl.ds(pl.multiple_of((pos ^ flip) * tok + start, half), size)

    seg[...] = column_of(segr_ref[...])
    dh[at(0), :] = own_ref[...]
    dh[at(1), :] = px_ref[...]
    dh[at(2), :] = py_ref[...]
    dh[at(3), :] = pd_ref[...]
    dall = dot(dh[...], wo_ref[...]).astype(bf16)
    for h in range(heads):
        do[h] = dall[:, h * HEAD:(h + 1) * HEAD]
        qs[h] = qkv_ref[:, h * HEAD:(h + 1) * HEAD] * bf16(0.125)
        ks[h] = qkv_ref[:, width + h * HEAD: width + (h + 1) * HEAD]
        vs[h] = qkv_ref[:, 2 * width + h * HEAD: 2 * width + (h + 1) * HEAD]
    blocks = qkv_ref.shape[0] // QB
    off = near_offset()
    per = gtab_ref.shape[1]
    gtab_ref[...] = jnp.zeros_like(gtab_ref)
    for h in range(heads):
        near = near_bias(table_ref, h, buckets)
        far = table_ref[buckets - 1, TABLE + h]
        acc[...] = jnp.zeros_like(acc)
        dk[...] = jnp.zeros_like(dk)
        dv[...] = jnp.zeros_like(dv)
        far_sum = jnp.zeros((QB, 1), f32)
        for i in range(blocks):
            rows = slice(i * QB, (i + 1) * QB)
            lo = max(i - 1, 0) * QB
            hi = (i + 1) * QB
            q = qs[h, rows]
            s = scores_of(q, ks, h, i, near, far, seg[rows, :], segr_ref)
            p = jnp.exp(s - lse_ref[rows, h:h + 1])
            g = do[h, rows]
            dv[0:hi] += dot(p.astype(bf16), g, TN)
            dp = dot(g, vs[h, 0:hi], NT)
            pd = p * dp
            ds = (pd - p * jnp.sum(pd, axis=-1, keepdims=True)).astype(bf16)
            dq = dot(ds, ks[h, 0:hi]) * 0.125
            dqkv[rows, h * HEAD:(h + 1) * HEAD] = dq.astype(bf16)
            dk[0:hi] += dot(ds, q, TN)
            dsf = ds.astype(f32)
            if i == 0:
                acc[:, QB:] += dsf
            else:
                acc[...] += dsf[:, lo:hi]
            if lo > 0:
                far_sum = far_sum + jnp.sum(dsf[:, 0:lo], axis=-1, keepdims=True)
        dqkv[:, width + h * HEAD: width + (h + 1) * HEAD] = dk[...].astype(bf16)
        dqkv[:, 2 * width + h * HEAD: 2 * width + (h + 1) * HEAD] = dv[...].astype(bf16)
        total = acc[...]
        rest = jnp.sum(far_sum, axis=0, keepdims=True)
        for b in range(buckets):
            if b == buckets - 1:
                inside = off >= lowest[b]
            else:
                inside = (off >= lowest[b]) & (off < lowest[b + 1])
            part = jnp.sum(jnp.where(inside, total, 0.0), axis=0, keepdims=True)
            one = jnp.sum(part, axis=1, keepdims=True)
            gtab_ref[b // per, b % per:b % per + 1, TABLE + 1 + h:TABLE + 2 + h] = one + rest if b == buckets - 1 else one


def attn_grad_kernel(size, at_ref, dqkv, w_ref, xn_ref, own_ref, px_ref, py_ref, pd_ref, o_ref, keep_ref, send_ref, gain_ref,
                     out_own, out_x, out_y, out_d, dh, full):
    pos, rep = at_ref[2], at_ref[1]
    tok = out_own.shape[0]
    half = tok // 2
    width = o_ref.shape[1]

    def at(flip, start=0, size=tok):
        return pl.ds(pl.multiple_of((pos ^ flip) * tok + start, half), size)

    dh[at(0), :] = own_ref[...]
    dh[at(1), :] = px_ref[...]
    dh[at(2), :] = py_ref[...]
    dh[at(3), :] = pd_ref[...]
    w = w_ref[...]
    for flip, ref in enumerate((out_own, out_x, out_y, out_d)):
        ref[...] = dot(dqkv[at(flip), :], w, NT).astype(bf16)
    grad = dot(xn_ref[...], dqkv[...], TN)
    gain_sum = jnp.sum(grad * w.astype(f32), axis=1, keepdims=True)
    gain_ref[...] = jnp.broadcast_to(gain_sum, (gain_sum.shape[0], 128)).T[0:8, :]
    grad_out = dot(dh[...], o_ref[...], TN)
    part_rows = keep_ref.shape[1]
    for n in range(2 * size):
        full[n, :, 0:3 * width] = grad[n * part_rows:(n + 1) * part_rows].astype(bf16)
        full[n, :, 3 * width:] = grad_out[n * part_rows:(n + 1) * part_rows].astype(bf16)
    for z in range(size):
        keep_ref[z] = full[2 * z + rep]
        send_ref[z] = full[2 * z + 1 - rep]


def project(at, pieces, w, gains):
    tok, width = pieces[0].shape
    return call(project_kernel, "project", [sd((4 * tok, width), bf16), sd((4 * tok, w.shape[1]), bf16)], (at, *pieces, w, gains),
                smem=1, flops=2_000_000_000, moved=5_000_000)


def attn_fwd(at, table, qkv, segr, wo, deps):
    width = wo.shape[0]
    length = qkv.shape[0]
    heads = wo.shape[1] // HEAD
    outs = [sd((length, heads * HEAD), bf16), sd((length, heads), f32)]
    return call(functools.partial(attn_fwd_kernel, heads), "attn_fwd", outs + piece_shapes(length // 4, width),
                (at, table, qkv, segr, wo),
                scratch=[pltpu.VMEM((heads, length, HEAD), bf16)] * 3 + [pltpu.VMEM((length, 1), i32)], smem=2,
                flops=8_000_000_000, moved=5_000_000, deps=deps)


def attn_bwd(at, size, table, pieces, segr, wo, qkv, lse, deps):
    tok, width = pieces[0].shape
    length = qkv.shape[0]
    heads = wo.shape[1] // HEAD
    outs = [sd((size, table.shape[0] // size, 128), f32), sd(qkv.shape, bf16)]
    scratch = [pltpu.VMEM((length, width), bf16)] + [pltpu.VMEM((heads, length, HEAD), bf16)] * 4 + [pltpu.VMEM((length, HEAD), f32)] * 2
    scratch += [pltpu.VMEM((QB, 2 * QB), f32), pltpu.VMEM((length, 1), i32)]
    return call(functools.partial(attn_bwd_kernel, heads, size), "attn_bwd", outs, (at, table, *pieces, segr, wo, qkv, lse),
                scratch=scratch, smem=2, flops=12_000_000_000, moved=8_000_000, deps=deps)


def attn_grad(at, size, dqkv, w, xn, pieces, o, deps):
    tok, width = pieces[0].shape
    cols = w.shape[1] + o.shape[1]
    rows = width // (2 * size)
    outs = [sd((size, rows, cols), bf16)] * 2 + [sd((8, width), f32)] + piece_shapes(tok, width)
    return call(functools.partial(attn_grad_kernel, size), "attn_grad", outs, (at, dqkv, w, xn, *pieces, o),
                scratch=[pltpu.VMEM((4 * tok, width), bf16), pltpu.VMEM((2 * size, rows, cols), bf16)], smem=1,
                flops=4_000_000_000, moved=9_000_000, deps=deps)


def route_kernel(size, chunks, idx_ref, tokens_ref, own, rx, ry, rd, router_ref, gains_ref, h_ref, xn_ref, probs_ref, gate_ref, *blocks):
    count, width = tokens_ref.shape
    experts = router_ref.shape[1]
    local = experts // size
    rows_of = local // chunks * CAP
    lanes = lanes_of(size)
    h = tokens_ref[...].astype(f32) + add_terms((own, rx, ry, rd))
    r = lax.rsqrt(jnp.mean(h * h, axis=-1, keepdims=True) + epsilon)
    xn = (h * r * gains_ref[1:2, :]).astype(bf16)
    h_ref[...] = h
    xn_ref[...] = xn
    logits = dot(xn, router_ref[...])
    e = jnp.exp(logits - jnp.max(logits, axis=-1, keepdims=True))
    probs = e / jnp.sum(e, axis=-1, keepdims=True)
    probs_ref[...] = probs
    picked = [jnp.sum(jnp.where(onehot(idx_ref[:, 4 * j:4 * j + 1], experts), probs, 0.0), axis=-1, keepdims=True) for j in (0, 1)]
    total = picked[0] + picked[1]
    gates = [p / total for p in picked]
    gate_ref[:, 0:1], gate_ref[:, 1:2], gate_ref[:, 2:3] = gates[0], gates[1], total
    spread = as_bf16(onehot(idx_ref[:, 1:2], size * rows_of)) + as_bf16(onehot(idx_ref[:, 5:6], size * rows_of))
    slots = dot(spread, xn, TN).astype(bf16)
    held = jnp.zeros((experts, lanes), f32)
    for j in (0, 1):
        to = as_bf16(onehot(idx_ref[:, 4 * j + 2:4 * j + 3], experts))
        at = jnp.where(onehot(idx_ref[:, 4 * j + 3:4 * j + 4], lanes), gates[j], 0.0).astype(bf16)
        held = held + dot(to, at, TN)
    for k, ref in enumerate(blocks):
        ref[0:rows_of, :] = slots[k * rows_of:(k + 1) * rows_of]
        ref[rows_of:, :] = jnp.zeros((16, width), bf16)
        ref[rows_of:rows_of + local, 0:lanes] = held[k * local:(k + 1) * local].astype(bf16)


def lanes_of(size):
    return -(-size * CAP // 128) * 128


def route(idx, tokens, parts, router, gains, size, chunks, deps):
    count, width = tokens.shape
    experts = router.shape[1]
    rows_of = experts // size // chunks * CAP
    outs = [sd((count, width), f32), sd((count, width), bf16), sd((count, experts), f32), sd((count, 8), f32)]
    outs += [sd((rows_of + 16, width), bf16)] * size
    return call(functools.partial(route_kernel, size, chunks), "route", outs, (idx, tokens, *parts, router, gains),
                flops=400_000_000, moved=5_000_000, deps=deps)


def moe_kernel(rows, part, offset, last, skip, at_ref, own, px, py, far, e_own, e_px, e_py, e_d, g_own, g_px, g_py, g_d0, g_d1, win_ref, wout_ref,
               dg_in, *refs):
    outs, y_outs, dg_ref, acts = refs[skip:skip + 4], refs[skip + 4:-2], refs[-2], refs[-1]
    e, j = pl.program_id(0), pl.program_id(1)
    steps = pl.num_programs(1)

    @pl.when((e == 0) & (j == 0))
    def _():
        dg_ref[...] = dg_in[...]

    wide = e_own.shape[1]
    pick = lax.broadcasted_iota(i32, (16, wide), 0) == e + offset
    square = lax.broadcasted_iota(i32, (rows, wide), 0) + j * rows == lax.broadcasted_iota(i32, (rows, wide), 1)

    def gate_of(ref):
        row = jnp.sum(jnp.where(pick, ref[...].astype(f32), 0.0), axis=0, keepdims=True)
        return jnp.sum(jnp.where(square, jnp.broadcast_to(row, square.shape), 0.0), axis=1, keepdims=True)

    def keep(n, value):
        for flip in range(4):
            acts[n, 0, flip] = value[flip * rows:(flip + 1) * rows]

    def put(value, outs):
        at = pl.ds(pl.multiple_of((e * steps + j) * rows, 16), rows)
        for flip, ref in enumerate(outs):
            ref[at, :] = value[flip * rows:(flip + 1) * rows]

    gate = jnp.concatenate([gate_of(r) for r in (e_own, e_px, e_py, e_d)], axis=0)
    s = jnp.concatenate([own[...], px[...], py[...], far[...]], axis=0)
    g_far = jnp.where(e < part // 2, g_d0[...].astype(f32), g_d1[...].astype(f32))
    g = jnp.concatenate([g_own[...].astype(f32), g_px[...].astype(f32), g_py[...].astype(f32), g_far], axis=0)
    keep(0, s)
    win, wout = win_ref[0], wout_ref[0]
    dy = (g * gate).astype(bf16)
    keep(1, dy)
    a = dot(s, win)
    dhid = dot(dy, wout, NT)
    c = math.sqrt(2.0 / math.pi)
    t = jnp.tanh(a * (c + (c * 0.044715) * (a * a)))
    up = 0.5 + 0.5 * t
    hid = (a * up).astype(bf16)
    slope = up + (0.5 * a) * (1.0 - t * t) * (c + (3 * c * 0.044715) * (a * a))
    da = (dhid * slope).astype(bf16)
    keep(2, hid)
    keep(3, da)
    put(dot(da, win, NT).astype(bf16), outs)
    y = dot(hid, wout)
    ones = jnp.ones((8, y.shape[1]), bf16)
    sums = dot(ones, (y * g).astype(bf16), NT)
    if len(y_outs) == 4:
        put(y.astype(bf16), y_outs)
    else:
        near = 1 if offset == 0 else 2
        own_ref, pack, once = y_outs
        put(y.astype(bf16), [own_ref] + ([pack.at[1], once] if near == 1 else [once, pack.at[1]]) + [pack.at[0]])
    for flip in range(4):
        row = sums[0:1, flip * rows:(flip + 1) * rows]
        dg_ref[flip, j, pl.ds(e + offset, 1), 0:rows] = row

    if last:
        @pl.when((e == part - 1) & (j == steps - 1))
        def _():
            for flip, ref in enumerate(outs):
                ref[-16:, :] = jnp.zeros((16, ref.shape[1]), bf16)
                for n in range(wide // 128):
                    ref[-16:, n * 128:(n + 1) * 128] = dg_ref[flip, n].astype(bf16)


def moe(at, size, chunks, chunk, pieces, extras, g, w_in, w_out, dg, deps):
    all_rows = size * CAP
    rows = 128 if all_rows % 128 == 0 else all_rows
    steps = all_rows // rows
    local, width, hidden = w_in.shape
    part = local // chunks
    half = part // 2
    lanes = -(-all_rows // 128) * 128
    first = chunk * part
    whole = lambda e, j: (e * steps + j, 0)
    flat = pl.BlockSpec((rows, width), whole)
    low = pl.BlockSpec((rows, width), lambda e, j: (jnp.where(e < half, e * steps + j, half * steps - 1), 0))
    high = pl.BlockSpec((rows, width), lambda e, j: (jnp.where(e < half, 0, (e - half) * steps + j), 0))
    ext = pl.BlockSpec((16, lanes), lambda e, j: (part * all_rows // 16, 0))
    in_specs = [SM] + [flat] * 4 + [ext] * 4 + [flat] * 3 + [low, high]
    in_specs += [pl.BlockSpec((1, width, hidden), lambda e, j: (first + e, 0, 0)), pl.BlockSpec((1, hidden, width), lambda e, j: (first + e, 0, 0))]
    operands = [at, *pieces, *extras, *g, w_in, w_out]
    last = chunk == chunks - 1
    shape = (part * all_rows + 16 * last, width)
    total = part * all_rows
    y_shapes = [(total, width), (2, total, width), (total, width)] if chunks == 2 else [(total, width)] * 4
    outs = [sd(shape, bf16)] * 4 + [sd(y, bf16) for y in y_shapes] + [sd(dg.shape, f32), sd((4, part, 4, all_rows, width), bf16)]
    every = lambda dims: pl.BlockSpec(dims, lambda e, j: (0,) * len(dims))
    out_specs = [every(shape)] * 4 + [every(y) for y in y_shapes]
    out_specs += [every(dg.shape), pl.BlockSpec((4, 1, 4, rows, width), lambda e, j: (0, e, 0, j, 0))]
    operands.append(dg)
    in_specs.append(every(dg.shape))
    operands += list(deps)
    in_specs += [ANY] * len(deps)
    return pl.pallas_call(
        functools.partial(moe_kernel, rows, part, first, last, len(deps)),
        grid=(part, steps),
        out_shape=tuple(outs), in_specs=in_specs, out_specs=tuple(out_specs),
        compiler_params=pltpu.CompilerParams(vmem_limit_bytes=58 << 20),
        cost_estimate=cost("moe"),
        name="moe",
    )(*operands)


def expert_grad_kernel(steps, at_ref, mine, other, *refs):
    gin, gout, mark = refs[-3:]
    mark[...] = jnp.zeros_like(mark)

    def put(a, b):
        both = [jnp.concatenate([r[n, 0, flip] for r in (a, b) for flip in range(4)], axis=0) for n in range(4)]
        for ref, left, right in ((gin, both[0], both[3]), (gout, both[2], both[1])):
            if steps == 1:
                ref[0] = dot(left, right, TN)
            else:
                part = dot(left, right, TN)
                ref[0] = jnp.where(pl.program_id(1) == 0, part, ref[0] + part)

    pl.when(at_ref[1] == 0)(lambda: put(mine, other))
    pl.when(at_ref[1] == 1)(lambda: put(other, mine))


def expert_grad(at, first, start, part, local, mine, other, before, deps):
    four, all_rows, width = mine.shape[2:]
    rows = 128 if all_rows % 128 == 0 else all_rows
    steps = all_rows // rows
    spec = pl.BlockSpec((4, 1, 4, rows, width), lambda e, j: (0, start + e, 0, j, 0))
    in_specs = [SM, spec, spec]
    operands = [at, mine, other]
    alias = {}
    if before:
        alias = {3: 0, 4: 1}
        operands += list(before)
        in_specs += [ANY] * 2
    operands += list(deps)
    in_specs += [ANY] * len(deps)
    out = pl.BlockSpec((1, width, width), lambda e, j: (first + start + e, 0, 0))
    return pl.pallas_call(
        functools.partial(expert_grad_kernel, steps),
        grid=(part, steps),
        out_shape=(sd((local, width, width), f32),) * 2 + (sd((8, 128), f32),), in_specs=in_specs,
        out_specs=(out, out, pl.BlockSpec((8, 128), lambda e, j: (0, 0))),
        input_output_aliases=alias,
        compiler_params=pltpu.CompilerParams(vmem_limit_bytes=56 << 20),
        cost_estimate=cost("expert_grad"),
        name="expert_grad",
    )(*operands)


def back_kernel(size, chunks, idx_ref, cot_ref, h_ref, xn_ref, probs_ref, gate_ref, router_ref, gains_ref, *refs):
    blocks = refs[:chunks * size]
    dh_ref, dhb_ref, small_ref, ds = refs[chunks * size:]
    experts = router_ref.shape[1]
    local = experts // size
    rows_of = local // chunks * CAP
    lanes = lanes_of(size)
    for n, block in enumerate(blocks):
        ds[n * rows_of:(n + 1) * rows_of, :] = block[0:rows_of, :]
    last = blocks[(chunks - 1) * size:]
    held = jnp.concatenate([last[k][rows_of:rows_of + local, 0:lanes].astype(f32) for k in range(size)], axis=0).astype(bf16)
    spread = as_bf16(onehot(idx_ref[:, 1:2], experts * CAP)) + as_bf16(onehot(idx_ref[:, 5:6], experts * CAP))
    dxn = dot(spread, ds[...])
    probs = probs_ref[...]
    gates, dgates, chosen = [], [], []
    for j in (0, 1):
        got = dot(as_bf16(onehot(idx_ref[:, 4 * j + 2:4 * j + 3], experts)), held)
        dgates.append(jnp.sum(jnp.where(onehot(idx_ref[:, 4 * j + 3:4 * j + 4], lanes), got, 0.0), axis=-1, keepdims=True))
        gates.append(gate_ref[:, j:j + 1])
        chosen.append(onehot(idx_ref[:, 4 * j:4 * j + 1], experts))
    mean = gates[0] * dgates[0] + gates[1] * dgates[1]
    scale = 1.0 / gate_ref[:, 2:3]
    dprobs = jnp.where(chosen[0], (dgates[0] - mean) * scale, 0.0) + jnp.where(chosen[1], (dgates[1] - mean) * scale, 0.0)
    dlogits = (probs * (dprobs - jnp.sum(probs * dprobs, axis=-1, keepdims=True))).astype(bf16)
    small_ref[...] = jnp.zeros_like(small_ref)
    small_ref[:, 0:experts] = dot(xn_ref[...], dlogits, TN).astype(bf16)
    dxn = dxn + dot(dlogits, router_ref[...], NT)
    h = h_ref[...]
    r = lax.rsqrt(jnp.mean(h * h, axis=-1, keepdims=True) + epsilon)
    gain_row = jnp.sum(dxn * h * r, axis=0, keepdims=True)
    small_ref[:, experts:experts + 1] = column_of(gain_row).astype(bf16)
    scaled = dxn * gains_ref[1:2, :]
    dh = cot_ref[...].astype(f32) + r * scaled - h * (r * r * r) * jnp.mean(h * scaled, axis=-1, keepdims=True)
    dh_ref[...] = dh
    dhb_ref[...] = dh.astype(bf16)


def back(idx, cot, h, xn, probs, gate, router, gains, blocks, size, chunks, deps):
    count, width = h.shape
    experts = router.shape[1]
    outs = [sd((count, width), f32), sd((count, width), bf16), sd((width, 128), bf16)]
    return call(functools.partial(back_kernel, size, chunks), "back", outs, (idx, cot, h, xn, probs, gate, router, gains, *blocks),
                scratch=[pltpu.VMEM((experts * CAP, width), bf16)], deps=deps)


def mix_kernel(count, chunks, idx_ref, h_ref, gate_ref, *refs):
    blocks, out_ref, ys = refs[:count], refs[count], refs[count + 1]
    rows_of = blocks[0].shape[0]
    part = rows_of // chunks
    for k, block in enumerate(blocks):
        for c in range(chunks):
            ys[(c * count + k) * part:(c * count + k + 1) * part, :] = block[c * part:(c + 1) * part, :]
    out = h_ref[...]
    for j in (0, 1):
        out = out + gate_ref[:, j:j + 1] * dot(as_bf16(onehot(idx_ref[:, 4 * j + 1:4 * j + 2], rows_of * count)), ys[...])
    out_ref[...] = out.astype(bf16)


def mix(idx, h, gate, blocks, size, chunks):
    count, width = h.shape
    return call(functools.partial(mix_kernel, len(blocks), chunks), "mix", [sd((count, width), bf16)], (idx, h, gate, *blocks),
                scratch=[pltpu.VMEM((len(blocks) * blocks[0].shape[0], width), bf16)])[0]


def last_kernel(tokens_ref, dh_ref, own, rx, ry, rd, gains_ref, out_ref):
    x = tokens_ref[...].astype(f32)
    r = lax.rsqrt(jnp.mean(x * x, axis=-1, keepdims=True) + epsilon)
    scaled = add_terms((own, rx, ry, rd)) * gains_ref[0:1, :]
    out_ref[...] = dh_ref[...] + r * scaled - x * (r * r * r) * jnp.mean(x * scaled, axis=-1, keepdims=True)


def total_kernel(*refs):
    out = refs[-1]
    out[...] = sum(r[...].astype(f32) for r in refs[:-1])


def merge_kernel(size, at_ref, keep_ref, got_ref, small_ref, gain_ref, gtab_ref, *refs):
    outs, few, gains = refs[:size], refs[size], refs[size + 1]
    me, rep = at_ref[0], at_ref[1]
    half, width = keep_ref.shape[1:]
    rows = gtab_ref.shape[1]
    column = gain_ref[...].T
    for n in range(2 * size):
        few[n] = small_ref[n * half:(n + 1) * half, :].astype(f32)
        gains[n] = column[n * half:(n + 1) * half, :]
    lane = lax.broadcasted_iota(i32, (half, 128), 1)
    for k in range(size):
        to = (me + k) & (size - 1)
        outs[k][:, 0:width] = (keep_ref[to].astype(f32) + got_ref[to].astype(f32)).astype(bf16)
        own = jnp.broadcast_to(gains[2 * to + rep][:, 0:1], lane.shape)
        other = jnp.broadcast_to(gains[2 * to + 1 - rep][:, 0:1], lane.shape)
        tail = jnp.where(lane < TABLE - 1, few[2 * to + rep], jnp.where(lane == TABLE - 1, own, jnp.where(lane == TABLE, other, 0.0)))
        outs[k][:, width:] = tail.astype(bf16)
        outs[k][0:rows, width:] = (tail[0:rows] + gtab_ref[to]).astype(bf16)


def finish_kernel(at_ref, mine_ref, other_ref, gain_ref, q_ref, k_ref, v_ref, o_ref, router_ref, table_ref, ga_ref, gm_ref, few):
    half = mine_ref.shape[0]
    width = q_ref.shape[1]
    experts = router_ref.shape[0]

    def put(first, second):
        for n, ref in enumerate((q_ref, k_ref, v_ref, o_ref)):
            ref[0:half, :] = first[:, n * width:(n + 1) * width]
            ref[half:, :] = second[:, n * width:(n + 1) * width]
        a, b = first[:, 4 * width:], second[:, 4 * width:]
        lane = lax.broadcasted_iota(i32, a.shape, 1)
        few[0:half, :] = jnp.where(lane == TABLE - 1, a + jnp.broadcast_to(b[:, TABLE:TABLE + 1], a.shape), jnp.where(lane > TABLE, a + b, a))
        few[half:, :] = jnp.where(lane == TABLE - 1, b + jnp.broadcast_to(a[:, TABLE:TABLE + 1], b.shape), b)

    pl.when(at_ref[1] == 0)(lambda: put(mine_ref, other_ref))
    pl.when(at_ref[1] == 1)(lambda: put(other_ref, mine_ref))
    turned = few[...].T
    router_ref[...] = turned[0:experts, :]
    table_ref[...] = turned[TABLE + 1:TABLE + 1 + table_ref.shape[0], 0:table_ref.shape[1]]
    ga_ref[...] = turned[TABLE - 1:TABLE, :] / gain_ref[...].astype(f32)
    gm_ref[...] = turned[TABLE - 2:TABLE - 1, :]


def on_device(size, tokens, segments, routes, capacity, cotangent, rel_table, w_query, w_key, w_value, w_attn_out, gain_attn, gain_moe, w_router, w_in, w_out):
    z = lax.axis_index("expert").astype(i32)
    rep = lax.axis_index("rep").astype(i32)
    pos = lax.axis_index("tensor").astype(i32)
    at = jnp.stack([z, rep, pos])
    tok = tokens[0]
    cot = cotangent[0]
    count, width = tok.shape
    local = w_in.shape[0]
    experts = w_router.shape[1]
    chunks = 2 if local >= 4 else 1
    part = local // chunks
    rows_dev = w_query.shape[0]
    half = rows_dev // 2
    buckets = rel_table.shape[0] * size
    part_rows = part * CAP
    half_rows = part_rows * size // 2
    matrix = order_matrix(size, part, part_rows, 0, 0)

    packed = call(pack_kernel, "pack", [sd((half, 896), bf16)],
                  (at, w_query, w_key, w_value, w_router.T, w_attn_out, gain_attn, gain_moe, rel_table.T),
                  scratch=[pltpu.VMEM((rows_dev, 896), f32)], smem=1)[0]
    mine = [packed] + [to_expert(packed, k, size) for k in range(1, size)]
    idx = call(functools.partial(prepare_kernel, size, chunks), "prepare", [sd((count, 8), i32)], (z[None], routes[0].T, capacity[None]),
               smem=1, deps=(packed,))[0]
    pieces = gather_pieces(tok, count // 2)
    joined = call(join_kernel, "join", [sd((size * half, packed.shape[1]), bf16)], tuple(mine), deps=(*pieces[1:3], idx))[0]
    qkv_w, wo, router, gains, table = unpack(at, mine, to_core(joined), buckets)

    g_blocks = spread(idx, cot, 0, chunks * size, part_rows, (joined,), "spread_g")
    g_arrived = shifted(g_blocks[:size])

    xn, qkv = project(at, pieces, qkv_w, gains)
    g_ordered = [reorder(matrix, g_arrived, "order_g", (qkv,))]
    g_pieces = [gather_pieces(g_ordered[0], half_rows)]
    ready, window = (g_ordered[0],), g_pieces[0][1:3]
    if chunks == 2:
        g_late = shifted([after(b, g_ordered[0]) for b in g_blocks[size:]])
        window = (*window, *g_late[1:])
    o, lse, own, *parts = attn_fwd(at, table, qkv, segments, wo, ready)
    terms = scatter_direct(own, after(parts[0], *window), *parts[1:])
    h, xn2, probs, gate, *blocks = route(idx, tok, terms, router, gains, size, chunks, ())

    arrived = shifted(blocks)
    if chunks == 2:
        g_ordered.append(reorder(matrix, [after(g_late[0], xn2)] + g_late[1:], "order_g", (*blocks[1:], *g_pieces[0][3:])))
        g_pieces.append(gather_pieces(g_ordered[1], half_rows))
    ordered = [reorder(order_matrix(size, part, part_rows + 16, 16, 16), arrived, "order", g_ordered[1:])]
    got = [gather_direct(ordered[0])]
    if chunks == 2:
        blocks = spread(idx, xn2, 1, size, part_rows, (ordered[0], *g_pieces[1][1:]), "spread")
        ordered.append(reorder(matrix, shifted(blocks), "order"))
        got.append(gather_direct(ordered[1]))
    extras = got[0]
    ready = ordered[1:]

    step = max(part // 4, 1)
    pending = [(c, start) for c in range(chunks) for start in range(0, part, step)]
    grads = ()

    def expert_grads(many, *ready):
        nonlocal grads
        mark = ready[0]
        for c, start in pending[:many]:
            *grads, mark = expert_grad(at, c * part, start, step, local, acts[c], other_acts[c], grads, ready)
        del pending[:many]
        return mark

    acts, sums, ys = [], [], []
    dg_full = jnp.zeros((4, lanes_of(size) // 128, 16, 128), f32)
    for c in range(chunks):
        *outs, dg_full, act = moe(at, size, chunks, c, got[c], extras, g_pieces[c], w_in, w_out, dg_full, () if c else ready)
        sums.append(scatter_direct(*outs[:4]) if c < chunks - 1 else outs[:4])
        ys.append(outs[4:])
        acts.append(act)
    other_acts = [to_core(acts[0])]


    def give(c, extra, deps):
        given = call(functools.partial(give_back_kernel, size, extra), "give_back", [sd((part_rows + 16 * extra, width), bf16)] * size,
                     (matrix, *sums[c]), deps=deps)
        return given[0], [given[0]] + [to_expert(given[k], size - k, size) for k in range(1, size)]

    outs = list(sums[-1])
    if chunks == 2:
        outs = [*outs[:1], *[after(piece, *sums[0][1:]) for piece in outs[1:4]]]
    sums[-1] = scatter_direct(*outs)
    back_blocks = []
    mark = outs[0]
    if chunks == 2:
        mark, back_blocks = give(0, False, (mark,))
    mark = expert_grads(2, mark)
    mark = expert_grads(1, mark, *back_blocks[1:])
    if chunks == 2:
        acts[1] = after(acts[1], mark, *sums[-1][1:])
        other_acts.append(to_core(acts[1]))
    ready, blocks = give(chunks - 1, True, (mark,))
    if chunks == 2:
        y_packs = [after(ys[c][1], *sums[-1][1:]) for c in (0, 1)]
        y_got = [to_tensor(pack, flip) for flip, pack in zip((1, 2), y_packs)]
    else:
        y_terms = scatter_direct(*ys[0])
    mark = expert_grads(1, ready)
    ready = (mark, *y_packs) if chunks == 2 else (mark,)
    dh, dhb, small = back(idx, cot, h, xn2, probs, gate, router, gains, back_blocks + blocks, size, chunks, ready)
    dh_pieces = gather_direct(dhb)
    mark = expert_grads(2, dhb)
    small = after(small, mark)
    small = small + to_tensor(small, 1)
    if chunks == 2:
        y_parts, sent = scatter_end(*y_got, ys[1][2], ys[0][2], (mark,))
        mark = sent[0]

    gtab, dqkv = attn_bwd(at, size, table, dh_pieces, segments, wo, qkv, lse, (mark, small))
    small = small + to_tensor(small, 2)
    outs = [sd((local * CAP, width), bf16)] * size
    if chunks == 2:
        given = call(functools.partial(give_back_halves_kernel, size), "give_back_y", outs, (matrix, ys[0][0], ys[1][0], *y_parts), deps=(dqkv, small))
    else:
        given = call(functools.partial(give_back_kernel, size, False), "give_back_y", outs, (matrix, *y_terms), deps=(dqkv,))
    y_blocks = [given[0]] + [to_expert(given[k], size - k, size) for k in range(1, size)]
    keep, send, gain_row, own, *parts = attn_grad(at, size, dqkv, qkv_w, xn, dh_pieces, o, (given[0], small))
    small = small + to_core(small)
    terms = scatter_direct(own, *[after(p, *y_blocks[1:]) for p in parts])
    got = to_core(send)
    grad_tokens = call(last_kernel, "last", [sd((count, width), f32)], (tok, dh, *terms, gains))[0]
    output = mix(idx, h, gate, y_blocks, size, chunks)

    gain_row = gain_row + to_tensor(gain_row, 1)
    gain_row = gain_row + to_tensor(gain_row, 2)
    out_blocks = call(functools.partial(merge_kernel, size), "merge", [sd((half, packed.shape[1]), bf16)] * size,
                      (at, keep, got, small, gain_row, gtab), smem=1,
                      scratch=[pltpu.VMEM((2 * size, half, 128), f32), pltpu.VMEM((2 * size, half, 8), f32)])
    expert_grads(len(pending), out_blocks[0])
    total = call(total_kernel, "total", [sd(out_blocks[0].shape, f32)], tuple(shifted(out_blocks)), deps=(grads[0], *terms[1:]))[0]
    lw = w_query.shape[1]
    outs = [sd((rows_dev, lw), f32)] * 4 + [sd((experts, rows_dev), f32), sd(rel_table.T.shape, f32)] + [sd((1, rows_dev), f32)] * 2
    grad_q, grad_k, grad_v, grad_o, grad_router, grad_table, grad_ga, grad_gm = call(
        finish_kernel, "finish", outs, (at, total, to_core(total), gain_attn[None]), smem=1, scratch=[pltpu.VMEM((rows_dev, 128), f32)])
    return (output[None], grad_tokens[None], grad_table.T, grad_q, grad_k, grad_v, grad_o, grad_ga[0], grad_gm[0], grad_router.T, *grads)


def solution(mesh):
    by_token = P(("expert", "rep"), "tensor", None)
    both = P("expert", "tensor")
    return jax.shard_map(
        functools.partial(on_device, mesh.shape["expert"]),
        mesh=mesh,
        in_specs=(by_token, P(("expert", "rep"), None), by_token, P(), by_token, both, both, both, both, both, P("expert"), P("expert"),
                  P("expert", None), P("expert", None, "tensor"), P("expert", "tensor", None)),
        out_specs=(by_token, by_token, both, both, both, both, both, P("expert"), P("expert"), P("expert", None),
                   P("expert", None, "tensor"), P("expert", "tensor", None)),
        check_vma=False,
    )
```

```python
import functools
import math

import jax
import jax.numpy as jnp
from jax import lax
from jax.experimental import pallas as pl
from jax.experimental.pallas import tpu as pltpu
from jax.sharding import PartitionSpec as P

HEAD = 64
CAP = 12
QB = 128
TABLE = 66
epsilon = 1e-06
masked_value = -1e30
thresholds = (16, 19, 21, 24, 27, 31, 35, 40, 46, 52, 59, 67, 77, 87, 99, 113)
lowest = tuple(range(16)) + thresholds
f32 = jnp.float32
bf16 = jnp.bfloat16
i32 = jnp.int32
NN = (((1,), (0,)), ((), ()))
NT = (((1,), (1,)), ((), ()))
TN = (((0,), (0,)), ((), ()))
VM = pl.BlockSpec(memory_space=pltpu.VMEM)
SM = pl.BlockSpec(memory_space=pltpu.SMEM)
sd = jax.ShapeDtypeStruct


def dot(a, b, dims=NN):
    return lax.dot_general(a, b, dims, preferred_element_type=f32)


ANY = pl.BlockSpec(memory_space=pl.ANY)
TIMES = {"attn_fwd": 13, "attn_bwd": 400, "attn_grad": 9, "project": 5, "moe": 300, "expert_grad": 1, "back": 5, "route": 4}


def cost(name):
    return pl.CostEstimate(flops=int(TIMES.get(name, 0.5) * 1_150_000_000), bytes_accessed=1000, transcendentals=0)


def call(kernel, name, outs, operands, scratch=(), smem=0, flops=0, moved=4_000_000, deps=()):
    given = len(operands)

    def body(*refs):
        kernel(*refs[:given], *refs[given + len(deps):])

    return pl.pallas_call(
        body,
        out_shape=tuple(outs),
        in_specs=[SM] * smem + [VM] * (given - smem) + [ANY] * len(deps),
        out_specs=tuple(VM for _ in outs),
        scratch_shapes=list(scratch),
        compiler_params=pltpu.CompilerParams(vmem_limit_bytes=56 << 20),
        cost_estimate=cost(name),
        name=name,
    )(*operands, *deps)


def after(value, *deps):
    return pl.pallas_call(
        lambda *refs: None,
        out_shape=sd(value.shape, value.dtype),
        in_specs=[ANY] * (1 + len(deps)),
        out_specs=ANY,
        input_output_aliases={0: 0},
        name="after",
    )(value, *deps)


def to_tensor(a, flip):
    return lax.ppermute(a, "tensor", [(i, i ^ flip) for i in range(4)])


def to_expert(a, shift, size):
    return lax.ppermute(a, "expert", [(i, (i + shift) % size) for i in range(size)])


def to_core(a):
    return lax.ppermute(a, "rep", [(0, 1), (1, 0)])


def shifted(blocks):
    size = len(blocks)
    return [blocks[0]] + [to_expert(blocks[k], k, size) for k in range(1, size)]


def gather_pieces(own, half):
    px = to_tensor(own, 1)
    py = to_tensor(own, 2)
    d0 = to_tensor(px[:half], 2)
    d1 = to_tensor(py[half:], 1)
    return own, px, py, d0, d1


def gather_direct(own):
    return (own, *[to_tensor(own, flip) for flip in (1, 2, 3)])


def late_kernel(x_late, y_late, got_x, got_y, sum_x, sum_y):
    sum_x[...] = (x_late[...].astype(f32) + got_y[0].astype(f32)).astype(bf16)
    sum_y[...] = (y_late[...].astype(f32) + got_x[0].astype(f32)).astype(bf16)


def scatter_end(got_x, got_y, x_late, y_late, deps):
    shape = sd(x_late.shape, bf16)
    sent = call(late_kernel, "late", [shape, shape], (x_late, y_late, got_x, got_y), deps=deps)
    return (got_x, to_tensor(sent[1], 2), got_y, to_tensor(sent[0], 1)), sent


def scatter_direct(own, *pieces):
    return (own, *[to_tensor(piece, flip) for flip, piece in zip((1, 2, 3), pieces)])


def add_terms(refs):
    return sum(r[...].astype(f32) for r in refs)


def onehot(index, width):
    return lax.broadcasted_iota(i32, (index.shape[0], width), 1) == index


def as_bf16(mask):
    return jnp.where(mask, 1.0, 0.0).astype(bf16)


def prepare_kernel(size, chunks, me_ref, routes_ref, capacity_ref, idx_ref):
    count = routes_ref.shape[1]
    experts = capacity_ref.shape[1]
    local = experts // size
    part = local // chunks
    me = me_ref[0]
    first, second = (jnp.broadcast_to(routes_ref[j:j + 1, :], (8, count)).T[:, 0:1] for j in (0, 1))
    both = as_bf16(onehot(first, experts)) + as_bf16(onehot(second, experts))
    rows = lax.broadcasted_iota(i32, (count, count), 0)
    cols = lax.broadcasted_iota(i32, (count, count), 1)
    before = dot(as_bf16(cols < rows), both)
    capacity = capacity_ref[...].astype(f32)
    shift = int(math.log2(local))
    columns = []
    for route in (first, second):
        mine = onehot(route, experts)
        position = jnp.sum(jnp.where(mine, before, 0.0), axis=1, keepdims=True)
        limit = jnp.sum(jnp.where(mine, jnp.broadcast_to(capacity, mine.shape), 0.0), axis=1, keepdims=True)
        keep = position < limit
        position = position.astype(i32)
        owner = lax.shift_right_logical(route, jnp.full_like(route, shift))
        inner = route & (local - 1)
        away = (owner - me + size) & (size - 1)
        chunk = lax.shift_right_logical(inner, jnp.full_like(route, int(math.log2(part))))
        slot = ((chunk * size + away) * part + (inner & (part - 1))) * CAP + position
        columns += [route, jnp.where(keep, slot, -1), jnp.where(keep, away * local + inner, -1), away * CAP + position]
    for n, column in enumerate(columns):
        idx_ref[:, n:n + 1] = column


def spread_kernel(first, chunks, idx_ref, rows_ref, *outs):
    count = len(outs)
    block = outs[0].shape[0] // chunks
    width = block * chunks * count
    spread = as_bf16(onehot(idx_ref[:, 1:2] - first, width)) + as_bf16(onehot(idx_ref[:, 5:6] - first, width))
    slots = dot(spread, rows_ref[...], TN).astype(bf16)
    for c in range(chunks):
        for k, ref in enumerate(outs):
            ref[c * block:(c + 1) * block, :] = slots[(c * count + k) * block:(c * count + k + 1) * block]


def spread(idx, rows, chunk, count, block, deps, name, chunks):
    return call(functools.partial(spread_kernel, chunk * count * block, chunks), name, [sd((block, rows.shape[1]), bf16)] * count, (idx, rows), deps=deps)


def order_matrix(size, part, block, extra, out_extra):
    rows = part * size * CAP
    m = [[0.0] * (size * block) for _ in range(rows + out_extra)]
    for e in range(part):
        for k in range(size):
            for c in range(CAP):
                m[(e * size + k) * CAP + c][k * block + e * CAP + c] = 1.0
    for r in range(extra):
        for k in range(size):
            m[rows + r][k * block + part * CAP + r] = 1.0
    return jnp.array(m, dtype=bf16)


def reorder_kernel(count, m_ref, *refs):
    blocks, out_ref = refs[:count], refs[count]
    out_ref[...] = dot(m_ref[...], jnp.concatenate([b[...] for b in blocks], axis=0)).astype(bf16)


def reorder_all_kernel(count, m_ref, *refs):
    blocks, out_ref = refs[:count], refs[count]
    block = m_ref.shape[1] // count
    rows = m_ref.shape[0]
    for c in range(out_ref.shape[0] // rows):
        chosen = jnp.concatenate([b[c * block:(c + 1) * block, :] for b in blocks], axis=0)
        out_ref[c * rows:(c + 1) * rows, :] = dot(m_ref[...], chosen).astype(bf16)


def reorder(matrix, blocks, name, deps=()):
    rows = matrix.shape[0]
    width = blocks[0].shape[1]
    return call(functools.partial(reorder_kernel, len(blocks)), name, [sd((rows, width), bf16)], (matrix, *blocks),
                flops=2 * matrix.size * width, moved=2 * rows * width * 2, deps=deps)[0]


def give_back_kernel(count, extra, m_ref, *refs):
    outs = refs[4:]
    total = add_terms(refs[:4]).astype(bf16)
    rows = m_ref.shape[0]
    back = dot(m_ref[...], total[0:rows], TN).astype(bf16)
    block = back.shape[0] // count
    for k in range(count):
        outs[k][0:block, :] = back[k * block:(k + 1) * block]
        if extra:
            outs[k][block:, :] = total[rows:]


def give_back_halves_kernel(count, m_ref, own_a, own_b, got_x, late_y, got_y, late_x, *outs):
    halves = (own_a[...].astype(f32) + got_x[1].astype(f32) + late_y[...].astype(f32), own_b[...].astype(f32) + got_y[1].astype(f32) + late_x[...].astype(f32))
    for n, total in enumerate(halves):
        back = dot(m_ref[...], total.astype(bf16), TN).astype(bf16)
        block = back.shape[0] // count
        for k in range(count):
            outs[k][n * block:(n + 1) * block, :] = back[k * block:(k + 1) * block]


def pack_kernel(at_ref, q_ref, k_ref, v_ref, r_ref, o_ref, ga_ref, gm_ref, t_ref, out_ref, rest_ref, full):
    rows, width = q_ref.shape
    full[...] = jnp.zeros_like(full)
    place = 0
    for ref in (q_ref, k_ref, v_ref, r_ref, o_ref):
        value = ref[...].astype(f32)
        value = value.T if ref is r_ref else value
        full[:, place:place + value.shape[1]] = value
        place += value.shape[1]
    for ref in (ga_ref, gm_ref):
        full[:, place:place + 1] = column_of(ref[...].astype(f32)[None, :])
        place += 1
    full[0:t_ref.shape[1], place:place + t_ref.shape[0]] = t_ref[...].astype(f32).T
    half = rows // 2
    for r in (0, 1):
        @pl.when(at_ref[1] == r)
        def _():
            out_ref[...] = full[r * half:(r + 1) * half, :].astype(bf16)
            rest_ref[...] = full[(1 - r) * half:(2 - r) * half, :].astype(bf16)


def unpack_kernel(size, at_ref, *refs):
    mine, other = refs[:size], refs[size:2 * size]
    full, qkv_ref, wo_ref, router_ref, gains_ref, table_ref = refs[2 * size:]
    me, rep = at_ref[0], at_ref[1]
    half = mine[0].shape[0]
    for k in range(size):
        z = (me - k + size) & (size - 1)
        full[2 * z + rep] = mine[k][...].astype(f32)
        full[2 * z + 1 - rep] = other[k][...].astype(f32)
    full = jnp.concatenate([full[n] for n in range(2 * size)], axis=0)
    qkv_ref[...] = full[:, 0:576].astype(bf16)
    router_ref[...] = full[:, 576:640].astype(bf16)
    wo_ref[...] = full[:, 640:832].astype(bf16)
    tail = full[:, 768:896]
    turned = tail.T
    gains_ref[...] = turned[64:72, :]
    rows = table_ref.shape[0] // size
    for z in range(size):
        table_ref[z * rows:(z + 1) * rows, :] = tail[z * 2 * half: z * 2 * half + rows, :]


def unpack(at, mine, other, buckets, deps):
    size = len(mine)
    half, cols = mine[0].shape
    width = 2 * half * size

    def kernel(at_ref, *refs):
        unpack_kernel(size, at_ref, *refs[:2 * size], refs[-1], *refs[2 * size:-1])

    outs = [sd((width, 576), bf16), sd((width, 192), bf16), sd((width, 64), bf16), sd((8, width), f32), sd((buckets, 128), f32)]
    return call(kernel, "unpack", outs, (at, *mine, *other), scratch=[pltpu.VMEM((2 * size, half, cols), f32)], smem=1, deps=deps)


def piece_shapes(rows, width):
    return [sd((rows, width), bf16)] * 4


def near_offset():
    rows = lax.broadcasted_iota(jnp.int32, (QB, 2 * QB), 0)
    cols = lax.broadcasted_iota(jnp.int32, (QB, 2 * QB), 1)
    return QB + rows - cols


def near_bias(table_ref, head, buckets):
    off = near_offset()
    bias = jnp.where(off < 0, masked_value, table_ref[0, TABLE + head])
    for b in range(1, buckets):
        bias = jnp.where(off >= lowest[b], table_ref[b, TABLE + head], bias)
    return bias


def scores_of(q, k_ref, head, i, near, far, seg_col, seg_row_ref):
    lo = max(i - 1, 0) * QB
    hi = (i + 1) * QB
    s = dot(q, k_ref[head, 0:hi], NT)
    bias = near[:, QB:] if i == 0 else near
    same_near = seg_col == seg_row_ref[:, lo:hi]
    s_near = jnp.where(same_near, s[:, lo:hi] + bias, masked_value)
    if lo == 0:
        return s_near
    same_far = seg_col == seg_row_ref[:, 0:lo]
    s_far = jnp.where(same_far, s[:, 0:lo] + far, masked_value)
    return jnp.concatenate([s_far, s_near], axis=1)


def project_kernel(at_ref, own_ref, px_ref, py_ref, pd0_ref, pd1_ref, w_ref, gain_ref, xn_ref, qkv_ref):
    pos = at_ref[2]
    tok = own_ref.shape[0]
    half = tok // 2
    gain = gain_ref[0:1, :]

    def put(rows, flip, start=0):
        x = rows.astype(f32)
        r = lax.rsqrt(jnp.mean(x * x, axis=-1, keepdims=True) + epsilon)
        xn = (x * r * gain).astype(bf16)
        at = pl.ds(pl.multiple_of((pos ^ flip) * tok + start, half), rows.shape[0])
        xn_ref[at, :] = xn
        qkv_ref[at, :] = dot(xn, w_ref[...]).astype(bf16)

    put(own_ref[...], 0)
    put(px_ref[...], 1)
    put(py_ref[...], 2)
    put(pd0_ref[...], 3)
    put(pd1_ref[...], 3, half)


def column_of(row):
    return jnp.broadcast_to(row, (8, row.shape[1])).T[:, 0:1]


def attn_fwd_kernel(heads, at_ref, table_ref, qkv_ref, segr_ref, wo_ref, o_ref, lse_ref, out_own, out_x, out_y, out_d, qs, ks, vs, seg):
    pos = at_ref[2]
    tok = out_own.shape[0]
    half = tok // 2
    buckets = table_ref.shape[0]
    seg[...] = column_of(segr_ref[...])

    def at(flip, start=0, size=tok):
        return pl.ds(pl.multiple_of((pos ^ flip) * tok + start, half), size)

    width = heads * HEAD
    qkv = qkv_ref[...]
    for h in range(heads):
        qs[h] = qkv[:, h * HEAD:(h + 1) * HEAD] * bf16(0.125)
        ks[h] = qkv[:, width + h * HEAD: width + (h + 1) * HEAD]
        vs[h] = qkv[:, 2 * width + h * HEAD: 2 * width + (h + 1) * HEAD]
    blocks = qkv_ref.shape[0] // QB
    for h in range(heads):
        near = near_bias(table_ref, h, buckets)
        far = table_ref[buckets - 1, TABLE + h]
        for i in range(blocks):
            rows = slice(i * QB, (i + 1) * QB)
            s = scores_of(qs[h, rows], ks, h, i, near, far, seg[rows, :], segr_ref)
            top = jnp.max(s, axis=-1, keepdims=True)
            e = jnp.exp(s - top)
            total = jnp.sum(e, axis=-1, keepdims=True)
            p = (e * (1.0 / total)).astype(bf16)
            o_ref[rows, h * HEAD:(h + 1) * HEAD] = dot(p, vs[h, 0:(i + 1) * QB]).astype(bf16)
            lse_ref[rows, h:h + 1] = top + jnp.log(total)
    wo = wo_ref[...]
    for flip, ref in enumerate((out_own, out_x, out_y, out_d)):
        ref[...] = dot(o_ref[at(flip), :], wo, NT).astype(bf16)


def attn_bwd_kernel(heads, size, at_ref, table_ref, own_ref, px_ref, py_ref, pd_ref, segr_ref, wo_ref, qkv_ref, lse_ref,
                    gtab_ref, dqkv, dh, qs, ks, vs, do, dk, dv, acc, seg):
    pos = at_ref[2]
    tok = own_ref.shape[0]
    half = tok // 2
    buckets = table_ref.shape[0]
    width = heads * HEAD

    def at(flip, start=0, size=tok):
        return pl.ds(pl.multiple_of((pos ^ flip) * tok + start, half), size)

    seg[...] = column_of(segr_ref[...])
    dh[at(0), :] = own_ref[...]
    dh[at(1), :] = px_ref[...]
    dh[at(2), :] = py_ref[...]
    dh[at(3), :] = pd_ref[...]
    dall = dot(dh[...], wo_ref[...]).astype(bf16)
    for h in range(heads):
        do[h] = dall[:, h * HEAD:(h + 1) * HEAD]
        qs[h] = qkv_ref[:, h * HEAD:(h + 1) * HEAD] * bf16(0.125)
        ks[h] = qkv_ref[:, width + h * HEAD: width + (h + 1) * HEAD]
        vs[h] = qkv_ref[:, 2 * width + h * HEAD: 2 * width + (h + 1) * HEAD]
    blocks = qkv_ref.shape[0] // QB
    off = near_offset()
    per = gtab_ref.shape[1]
    gtab_ref[...] = jnp.zeros_like(gtab_ref)
    for h in range(heads):
        near = near_bias(table_ref, h, buckets)
        far = table_ref[buckets - 1, TABLE + h]
        acc[...] = jnp.zeros_like(acc)
        dk[...] = jnp.zeros_like(dk)
        dv[...] = jnp.zeros_like(dv)
        far_sum = jnp.zeros((QB, 1), f32)
        for i in range(blocks):
            rows = slice(i * QB, (i + 1) * QB)
            lo = max(i - 1, 0) * QB
            hi = (i + 1) * QB
            q = qs[h, rows]
            s = scores_of(q, ks, h, i, near, far, seg[rows, :], segr_ref)
            p = jnp.exp(s - lse_ref[rows, h:h + 1])
            g = do[h, rows]
            dv[0:hi] += dot(p.astype(bf16), g, TN)
            dp = dot(g, vs[h, 0:hi], NT)
            pd = p * dp
            ds = (pd - p * jnp.sum(pd, axis=-1, keepdims=True)).astype(bf16)
            dq = dot(ds, ks[h, 0:hi]) * 0.125
            dqkv[rows, h * HEAD:(h + 1) * HEAD] = dq.astype(bf16)
            dk[0:hi] += dot(ds, q, TN)
            dsf = ds.astype(f32)
            if i == 0:
                acc[:, QB:] += dsf
            else:
                acc[...] += dsf[:, lo:hi]
            if lo > 0:
                far_sum = far_sum + jnp.sum(dsf[:, 0:lo], axis=-1, keepdims=True)
        dqkv[:, width + h * HEAD: width + (h + 1) * HEAD] = dk[...].astype(bf16)
        dqkv[:, 2 * width + h * HEAD: 2 * width + (h + 1) * HEAD] = dv[...].astype(bf16)
        total = acc[...]
        rest = jnp.sum(far_sum, axis=0, keepdims=True)
        for b in range(buckets):
            if b == buckets - 1:
                inside = off >= lowest[b]
            else:
                inside = (off >= lowest[b]) & (off < lowest[b + 1])
            part = jnp.sum(jnp.where(inside, total, 0.0), axis=0, keepdims=True)
            one = jnp.sum(part, axis=1, keepdims=True)
            gtab_ref[b // per, b % per:b % per + 1, TABLE + 1 + h:TABLE + 2 + h] = one + rest if b == buckets - 1 else one


def attn_grad_kernel(size, at_ref, dqkv, w_ref, xn_ref, own_ref, px_ref, py_ref, pd_ref, o_ref, small_ref, gtab_ref, keep_ref, send_ref,
                     out_own, out_x, out_y, out_d, dh, full):
    pos, rep = at_ref[2], at_ref[1]
    tok = out_own.shape[0]
    half = tok // 2
    width = o_ref.shape[1]

    def at(flip, start=0, size=tok):
        return pl.ds(pl.multiple_of((pos ^ flip) * tok + start, half), size)

    dh[at(0), :] = own_ref[...]
    dh[at(1), :] = px_ref[...]
    dh[at(2), :] = py_ref[...]
    dh[at(3), :] = pd_ref[...]
    w = w_ref[...]
    for flip, ref in enumerate((out_own, out_x, out_y, out_d)):
        ref[...] = dot(dqkv[at(flip), :], w, NT).astype(bf16)
    grad = dot(xn_ref[...], dqkv[...], TN)
    grad_out = dot(dh[...], o_ref[...], TN)
    part_rows = keep_ref.shape[1]
    for n in range(2 * size):
        full[n, :, 0:3 * width] = grad[n * part_rows:(n + 1) * part_rows].astype(bf16)
        full[n, :, 3 * width:4 * width] = grad_out[n * part_rows:(n + 1) * part_rows].astype(bf16)
        few = small_ref[n * part_rows:(n + 1) * part_rows, :]
        full[n, :, 4 * width:] = few
        if n % 2 == 0:
            rows = gtab_ref.shape[1]
            full[n, 0:rows, 4 * width:] = (few[0:rows].astype(f32) + gtab_ref[n // 2]).astype(bf16)
    for z in range(size):
        keep_ref[z] = full[2 * z + rep]
        send_ref[z] = full[2 * z + 1 - rep]


def project(at, pieces, w, gains, deps):
    tok, width = pieces[0].shape
    return call(project_kernel, "project", [sd((4 * tok, width), bf16), sd((4 * tok, w.shape[1]), bf16)], (at, *pieces, w, gains),
                smem=1, deps=deps)


def attn_fwd(at, table, qkv, segr, wo, deps):
    width = wo.shape[0]
    length = qkv.shape[0]
    heads = wo.shape[1] // HEAD
    outs = [sd((length, heads * HEAD), bf16), sd((length, heads), f32)]
    return call(functools.partial(attn_fwd_kernel, heads), "attn_fwd", outs + piece_shapes(length // 4, width),
                (at, table, qkv, segr, wo),
                scratch=[pltpu.VMEM((heads, length, HEAD), bf16)] * 3 + [pltpu.VMEM((length, 1), i32)], smem=2,
                flops=8_000_000_000, moved=5_000_000, deps=deps)


def attn_bwd(at, size, table, pieces, segr, wo, qkv, lse, deps):
    tok, width = pieces[0].shape
    length = qkv.shape[0]
    heads = wo.shape[1] // HEAD
    outs = [sd((size, table.shape[0] // size, 128), f32), sd(qkv.shape, bf16)]
    scratch = [pltpu.VMEM((length, width), bf16)] + [pltpu.VMEM((heads, length, HEAD), bf16)] * 4 + [pltpu.VMEM((length, HEAD), f32)] * 2
    scratch += [pltpu.VMEM((QB, 2 * QB), f32), pltpu.VMEM((length, 1), i32)]
    return call(functools.partial(attn_bwd_kernel, heads, size), "attn_bwd", outs, (at, table, *pieces, segr, wo, qkv, lse),
                scratch=scratch, smem=2, flops=12_000_000_000, moved=8_000_000, deps=deps)


def attn_grad(at, size, dqkv, w, xn, pieces, o, small, gtab, deps):
    tok, width = pieces[0].shape
    cols = w.shape[1] + o.shape[1] + small.shape[1]
    rows = width // (2 * size)
    outs = [sd((size, rows, cols), bf16)] * 2 + piece_shapes(tok, width)
    return call(functools.partial(attn_grad_kernel, size), "attn_grad", outs, (at, dqkv, w, xn, *pieces, o, small, gtab),
                scratch=[pltpu.VMEM((4 * tok, width), bf16), pltpu.VMEM((2 * size, rows, cols), bf16)], smem=1,
                flops=4_000_000_000, moved=9_000_000, deps=deps)


def route_kernel(size, chunks, idx_ref, tokens_ref, own, rx, ry, rd, router_ref, gains_ref, h_ref, xn_ref, probs_ref, gate_ref, *blocks):
    count, width = tokens_ref.shape
    experts = router_ref.shape[1]
    local = experts // size
    rows_of = local // chunks * CAP
    lanes = lanes_of(size)
    h = tokens_ref[...].astype(f32) + add_terms((own, rx, ry, rd))
    r = lax.rsqrt(jnp.mean(h * h, axis=-1, keepdims=True) + epsilon)
    xn = (h * r * gains_ref[1:2, :]).astype(bf16)
    h_ref[...] = h
    xn_ref[...] = xn
    logits = dot(xn, router_ref[...])
    e = jnp.exp(logits - jnp.max(logits, axis=-1, keepdims=True))
    probs = e / jnp.sum(e, axis=-1, keepdims=True)
    probs_ref[...] = probs
    picked = [jnp.sum(jnp.where(onehot(idx_ref[:, 4 * j:4 * j + 1], experts), probs, 0.0), axis=-1, keepdims=True) for j in (0, 1)]
    total = picked[0] + picked[1]
    gates = [p / total for p in picked]
    gate_ref[:, 0:1], gate_ref[:, 1:2], gate_ref[:, 2:3] = gates[0], gates[1], total
    spread = as_bf16(onehot(idx_ref[:, 1:2], size * rows_of)) + as_bf16(onehot(idx_ref[:, 5:6], size * rows_of))
    slots = dot(spread, xn, TN).astype(bf16)
    held = jnp.zeros((experts, lanes), f32)
    for j in (0, 1):
        to = as_bf16(onehot(idx_ref[:, 4 * j + 2:4 * j + 3], experts))
        at = jnp.where(onehot(idx_ref[:, 4 * j + 3:4 * j + 4], lanes), gates[j], 0.0).astype(bf16)
        held = held + dot(to, at, TN)
    for k, ref in enumerate(blocks):
        ref[0:rows_of, :] = slots[k * rows_of:(k + 1) * rows_of]
        ref[rows_of:, :] = jnp.zeros((16, width), bf16)
        ref[rows_of:rows_of + local, 0:lanes] = held[k * local:(k + 1) * local].astype(bf16)


def lanes_of(size):
    return -(-size * CAP // 128) * 128


def route(idx, tokens, parts, router, gains, size, chunks, deps):
    count, width = tokens.shape
    experts = router.shape[1]
    rows_of = experts // size // chunks * CAP
    outs = [sd((count, width), f32), sd((count, width), bf16), sd((count, experts), f32), sd((count, 8), f32)]
    outs += [sd((rows_of + 16, width), bf16)] * size
    return call(functools.partial(route_kernel, size, chunks), "route", outs, (idx, tokens, *parts, router, gains),
                flops=400_000_000, moved=5_000_000, deps=deps)


def moe_kernel(rows, part, offset, last, skip, at_ref, own, px, py, d0, d1, e_own, e_px, e_py, e_d, g_own, g_px, g_py, g_far, win_ref, wout_ref,
               dg_in, *refs):
    outs, y_outs, dg_ref, acts = refs[skip:skip + 4], refs[skip + 4:-2], refs[-2], refs[-1]
    e, j = pl.program_id(0), pl.program_id(1)
    steps = pl.num_programs(1)

    @pl.when((e == 0) & (j == 0))
    def _():
        dg_ref[...] = dg_in[...]

    wide = e_own.shape[1]
    pick = lax.broadcasted_iota(i32, (16, wide), 0) == e + offset
    square = lax.broadcasted_iota(i32, (rows, wide), 0) + j * rows == lax.broadcasted_iota(i32, (rows, wide), 1)

    def gate_of(ref):
        row = jnp.sum(jnp.where(pick, ref[...].astype(f32), 0.0), axis=0, keepdims=True)
        return jnp.sum(jnp.where(square, jnp.broadcast_to(row, square.shape), 0.0), axis=1, keepdims=True)

    def keep(n, value):
        for flip in range(4):
            acts[n, 0, flip] = value[flip * rows:(flip + 1) * rows]

    def put(value, outs):
        at = pl.ds(pl.multiple_of((e * steps + j) * rows, 16), rows)
        for flip, ref in enumerate(outs):
            ref[at, :] = value[flip * rows:(flip + 1) * rows]

    gate = jnp.concatenate([gate_of(r) for r in (e_own, e_px, e_py, e_d)], axis=0)
    far = jnp.where(e < part // 2, d0[...].astype(f32), d1[...].astype(f32)).astype(bf16)
    s = jnp.concatenate([own[...], px[...], py[...], far], axis=0)
    g = jnp.concatenate([g_own[...], g_px[...], g_py[...], g_far[...]], axis=0).astype(f32)
    keep(0, s)
    win, wout = win_ref[0], wout_ref[0]
    dy = (g * gate).astype(bf16)
    keep(1, dy)
    a = dot(s, win)
    dhid = dot(dy, wout, NT)
    c = math.sqrt(2.0 / math.pi)
    t = jnp.tanh(a * (c + (c * 0.044715) * (a * a)))
    up = 0.5 + 0.5 * t
    hid = (a * up).astype(bf16)
    slope = up + (0.5 * a) * (1.0 - t * t) * (c + (3 * c * 0.044715) * (a * a))
    da = (dhid * slope).astype(bf16)
    keep(2, hid)
    keep(3, da)
    put(dot(da, win, NT).astype(bf16), outs)
    y = dot(hid, wout)
    ones = jnp.ones((8, y.shape[1]), bf16)
    sums = dot(ones, (y * g).astype(bf16), NT)
    if len(y_outs) == 4:
        put(y.astype(bf16), y_outs)
    else:
        near = 1 if offset == 0 else 2
        own_ref, pack, once = y_outs
        put(y.astype(bf16), [own_ref] + ([pack.at[1], once] if near == 1 else [once, pack.at[1]]) + [pack.at[0]])
    for flip in range(4):
        row = sums[0:1, flip * rows:(flip + 1) * rows]
        dg_ref[flip, j, pl.ds(e + offset, 1), 0:rows] = row

    if last:
        @pl.when((e == part - 1) & (j == steps - 1))
        def _():
            for flip, ref in enumerate(outs):
                ref[-16:, :] = jnp.zeros((16, ref.shape[1]), bf16)
                for n in range(wide // 128):
                    ref[-16:, n * 128:(n + 1) * 128] = dg_ref[flip, n].astype(bf16)


def moe(at, size, chunks, chunk, pieces, extras, g, w_in, w_out, dg, deps):
    all_rows = size * CAP
    rows = 128 if all_rows % 128 == 0 else all_rows
    steps = all_rows // rows
    local, width, hidden = w_in.shape
    part = local // chunks
    lanes = -(-all_rows // 128) * 128
    first = chunk * part
    whole = lambda e, j: (e * steps + j, 0)
    flat = pl.BlockSpec((rows, width), whole)
    of_all = pl.BlockSpec((rows, width), lambda e, j: ((first + e) * steps + j, 0))
    half = part // 2
    low = pl.BlockSpec((rows, width), lambda e, j: (jnp.where(e < half, e * steps + j, half * steps - 1), 0))
    high = pl.BlockSpec((rows, width), lambda e, j: (jnp.where(e < half, 0, (e - half) * steps + j), 0))
    ext = lambda start: pl.BlockSpec((16, lanes), lambda e, j: (start // 16, 0))
    two_steps = len(pieces) == 5
    in_specs = [SM] + [flat] * 3 + ([low, high] if two_steps else [flat, flat])
    in_specs += [ext(part * all_rows)] * 3 + [ext(half * all_rows)] + [of_all] * 3 + [flat]
    in_specs += [pl.BlockSpec((1, width, hidden), lambda e, j: (first + e, 0, 0)), pl.BlockSpec((1, hidden, width), lambda e, j: (first + e, 0, 0))]
    operands = [at, *pieces, *([] if two_steps else pieces[3:]), *extras, *g[:3], g[3 + chunk], w_in, w_out]
    last = chunk == chunks - 1
    shape = (part * all_rows + 16 * last, width)
    total = part * all_rows
    y_shapes = [(total, width), (2, total, width), (total, width)] if chunks == 2 else [(total, width)] * 4
    outs = [sd(shape, bf16)] * 4 + [sd(y, bf16) for y in y_shapes] + [sd(dg.shape, f32), sd((4, part, 4, all_rows, width), bf16)]
    every = lambda dims: pl.BlockSpec(dims, lambda e, j: (0,) * len(dims))
    out_specs = [every(shape)] * 4 + [every(y) for y in y_shapes]
    out_specs += [every(dg.shape), pl.BlockSpec((4, 1, 4, rows, width), lambda e, j: (0, e, 0, j, 0))]
    operands.append(dg)
    in_specs.append(every(dg.shape))
    operands += list(deps)
    in_specs += [ANY] * len(deps)
    return pl.pallas_call(
        functools.partial(moe_kernel, rows, part, first, last, len(deps)),
        grid=(part, steps),
        out_shape=tuple(outs), in_specs=in_specs, out_specs=tuple(out_specs),
        compiler_params=pltpu.CompilerParams(vmem_limit_bytes=58 << 20),
        cost_estimate=cost("moe"),
        name="moe",
    )(*operands)


def expert_grad_kernel(steps, at_ref, mine, other, *refs):
    gin, gout, mark = refs[-3:]
    mark[...] = jnp.zeros_like(mark)

    def put(a, b):
        both = [jnp.concatenate([r[n, 0, flip] for r in (a, b) for flip in range(4)], axis=0) for n in range(4)]
        for ref, left, right in ((gin, both[0], both[3]), (gout, both[2], both[1])):
            if steps == 1:
                ref[0] = dot(left, right, TN)
            else:
                part = dot(left, right, TN)
                ref[0] = jnp.where(pl.program_id(1) == 0, part, ref[0] + part)

    pl.when(at_ref[1] == 0)(lambda: put(mine, other))
    pl.when(at_ref[1] == 1)(lambda: put(other, mine))


def expert_grad(at, first, start, part, local, mine, other, before, deps):
    four, all_rows, width = mine.shape[2:]
    rows = 128 if all_rows % 128 == 0 else all_rows
    steps = all_rows // rows
    spec = pl.BlockSpec((4, 1, 4, rows, width), lambda e, j: (0, start + e, 0, j, 0))
    in_specs = [SM, spec, spec]
    operands = [at, mine, other]
    alias = {}
    if before:
        alias = {3: 0, 4: 1}
        operands += list(before)
        in_specs += [ANY] * 2
    operands += list(deps)
    in_specs += [ANY] * len(deps)
    out = pl.BlockSpec((1, width, width), lambda e, j: (first + start + e, 0, 0))
    return pl.pallas_call(
        functools.partial(expert_grad_kernel, steps),
        grid=(part, steps),
        out_shape=(sd((local, width, width), f32),) * 2 + (sd((8, 128), f32),), in_specs=in_specs,
        out_specs=(out, out, pl.BlockSpec((8, 128), lambda e, j: (0, 0))),
        input_output_aliases=alias,
        compiler_params=pltpu.CompilerParams(vmem_limit_bytes=56 << 20),
        cost_estimate=cost("expert_grad"),
        name="expert_grad",
    )(*operands)


def back_kernel(size, chunks, idx_ref, cot_ref, h_ref, xn_ref, probs_ref, gate_ref, router_ref, gains_ref, *refs):
    blocks = refs[:chunks * size]
    dh_ref, dhb_ref, small_ref, ds = refs[chunks * size:]
    experts = router_ref.shape[1]
    local = experts // size
    rows_of = local // chunks * CAP
    lanes = lanes_of(size)
    for n, block in enumerate(blocks):
        ds[n * rows_of:(n + 1) * rows_of, :] = block[0:rows_of, :]
    last = blocks[(chunks - 1) * size:]
    held = jnp.concatenate([last[k][rows_of:rows_of + local, 0:lanes].astype(f32) for k in range(size)], axis=0).astype(bf16)
    spread = as_bf16(onehot(idx_ref[:, 1:2], experts * CAP)) + as_bf16(onehot(idx_ref[:, 5:6], experts * CAP))
    dxn = dot(spread, ds[...])
    probs = probs_ref[...]
    gates, dgates, chosen = [], [], []
    for j in (0, 1):
        got = dot(as_bf16(onehot(idx_ref[:, 4 * j + 2:4 * j + 3], experts)), held)
        dgates.append(jnp.sum(jnp.where(onehot(idx_ref[:, 4 * j + 3:4 * j + 4], lanes), got, 0.0), axis=-1, keepdims=True))
        gates.append(gate_ref[:, j:j + 1])
        chosen.append(onehot(idx_ref[:, 4 * j:4 * j + 1], experts))
    mean = gates[0] * dgates[0] + gates[1] * dgates[1]
    scale = 1.0 / gate_ref[:, 2:3]
    dprobs = jnp.where(chosen[0], (dgates[0] - mean) * scale, 0.0) + jnp.where(chosen[1], (dgates[1] - mean) * scale, 0.0)
    dlogits = (probs * (dprobs - jnp.sum(probs * dprobs, axis=-1, keepdims=True))).astype(bf16)
    small_ref[...] = jnp.zeros_like(small_ref)
    small_ref[:, 0:experts] = dot(xn_ref[...], dlogits, TN).astype(bf16)
    dxn = dxn + dot(dlogits, router_ref[...], NT)
    h = h_ref[...]
    r = lax.rsqrt(jnp.mean(h * h, axis=-1, keepdims=True) + epsilon)
    gain_row = jnp.sum(dxn * h * r, axis=0, keepdims=True)
    small_ref[:, experts:experts + 1] = column_of(gain_row).astype(bf16)
    scaled = dxn * gains_ref[1:2, :]
    dh = cot_ref[...].astype(f32) + r * scaled - h * (r * r * r) * jnp.mean(h * scaled, axis=-1, keepdims=True)
    dh_ref[...] = dh
    dhb_ref[...] = dh.astype(bf16)


def back(idx, cot, h, xn, probs, gate, router, gains, blocks, size, chunks, deps):
    count, width = h.shape
    experts = router.shape[1]
    outs = [sd((count, width), f32), sd((count, width), bf16), sd((width, 128), bf16)]
    return call(functools.partial(back_kernel, size, chunks), "back", outs, (idx, cot, h, xn, probs, gate, router, gains, *blocks),
                scratch=[pltpu.VMEM((experts * CAP, width), bf16)], deps=deps)


def mix_kernel(count, chunks, idx_ref, h_ref, gate_ref, *refs):
    blocks, out_ref, ys = refs[:count], refs[count], refs[count + 1]
    rows_of = blocks[0].shape[0]
    part = rows_of // chunks
    for k, block in enumerate(blocks):
        for c in range(chunks):
            ys[(c * count + k) * part:(c * count + k + 1) * part, :] = block[c * part:(c + 1) * part, :]
    out = h_ref[...]
    for j in (0, 1):
        out = out + gate_ref[:, j:j + 1] * dot(as_bf16(onehot(idx_ref[:, 4 * j + 1:4 * j + 2], rows_of * count)), ys[...])
    out_ref[...] = out.astype(bf16)


def mix(idx, h, gate, blocks, size, chunks, deps):
    count, width = h.shape
    return call(functools.partial(mix_kernel, len(blocks), chunks), "mix", [sd((count, width), bf16)], (idx, h, gate, *blocks),
                scratch=[pltpu.VMEM((len(blocks) * blocks[0].shape[0], width), bf16)], deps=deps)[0]


def last_kernel(tokens_ref, dh_ref, own, rx, ry, rd, gains_ref, out_ref):
    x = tokens_ref[...].astype(f32)
    r = lax.rsqrt(jnp.mean(x * x, axis=-1, keepdims=True) + epsilon)
    scaled = add_terms((own, rx, ry, rd)) * gains_ref[0:1, :]
    out_ref[...] = dh_ref[...] + r * scaled - x * (r * r * r) * jnp.mean(x * scaled, axis=-1, keepdims=True)


def merge_kernel(size, at_ref, keep_ref, got_ref, *outs):
    me = at_ref[0]
    for k in range(size):
        to = (me + k) & (size - 1)
        outs[k][...] = (keep_ref[to].astype(f32) + got_ref[to].astype(f32)).astype(bf16)


def total_kernel(size, at_ref, q_ref, k_ref, v_ref, *refs):
    blocks, out_ref, few_ref = refs[:size], refs[size], refs[size + 1]
    total = sum(b[...].astype(f32) for b in blocks)
    out_ref[...] = total
    half = total.shape[0]
    width = q_ref.shape[1]
    few = total[:, 4 * width:]
    lane = lax.broadcasted_iota(i32, few.shape, 1)
    for r in (0, 1):
        @pl.when(at_ref[1] == r)
        def _():
            product = sum(total[:, n * width:(n + 1) * width] * ref[r * half:(r + 1) * half, :].astype(f32) for n, ref in enumerate((q_ref, k_ref, v_ref)))
            few_ref[...] = jnp.where(lane == TABLE - 1, jnp.sum(product, axis=1, keepdims=True), few)


def finish_kernel(at_ref, mine_ref, other_ref, few_mine, few_other, gain_ref, q_ref, k_ref, v_ref, o_ref, router_ref, table_ref, ga_ref, gm_ref, few):
    half = mine_ref.shape[0]
    width = q_ref.shape[1]
    experts = router_ref.shape[0]
    rows = table_ref.shape[1]

    def put(first, second, few_first, few_second):
        for n, ref in enumerate((q_ref, k_ref, v_ref, o_ref)):
            ref[0:half, :] = first[:, n * width:(n + 1) * width]
            ref[half:, :] = second[:, n * width:(n + 1) * width]
        few[0:half, :] = few_first[...]
        few[half:, :] = few_second[...]
        table_ref[...] = first[:, 4 * width:].T[TABLE + 1:TABLE + 1 + table_ref.shape[0], 0:rows]

    pl.when(at_ref[1] == 0)(lambda: put(mine_ref, other_ref, few_mine, few_other))
    pl.when(at_ref[1] == 1)(lambda: put(other_ref, mine_ref, few_other, few_mine))
    turned = few[...].T
    router_ref[...] = turned[0:experts, :]
    ga_ref[...] = turned[TABLE - 1:TABLE, :] / gain_ref[...].astype(f32)
    gm_ref[...] = turned[TABLE - 2:TABLE - 1, :]


def on_device(size, tokens, segments, routes, capacity, cotangent, rel_table, w_query, w_key, w_value, w_attn_out, gain_attn, gain_moe, w_router, w_in, w_out):
    z = lax.axis_index("expert").astype(i32)
    rep = lax.axis_index("rep").astype(i32)
    pos = lax.axis_index("tensor").astype(i32)
    at = jnp.stack([z, rep, pos])
    tok = tokens[0]
    cot = cotangent[0]
    count, width = tok.shape
    local = w_in.shape[0]
    experts = w_router.shape[1]
    chunks = 2 if local >= 4 else 1
    part = local // chunks
    rows_dev = w_query.shape[0]
    half = rows_dev // 2
    buckets = rel_table.shape[0] * size
    part_rows = part * CAP
    half_rows = part_rows * size // 2
    matrix = order_matrix(size, part, part_rows, 0, 0)

    packed, rest = call(pack_kernel, "pack", [sd((half, 896), bf16)] * 2,
                        (at, w_query, w_key, w_value, w_router.T, w_attn_out, gain_attn, gain_moe, rel_table.T),
                        scratch=[pltpu.VMEM((rows_dev, 896), f32)], smem=1)
    mine = [to_expert(packed, k, size) for k in range(1, size)]
    other = [to_core(m) for m in mine]
    pieces = gather_pieces(tok, count // 2)
    idx = call(functools.partial(prepare_kernel, size, chunks), "prepare", [sd((count, 8), i32)], (z[None], routes[0].T, capacity[None]),
               smem=1, deps=(packed,))[0]

    g_blocks = spread(idx, cot, 0, size, local * CAP, (*mine, *pieces[1:3]), "spread_g", chunks)
    g_arrived = shifted(g_blocks)
    qkv_w, wo, router, gains, table = unpack(at, [packed, *mine], [rest, *other], buckets, (idx,))

    xn, qkv = project(at, pieces, qkv_w, gains, (g_blocks[0],))
    o, lse, *parts = attn_fwd(at, table, qkv, segments, wo, ())
    g_ordered = call(functools.partial(reorder_all_kernel, size), "order_g", [sd((local * CAP * size, width), bf16)], (matrix, *g_arrived), deps=(o,))[0]
    terms = scatter_direct(parts[0], after(parts[1], g_ordered), *parts[2:])
    h, xn2, probs, gate, *blocks = route(idx, tok, terms, router, gains, size, chunks, ())
    g_pieces = gather_pieces(after(g_ordered, xn2), half_rows * chunks)

    arrived = shifted(blocks)
    ordered = [reorder(order_matrix(size, part, part_rows + 16, 16, 16), arrived, "order")]
    got = [gather_pieces(ordered[0], half_rows)]
    if chunks == 2:
        blocks = spread(idx, xn2, 1, size, part_rows, (ordered[0], *g_pieces[1:3]), "spread", 1)
        ordered.append(reorder(matrix, shifted(blocks), "order"))
        got.append(gather_direct(ordered[1]))
    extras = (*got[0][:3], got[0][4])
    ready = ordered[1:]

    step = max(part // 4, 1)
    pending = [(c, start) for c in range(chunks) for start in range(0, part, step)]
    grads = ()

    def expert_grads(many, *ready):
        nonlocal grads
        mark = ready[0]
        for c, start in pending[:many]:
            *grads, mark = expert_grad(at, c * part, start, step, local, acts[c], other_acts[c], grads, ready)
        del pending[:many]
        return mark

    acts, sums, ys = [], [], []
    dg_full = jnp.zeros((4, lanes_of(size) // 128, 16, 128), f32)
    for c in range(chunks):
        *outs, dg_full, act = moe(at, size, chunks, c, got[c], extras, g_pieces, w_in, w_out, dg_full, () if c else ready)
        sums.append(scatter_direct(*outs[:4]) if c < chunks - 1 else outs[:4])
        ys.append(outs[4:])
        acts.append(act)
    other_acts = [to_core(acts[0])]


    def give(c, extra, deps):
        given = call(functools.partial(give_back_kernel, size, extra), "give_back", [sd((part_rows + 16 * extra, width), bf16)] * size,
                     (matrix, *sums[c]), deps=deps)
        return given[0], [given[0]] + [to_expert(given[k], size - k, size) for k in range(1, size)]

    outs = list(sums[-1])
    if chunks == 2:
        outs = [*outs[:1], *[after(piece, *sums[0][1:]) for piece in outs[1:4]]]
    sums[-1] = scatter_direct(*outs)
    back_blocks = []
    mark = outs[0]
    if chunks == 2:
        mark, back_blocks = give(0, False, (mark,))
    mark = expert_grads(1, mark)
    mark = expert_grads(1, mark, *back_blocks[1:])
    mark = expert_grads(1, mark)
    ready, blocks = give(chunks - 1, True, (mark,))
    if chunks == 2:
        y_packs = [after(ys[c][1], mark, *sums[-1][1:]) for c in (0, 1)]
        y_got = [to_tensor(pack, flip) for flip, pack in zip((1, 2), y_packs)]
    else:
        y_terms = scatter_direct(*ys[0])
    ready = (ready, *y_packs) if chunks == 2 else (ready,)
    dh, dhb, small = back(idx, cot, h, xn2, probs, gate, router, gains, back_blocks + blocks, size, chunks, ready)
    dh_pieces = gather_direct(dhb)
    mark = expert_grads(1, dhb)
    if chunks == 2:
        acts[1] = after(acts[1], mark)
        other_acts.append(to_core(acts[1]))
    if chunks == 2:
        y_parts, sent = scatter_end(*y_got, ys[1][2], ys[0][2], (mark,))
        mark = sent[0]

    y_late = (y_parts[1], y_parts[3]) if chunks == 2 else ()
    gtab, dqkv = attn_bwd(at, size, table, dh_pieces, segments, wo, qkv, lse, (mark,))
    keep, send, own, *parts = attn_grad(at, size, dqkv, qkv_w, xn, dh_pieces, o, small, gtab, y_late)
    terms = scatter_direct(own, *parts)
    got = to_core(send)
    out_blocks = call(functools.partial(merge_kernel, size), "merge", [sd((half, packed.shape[1]), bf16)] * size,
                      (at, keep, got), smem=1)
    outs = [sd((local * CAP, width), bf16)] * size
    if chunks == 2:
        given = call(functools.partial(give_back_halves_kernel, size), "give_back_y", outs, (matrix, ys[0][0], ys[1][0], *y_parts), deps=(out_blocks[0],))
    else:
        given = call(functools.partial(give_back_kernel, size, False), "give_back_y", outs, (matrix, *y_terms), deps=(out_blocks[0],))
    y_blocks = [given[0]] + [to_expert(given[k], size - k, size) for k in range(1, size)]
    grad_tokens = call(last_kernel, "last", [sd((count, width), f32)], (tok, dh, *terms, gains))[0]
    mark = expert_grads(1, out_blocks[0], given[0])
    mark = expert_grads(max(len(pending) - 2, 0), mark, *terms[1:])
    total, gain = call(functools.partial(total_kernel, size), "total", [sd(out_blocks[0].shape, f32), sd((half, 128), f32)],
                       (at, w_query, w_key, w_value, *shifted(out_blocks)), smem=1, deps=(mark, *terms[1:]))
    mark = expert_grads(1, total)
    gain = gain + to_tensor(gain, 1)
    mark = expert_grads(1, mark, gain)
    gain = gain + to_tensor(gain, 2)
    output = mix(idx, h, gate, y_blocks, size, chunks, (total,))
    lw = w_query.shape[1]
    outs = [sd((rows_dev, lw), f32)] * 4 + [sd((experts, rows_dev), f32), sd(rel_table.T.shape, f32)] + [sd((1, rows_dev), f32)] * 2
    grad_q, grad_k, grad_v, grad_o, grad_router, grad_table, grad_ga, grad_gm = call(
        finish_kernel, "finish", outs, (at, total, to_core(total), gain, to_core(gain), gain_attn[None]), smem=1, scratch=[pltpu.VMEM((rows_dev, 128), f32)], deps=(output, mark))
    return (output[None], grad_tokens[None], grad_table.T, grad_q, grad_k, grad_v, grad_o, grad_ga[0], grad_gm[0], grad_router.T, *grads)


def solution(mesh):
    by_token = P(("expert", "rep"), "tensor", None)
    both = P("expert", "tensor")
    return jax.shard_map(
        functools.partial(on_device, mesh.shape["expert"]),
        mesh=mesh,
        in_specs=(by_token, P(("expert", "rep"), None), by_token, P(), by_token, both, both, both, both, both, P("expert"), P("expert"),
                  P("expert", None), P("expert", None, "tensor"), P("expert", "tensor", None)),
        out_specs=(by_token, by_token, both, both, both, both, both, P("expert"), P("expert"), P("expert", None),
                   P("expert", None, "tensor"), P("expert", "tensor", None)),
        check_vma=False,
    )
```

```python
import functools
import math

import jax
import jax.numpy as jnp
from jax import lax
from jax.experimental import pallas as pl
from jax.experimental.pallas import tpu as pltpu
from jax.sharding import PartitionSpec as P

HEAD = 64
CAP = 12
QB = 128
TABLE = 66
epsilon = 1e-06
masked_value = -1e30
thresholds = (16, 19, 21, 24, 27, 31, 35, 40, 46, 52, 59, 67, 77, 87, 99, 113)
lowest = tuple(range(16)) + thresholds
f32 = jnp.float32
bf16 = jnp.bfloat16
i32 = jnp.int32
NN = (((1,), (0,)), ((), ()))
NT = (((1,), (1,)), ((), ()))
TN = (((0,), (0,)), ((), ()))
VM = pl.BlockSpec(memory_space=pltpu.VMEM)
SM = pl.BlockSpec(memory_space=pltpu.SMEM)
sd = jax.ShapeDtypeStruct


def dot(a, b, dims=NN):
    return lax.dot_general(a, b, dims, preferred_element_type=f32)


ANY = pl.BlockSpec(memory_space=pl.ANY)
TIMES = {"attn_fwd": 13, "attn_bwd": 400, "attn_grad": 9, "project": 5, "moe": 300, "expert_grad": 1, "back": 5, "route": 4}


def cost(name):
    return pl.CostEstimate(flops=int(TIMES.get(name, 0.5) * 1_150_000_000), bytes_accessed=1000, transcendentals=0)


def call(kernel, name, outs, operands, scratch=(), smem=0, flops=0, moved=4_000_000, deps=()):
    given = len(operands)

    def body(*refs):
        kernel(*refs[:given], *refs[given + len(deps):])

    return pl.pallas_call(
        body,
        out_shape=tuple(outs),
        in_specs=[SM] * smem + [VM] * (given - smem) + [ANY] * len(deps),
        out_specs=tuple(VM for _ in outs),
        scratch_shapes=list(scratch),
        compiler_params=pltpu.CompilerParams(vmem_limit_bytes=56 << 20),
        cost_estimate=cost(name),
        name=name,
    )(*operands, *deps)


def after(value, *deps):
    return pl.pallas_call(
        lambda *refs: None,
        out_shape=sd(value.shape, value.dtype),
        in_specs=[ANY] * (1 + len(deps)),
        out_specs=ANY,
        input_output_aliases={0: 0},
        name="after",
    )(value, *deps)


def to_tensor(a, flip):
    return lax.ppermute(a, "tensor", [(i, i ^ flip) for i in range(4)])


def to_expert(a, shift, size):
    return lax.ppermute(a, "expert", [(i, (i + shift) % size) for i in range(size)])


def to_core(a):
    return lax.ppermute(a, "rep", [(0, 1), (1, 0)])


def shifted(blocks):
    size = len(blocks)
    return [blocks[0]] + [to_expert(blocks[k], k, size) for k in range(1, size)]


def gather_pieces(own, half):
    px = to_tensor(own, 1)
    py = to_tensor(own, 2)
    d0 = to_tensor(px[:half], 2)
    d1 = to_tensor(py[half:], 1)
    return own, px, py, d0, d1


def gather_direct(own):
    return (own, *[to_tensor(own, flip) for flip in (1, 2, 3)])


def late_kernel(x_late, y_late, got_x, got_y, sum_x, sum_y):
    sum_x[...] = (x_late[...].astype(f32) + got_y[0].astype(f32)).astype(bf16)
    sum_y[...] = (y_late[...].astype(f32) + got_x[0].astype(f32)).astype(bf16)


def scatter_end(got_x, got_y, x_late, y_late, deps):
    shape = sd(x_late.shape, bf16)
    sent = call(late_kernel, "late", [shape, shape], (x_late, y_late, got_x, got_y), deps=deps)
    return (got_x, to_tensor(sent[1], 2), got_y, to_tensor(sent[0], 1)), sent


def scatter_direct(own, *pieces):
    return (own, *[to_tensor(piece, flip) for flip, piece in zip((1, 2, 3), pieces)])


def add_terms(refs):
    return sum(r[...].astype(f32) for r in refs)


def onehot(index, width):
    return lax.broadcasted_iota(i32, (index.shape[0], width), 1) == index


def as_bf16(mask):
    return jnp.where(mask, 1.0, 0.0).astype(bf16)


def prepare_kernel(size, chunks, me_ref, routes_ref, capacity_ref, idx_ref):
    count = routes_ref.shape[1]
    experts = capacity_ref.shape[1]
    local = experts // size
    part = local // chunks
    me = me_ref[0]
    first, second = (jnp.broadcast_to(routes_ref[j:j + 1, :], (8, count)).T[:, 0:1] for j in (0, 1))
    both = as_bf16(onehot(first, experts)) + as_bf16(onehot(second, experts))
    rows = lax.broadcasted_iota(i32, (count, count), 0)
    cols = lax.broadcasted_iota(i32, (count, count), 1)
    before = dot(as_bf16(cols < rows), both)
    capacity = capacity_ref[...].astype(f32)
    shift = int(math.log2(local))
    columns = []
    for route in (first, second):
        mine = onehot(route, experts)
        position = jnp.sum(jnp.where(mine, before, 0.0), axis=1, keepdims=True)
        limit = jnp.sum(jnp.where(mine, jnp.broadcast_to(capacity, mine.shape), 0.0), axis=1, keepdims=True)
        keep = position < limit
        position = position.astype(i32)
        owner = lax.shift_right_logical(route, jnp.full_like(route, shift))
        inner = route & (local - 1)
        away = (owner - me + size) & (size - 1)
        chunk = lax.shift_right_logical(inner, jnp.full_like(route, int(math.log2(part))))
        slot = ((chunk * size + away) * part + (inner & (part - 1))) * CAP + position
        columns += [route, jnp.where(keep, slot, -1), jnp.where(keep, away * local + inner, -1), away * CAP + position]
    for n, column in enumerate(columns):
        idx_ref[:, n:n + 1] = column


def spread_kernel(first, chunks, idx_ref, rows_ref, *outs):
    count = len(outs)
    block = outs[0].shape[0] // chunks
    width = block * chunks * count
    spread = as_bf16(onehot(idx_ref[:, 1:2] - first, width)) + as_bf16(onehot(idx_ref[:, 5:6] - first, width))
    slots = dot(spread, rows_ref[...], TN).astype(bf16)
    for c in range(chunks):
        for k, ref in enumerate(outs):
            ref[c * block:(c + 1) * block, :] = slots[(c * count + k) * block:(c * count + k + 1) * block]


def spread(idx, rows, chunk, count, block, deps, name, chunks):
    return call(functools.partial(spread_kernel, chunk * count * block, chunks), name, [sd((block, rows.shape[1]), bf16)] * count, (idx, rows), deps=deps)


def order_matrix(size, part, block, extra, out_extra):
    rows = part * size * CAP
    m = [[0.0] * (size * block) for _ in range(rows + out_extra)]
    for e in range(part):
        for k in range(size):
            for c in range(CAP):
                m[(e * size + k) * CAP + c][k * block + e * CAP + c] = 1.0
    for r in range(extra):
        for k in range(size):
            m[rows + r][k * block + part * CAP + r] = 1.0
    return jnp.array(m, dtype=bf16)


def reorder_kernel(count, m_ref, *refs):
    blocks, out_ref = refs[:count], refs[count]
    out_ref[...] = dot(m_ref[...], jnp.concatenate([b[...] for b in blocks], axis=0)).astype(bf16)


def reorder_all_kernel(count, m_ref, *refs):
    blocks, out_ref = refs[:count], refs[count]
    block = m_ref.shape[1] // count
    rows = m_ref.shape[0]
    for c in range(out_ref.shape[0] // rows):
        chosen = jnp.concatenate([b[c * block:(c + 1) * block, :] for b in blocks], axis=0)
        out_ref[c * rows:(c + 1) * rows, :] = dot(m_ref[...], chosen).astype(bf16)


def reorder(matrix, blocks, name, deps=()):
    rows = matrix.shape[0]
    width = blocks[0].shape[1]
    return call(functools.partial(reorder_kernel, len(blocks)), name, [sd((rows, width), bf16)], (matrix, *blocks),
                flops=2 * matrix.size * width, moved=2 * rows * width * 2, deps=deps)[0]


def give_back_kernel(count, extra, m_ref, *refs):
    outs = refs[4:]
    total = add_terms(refs[:4]).astype(bf16)
    rows = m_ref.shape[0]
    back = dot(m_ref[...], total[0:rows], TN).astype(bf16)
    block = back.shape[0] // count
    for k in range(count):
        outs[k][0:block, :] = back[k * block:(k + 1) * block]
        if extra:
            outs[k][block:, :] = total[rows:]


def give_back_halves_kernel(count, m_ref, own_a, own_b, got_x, late_y, got_y, late_x, *outs):
    halves = (own_a[...].astype(f32) + got_x[1].astype(f32) + late_y[...].astype(f32), own_b[...].astype(f32) + got_y[1].astype(f32) + late_x[...].astype(f32))
    for n, total in enumerate(halves):
        back = dot(m_ref[...], total.astype(bf16), TN).astype(bf16)
        block = back.shape[0] // count
        for k in range(count):
            outs[k][n * block:(n + 1) * block, :] = back[k * block:(k + 1) * block]


def pack_kernel(at_ref, q_ref, k_ref, v_ref, r_ref, o_ref, ga_ref, gm_ref, t_ref, out_ref, rest_ref, full):
    rows, width = q_ref.shape
    full[...] = jnp.zeros_like(full)
    place = 0
    for ref in (q_ref, k_ref, v_ref, r_ref, o_ref):
        value = ref[...].astype(f32)
        value = value.T if ref is r_ref else value
        full[:, place:place + value.shape[1]] = value
        place += value.shape[1]
    for ref in (ga_ref, gm_ref):
        full[:, place:place + 1] = column_of(ref[...].astype(f32)[None, :])
        place += 1
    full[0:t_ref.shape[1], place:place + t_ref.shape[0]] = t_ref[...].astype(f32).T
    half = rows // 2
    for r in (0, 1):
        @pl.when(at_ref[1] == r)
        def _():
            out_ref[...] = full[r * half:(r + 1) * half, :].astype(bf16)
            rest_ref[...] = full[(1 - r) * half:(2 - r) * half, :].astype(bf16)


def unpack_kernel(size, at_ref, *refs):
    mine, other = refs[:size], refs[size:2 * size]
    full, qkv_ref, wo_ref, router_ref, gains_ref, table_ref = refs[2 * size:]
    me, rep = at_ref[0], at_ref[1]
    half = mine[0].shape[0]
    for k in range(size):
        z = (me - k + size) & (size - 1)
        full[2 * z + rep] = mine[k][...].astype(f32)
        full[2 * z + 1 - rep] = other[k][...].astype(f32)
    full = jnp.concatenate([full[n] for n in range(2 * size)], axis=0)
    qkv_ref[...] = full[:, 0:576].astype(bf16)
    router_ref[...] = full[:, 576:640].astype(bf16)
    wo_ref[...] = full[:, 640:832].astype(bf16)
    tail = full[:, 768:896]
    turned = tail.T
    gains_ref[...] = turned[64:72, :]
    rows = table_ref.shape[0] // size
    for z in range(size):
        table_ref[z * rows:(z + 1) * rows, :] = tail[z * 2 * half: z * 2 * half + rows, :]


def unpack(at, mine, other, buckets, deps):
    size = len(mine)
    half, cols = mine[0].shape
    width = 2 * half * size

    def kernel(at_ref, *refs):
        unpack_kernel(size, at_ref, *refs[:2 * size], refs[-1], *refs[2 * size:-1])

    outs = [sd((width, 576), bf16), sd((width, 192), bf16), sd((width, 64), bf16), sd((8, width), f32), sd((buckets, 128), f32)]
    return call(kernel, "unpack", outs, (at, *mine, *other), scratch=[pltpu.VMEM((2 * size, half, cols), f32)], smem=1, deps=deps)


def piece_shapes(rows, width):
    return [sd((rows, width), bf16)] * 4


def near_offset():
    rows = lax.broadcasted_iota(jnp.int32, (QB, 2 * QB), 0)
    cols = lax.broadcasted_iota(jnp.int32, (QB, 2 * QB), 1)
    return QB + rows - cols


def near_bias(table_ref, head, buckets):
    off = near_offset()
    bias = jnp.where(off < 0, masked_value, table_ref[0, TABLE + head])
    for b in range(1, buckets):
        bias = jnp.where(off >= lowest[b], table_ref[b, TABLE + head], bias)
    return bias


def scores_of(q, k_ref, head, i, near, far, seg_col, seg_row_ref):
    lo = max(i - 1, 0) * QB
    hi = (i + 1) * QB
    s = dot(q, k_ref[head, 0:hi], NT)
    bias = near[:, QB:] if i == 0 else near
    same_near = seg_col == seg_row_ref[:, lo:hi]
    s_near = jnp.where(same_near, s[:, lo:hi] + bias, masked_value)
    if lo == 0:
        return s_near
    same_far = seg_col == seg_row_ref[:, 0:lo]
    s_far = jnp.where(same_far, s[:, 0:lo] + far, masked_value)
    return jnp.concatenate([s_far, s_near], axis=1)


def project_kernel(at_ref, own_ref, px_ref, py_ref, pd0_ref, pd1_ref, w_ref, gain_ref, xn_ref, qkv_ref):
    pos = at_ref[2]
    tok = own_ref.shape[0]
    half = tok // 2
    gain = gain_ref[0:1, :]

    def put(rows, flip, start=0):
        x = rows.astype(f32)
        r = lax.rsqrt(jnp.mean(x * x, axis=-1, keepdims=True) + epsilon)
        xn = (x * r * gain).astype(bf16)
        at = pl.ds(pl.multiple_of((pos ^ flip) * tok + start, half), rows.shape[0])
        xn_ref[at, :] = xn
        qkv_ref[at, :] = dot(xn, w_ref[...]).astype(bf16)

    put(own_ref[...], 0)
    put(px_ref[...], 1)
    put(py_ref[...], 2)
    put(pd0_ref[...], 3)
    put(pd1_ref[...], 3, half)


def column_of(row):
    return jnp.broadcast_to(row, (8, row.shape[1])).T[:, 0:1]


def attn_fwd_kernel(heads, at_ref, table_ref, qkv_ref, segr_ref, wo_ref, o_ref, lse_ref, out_own, out_x, out_y, out_d, qs, ks, vs, seg):
    pos = at_ref[2]
    tok = out_own.shape[0]
    half = tok // 2
    buckets = table_ref.shape[0]
    seg[...] = column_of(segr_ref[...])

    def at(flip, start=0, size=tok):
        return pl.ds(pl.multiple_of((pos ^ flip) * tok + start, half), size)

    width = heads * HEAD
    qkv = qkv_ref[...]
    for h in range(heads):
        qs[h] = qkv[:, h * HEAD:(h + 1) * HEAD] * bf16(0.125)
        ks[h] = qkv[:, width + h * HEAD: width + (h + 1) * HEAD]
        vs[h] = qkv[:, 2 * width + h * HEAD: 2 * width + (h + 1) * HEAD]
    blocks = qkv_ref.shape[0] // QB
    for h in range(heads):
        near = near_bias(table_ref, h, buckets)
        far = table_ref[buckets - 1, TABLE + h]
        for i in range(blocks):
            rows = slice(i * QB, (i + 1) * QB)
            s = scores_of(qs[h, rows], ks, h, i, near, far, seg[rows, :], segr_ref)
            top = jnp.max(s, axis=-1, keepdims=True)
            e = jnp.exp(s - top)
            total = jnp.sum(e, axis=-1, keepdims=True)
            p = (e * (1.0 / total)).astype(bf16)
            o_ref[rows, h * HEAD:(h + 1) * HEAD] = dot(p, vs[h, 0:(i + 1) * QB]).astype(bf16)
            lse_ref[rows, h:h + 1] = top + jnp.log(total)
    wo = wo_ref[...]
    for flip, ref in enumerate((out_own, out_x, out_y, out_d)):
        ref[...] = dot(o_ref[at(flip), :], wo, NT).astype(bf16)


def attn_bwd_kernel(heads, size, at_ref, table_ref, own_ref, px_ref, py_ref, pd_ref, segr_ref, wo_ref, qkv_ref, lse_ref,
                    gtab_ref, dqkv, dh, qs, ks, vs, do, dk, dv, acc, seg):
    pos = at_ref[2]
    tok = own_ref.shape[0]
    half = tok // 2
    buckets = table_ref.shape[0]
    width = heads * HEAD

    def at(flip, start=0, size=tok):
        return pl.ds(pl.multiple_of((pos ^ flip) * tok + start, half), size)

    seg[...] = column_of(segr_ref[...])
    dh[at(0), :] = own_ref[...]
    dh[at(1), :] = px_ref[...]
    dh[at(2), :] = py_ref[...]
    dh[at(3), :] = pd_ref[...]
    dall = dot(dh[...], wo_ref[...]).astype(bf16)
    for h in range(heads):
        do[h] = dall[:, h * HEAD:(h + 1) * HEAD]
        qs[h] = qkv_ref[:, h * HEAD:(h + 1) * HEAD] * bf16(0.125)
        ks[h] = qkv_ref[:, width + h * HEAD: width + (h + 1) * HEAD]
        vs[h] = qkv_ref[:, 2 * width + h * HEAD: 2 * width + (h + 1) * HEAD]
    blocks = qkv_ref.shape[0] // QB
    off = near_offset()
    per = gtab_ref.shape[1]
    gtab_ref[...] = jnp.zeros_like(gtab_ref)
    for h in range(heads):
        near = near_bias(table_ref, h, buckets)
        far = table_ref[buckets - 1, TABLE + h]
        acc[...] = jnp.zeros_like(acc)
        dk[...] = jnp.zeros_like(dk)
        dv[...] = jnp.zeros_like(dv)
        far_sum = jnp.zeros((QB, 1), f32)
        for i in range(blocks):
            rows = slice(i * QB, (i + 1) * QB)
            lo = max(i - 1, 0) * QB
            hi = (i + 1) * QB
            q = qs[h, rows]
            s = scores_of(q, ks, h, i, near, far, seg[rows, :], segr_ref)
            p = jnp.exp(s - lse_ref[rows, h:h + 1])
            g = do[h, rows]
            dv[0:hi] += dot(p.astype(bf16), g, TN)
            dp = dot(g, vs[h, 0:hi], NT)
            pd = p * dp
            ds = (pd - p * jnp.sum(pd, axis=-1, keepdims=True)).astype(bf16)
            dq = dot(ds, ks[h, 0:hi]) * 0.125
            dqkv[rows, h * HEAD:(h + 1) * HEAD] = dq.astype(bf16)
            dk[0:hi] += dot(ds, q, TN)
            dsf = ds.astype(f32)
            if i == 0:
                acc[:, QB:] += dsf
            else:
                acc[...] += dsf[:, lo:hi]
            if lo > 0:
                far_sum = far_sum + jnp.sum(dsf[:, 0:lo], axis=-1, keepdims=True)
        dqkv[:, width + h * HEAD: width + (h + 1) * HEAD] = dk[...].astype(bf16)
        dqkv[:, 2 * width + h * HEAD: 2 * width + (h + 1) * HEAD] = dv[...].astype(bf16)
        total = acc[...]
        rest = jnp.sum(far_sum, axis=0, keepdims=True)
        for b in range(buckets):
            if b == buckets - 1:
                inside = off >= lowest[b]
            else:
                inside = (off >= lowest[b]) & (off < lowest[b + 1])
            part = jnp.sum(jnp.where(inside, total, 0.0), axis=0, keepdims=True)
            one = jnp.sum(part, axis=1, keepdims=True)
            gtab_ref[b // per, b % per:b % per + 1, TABLE + 1 + h:TABLE + 2 + h] = one + rest if b == buckets - 1 else one


def attn_grad_kernel(size, at_ref, dqkv, w_ref, xn_ref, own_ref, px_ref, py_ref, pd_ref, o_ref, small_ref, gtab_ref, keep_ref, send_ref,
                     out_own, out_x, out_y, out_d, dh, full):
    pos, rep = at_ref[2], at_ref[1]
    tok = out_own.shape[0]
    half = tok // 2
    width = o_ref.shape[1]

    def at(flip, start=0, size=tok):
        return pl.ds(pl.multiple_of((pos ^ flip) * tok + start, half), size)

    dh[at(0), :] = own_ref[...]
    dh[at(1), :] = px_ref[...]
    dh[at(2), :] = py_ref[...]
    dh[at(3), :] = pd_ref[...]
    w = w_ref[...]
    for flip, ref in enumerate((out_own, out_x, out_y, out_d)):
        ref[...] = dot(dqkv[at(flip), :], w, NT).astype(bf16)
    grad = dot(xn_ref[...], dqkv[...], TN)
    grad_out = dot(dh[...], o_ref[...], TN)
    part_rows = keep_ref.shape[1]
    for n in range(2 * size):
        full[n, :, 0:3 * width] = grad[n * part_rows:(n + 1) * part_rows].astype(bf16)
        full[n, :, 3 * width:4 * width] = grad_out[n * part_rows:(n + 1) * part_rows].astype(bf16)
        few = small_ref[n * part_rows:(n + 1) * part_rows, :]
        full[n, :, 4 * width:] = few
        if n % 2 == 0:
            rows = gtab_ref.shape[1]
            full[n, 0:rows, 4 * width:] = (few[0:rows].astype(f32) + gtab_ref[n // 2]).astype(bf16)
    for z in range(size):
        keep_ref[z] = full[2 * z + rep]
        send_ref[z] = full[2 * z + 1 - rep]


def project(at, pieces, w, gains, deps):
    tok, width = pieces[0].shape
    return call(project_kernel, "project", [sd((4 * tok, width), bf16), sd((4 * tok, w.shape[1]), bf16)], (at, *pieces, w, gains),
                smem=1, deps=deps)


def attn_fwd(at, table, qkv, segr, wo, deps):
    width = wo.shape[0]
    length = qkv.shape[0]
    heads = wo.shape[1] // HEAD
    outs = [sd((length, heads * HEAD), bf16), sd((length, heads), f32)]
    return call(functools.partial(attn_fwd_kernel, heads), "attn_fwd", outs + piece_shapes(length // 4, width),
                (at, table, qkv, segr, wo),
                scratch=[pltpu.VMEM((heads, length, HEAD), bf16)] * 3 + [pltpu.VMEM((length, 1), i32)], smem=2,
                flops=8_000_000_000, moved=5_000_000, deps=deps)


def attn_bwd(at, size, table, pieces, segr, wo, qkv, lse, deps):
    tok, width = pieces[0].shape
    length = qkv.shape[0]
    heads = wo.shape[1] // HEAD
    outs = [sd((size, table.shape[0] // size, 128), f32), sd(qkv.shape, bf16)]
    scratch = [pltpu.VMEM((length, width), bf16)] + [pltpu.VMEM((heads, length, HEAD), bf16)] * 4 + [pltpu.VMEM((length, HEAD), f32)] * 2
    scratch += [pltpu.VMEM((QB, 2 * QB), f32), pltpu.VMEM((length, 1), i32)]
    return call(functools.partial(attn_bwd_kernel, heads, size), "attn_bwd", outs, (at, table, *pieces, segr, wo, qkv, lse),
                scratch=scratch, smem=2, flops=12_000_000_000, moved=8_000_000, deps=deps)


def attn_grad(at, size, dqkv, w, xn, pieces, o, small, gtab, deps):
    tok, width = pieces[0].shape
    cols = w.shape[1] + o.shape[1] + small.shape[1]
    rows = width // (2 * size)
    outs = [sd((size, rows, cols), bf16)] * 2 + piece_shapes(tok, width)
    return call(functools.partial(attn_grad_kernel, size), "attn_grad", outs, (at, dqkv, w, xn, *pieces, o, small, gtab),
                scratch=[pltpu.VMEM((4 * tok, width), bf16), pltpu.VMEM((2 * size, rows, cols), bf16)], smem=1,
                flops=4_000_000_000, moved=9_000_000, deps=deps)


def route_kernel(size, chunks, idx_ref, tokens_ref, own, rx, ry, rd, router_ref, gains_ref, h_ref, xn_ref, probs_ref, gate_ref, *blocks):
    count, width = tokens_ref.shape
    experts = router_ref.shape[1]
    local = experts // size
    rows_of = local // chunks * CAP
    lanes = lanes_of(size)
    h = tokens_ref[...].astype(f32) + add_terms((own, rx, ry, rd))
    r = lax.rsqrt(jnp.mean(h * h, axis=-1, keepdims=True) + epsilon)
    xn = (h * r * gains_ref[1:2, :]).astype(bf16)
    h_ref[...] = h
    xn_ref[...] = xn
    logits = dot(xn, router_ref[...])
    e = jnp.exp(logits - jnp.max(logits, axis=-1, keepdims=True))
    probs = e / jnp.sum(e, axis=-1, keepdims=True)
    probs_ref[...] = probs
    picked = [jnp.sum(jnp.where(onehot(idx_ref[:, 4 * j:4 * j + 1], experts), probs, 0.0), axis=-1, keepdims=True) for j in (0, 1)]
    total = picked[0] + picked[1]
    gates = [p / total for p in picked]
    gate_ref[:, 0:1], gate_ref[:, 1:2], gate_ref[:, 2:3] = gates[0], gates[1], total
    spread = as_bf16(onehot(idx_ref[:, 1:2], size * rows_of)) + as_bf16(onehot(idx_ref[:, 5:6], size * rows_of))
    slots = dot(spread, xn, TN).astype(bf16)
    held = jnp.zeros((experts, lanes), f32)
    for j in (0, 1):
        to = as_bf16(onehot(idx_ref[:, 4 * j + 2:4 * j + 3], experts))
        at = jnp.where(onehot(idx_ref[:, 4 * j + 3:4 * j + 4], lanes), gates[j], 0.0).astype(bf16)
        held = held + dot(to, at, TN)
    for k, ref in enumerate(blocks):
        ref[0:rows_of, :] = slots[k * rows_of:(k + 1) * rows_of]
        ref[rows_of:, :] = jnp.zeros((16, width), bf16)
        ref[rows_of:rows_of + local, 0:lanes] = held[k * local:(k + 1) * local].astype(bf16)


def lanes_of(size):
    return -(-size * CAP // 128) * 128


def route(idx, tokens, parts, router, gains, size, chunks, deps):
    count, width = tokens.shape
    experts = router.shape[1]
    rows_of = experts // size // chunks * CAP
    outs = [sd((count, width), f32), sd((count, width), bf16), sd((count, experts), f32), sd((count, 8), f32)]
    outs += [sd((rows_of + 16, width), bf16)] * size
    return call(functools.partial(route_kernel, size, chunks), "route", outs, (idx, tokens, *parts, router, gains),
                flops=400_000_000, moved=5_000_000, deps=deps)


def moe_kernel(rows, part, offset, last, skip, at_ref, own, px, py, d0, d1, e_own, e_px, e_py, e_d, g_own, g_px, g_py, g_far, win_ref, wout_ref,
               dg_in, *refs):
    outs, y_outs, dg_ref, acts = refs[skip:skip + 4], refs[skip + 4:-2], refs[-2], refs[-1]
    e, j = pl.program_id(0), pl.program_id(1)
    steps = pl.num_programs(1)

    @pl.when((e == 0) & (j == 0))
    def _():
        dg_ref[...] = dg_in[...]

    wide = e_own.shape[1]
    pick = lax.broadcasted_iota(i32, (16, wide), 0) == e + offset
    square = lax.broadcasted_iota(i32, (rows, wide), 0) + j * rows == lax.broadcasted_iota(i32, (rows, wide), 1)

    def gate_of(ref):
        row = jnp.sum(jnp.where(pick, ref[...].astype(f32), 0.0), axis=0, keepdims=True)
        return jnp.sum(jnp.where(square, jnp.broadcast_to(row, square.shape), 0.0), axis=1, keepdims=True)

    def keep(n, value):
        for flip in range(4):
            acts[n, 0, flip] = value[flip * rows:(flip + 1) * rows]

    def put(value, outs):
        at = pl.ds(pl.multiple_of((e * steps + j) * rows, 16), rows)
        for flip, ref in enumerate(outs):
            ref[at, :] = value[flip * rows:(flip + 1) * rows]

    gate = jnp.concatenate([gate_of(r) for r in (e_own, e_px, e_py, e_d)], axis=0)
    far = jnp.where(e < part // 2, d0[...].astype(f32), d1[...].astype(f32)).astype(bf16)
    s = jnp.concatenate([own[...], px[...], py[...], far], axis=0)
    g = jnp.concatenate([g_own[...], g_px[...], g_py[...], g_far[...]], axis=0).astype(f32)
    keep(0, s)
    win, wout = win_ref[0], wout_ref[0]
    dy = (g * gate).astype(bf16)
    keep(1, dy)
    a = dot(s, win)
    dhid = dot(dy, wout, NT)
    c = math.sqrt(2.0 / math.pi)
    t = jnp.tanh(a * (c + (c * 0.044715) * (a * a)))
    up = 0.5 + 0.5 * t
    hid = (a * up).astype(bf16)
    slope = up + (0.5 * a) * (1.0 - t * t) * (c + (3 * c * 0.044715) * (a * a))
    da = (dhid * slope).astype(bf16)
    keep(2, hid)
    keep(3, da)
    put(dot(da, win, NT).astype(bf16), outs)
    y = dot(hid, wout)
    ones = jnp.ones((8, y.shape[1]), bf16)
    sums = dot(ones, (y * g).astype(bf16), NT)
    if len(y_outs) == 4:
        put(y.astype(bf16), y_outs)
    else:
        near = 1 if offset == 0 else 2
        own_ref, pack, once = y_outs
        put(y.astype(bf16), [own_ref] + ([pack.at[1], once] if near == 1 else [once, pack.at[1]]) + [pack.at[0]])
    for flip in range(4):
        row = sums[0:1, flip * rows:(flip + 1) * rows]
        dg_ref[flip, j, pl.ds(e + offset, 1), 0:rows] = row

    if last:
        @pl.when((e == part - 1) & (j == steps - 1))
        def _():
            for flip, ref in enumerate(outs):
                ref[-16:, :] = jnp.zeros((16, ref.shape[1]), bf16)
                for n in range(wide // 128):
                    ref[-16:, n * 128:(n + 1) * 128] = dg_ref[flip, n].astype(bf16)


def moe(at, size, chunks, chunk, pieces, extras, g, w_in, w_out, dg, deps):
    all_rows = size * CAP
    rows = 128 if all_rows % 128 == 0 else all_rows
    steps = all_rows // rows
    local, width, hidden = w_in.shape
    part = local // chunks
    lanes = -(-all_rows // 128) * 128
    first = chunk * part
    whole = lambda e, j: (e * steps + j, 0)
    flat = pl.BlockSpec((rows, width), whole)
    of_all = pl.BlockSpec((rows, width), lambda e, j: ((first + e) * steps + j, 0))
    half = part // 2
    low = pl.BlockSpec((rows, width), lambda e, j: (jnp.where(e < half, e * steps + j, half * steps - 1), 0))
    high = pl.BlockSpec((rows, width), lambda e, j: (jnp.where(e < half, 0, (e - half) * steps + j), 0))
    ext = lambda start: pl.BlockSpec((16, lanes), lambda e, j: (start // 16, 0))
    two_steps = len(pieces) == 5
    in_specs = [SM] + [flat] * 3 + ([low, high] if two_steps else [flat, flat])
    in_specs += [ext(part * all_rows)] * 3 + [ext(half * all_rows)] + [of_all] * 3 + [flat]
    in_specs += [pl.BlockSpec((1, width, hidden), lambda e, j: (first + e, 0, 0)), pl.BlockSpec((1, hidden, width), lambda e, j: (first + e, 0, 0))]
    operands = [at, *pieces, *([] if two_steps else pieces[3:]), *extras, *g[:3], g[3 + chunk], w_in, w_out]
    last = chunk == chunks - 1
    shape = (part * all_rows + 16 * last, width)
    total = part * all_rows
    y_shapes = [(total, width), (2, total, width), (total, width)] if chunks == 2 else [(total, width)] * 4
    outs = [sd(shape, bf16)] * 4 + [sd(y, bf16) for y in y_shapes] + [sd(dg.shape, f32), sd((4, part, 4, all_rows, width), bf16)]
    every = lambda dims: pl.BlockSpec(dims, lambda e, j: (0,) * len(dims))
    out_specs = [every(shape)] * 4 + [every(y) for y in y_shapes]
    out_specs += [every(dg.shape), pl.BlockSpec((4, 1, 4, rows, width), lambda e, j: (0, e, 0, j, 0))]
    operands.append(dg)
    in_specs.append(every(dg.shape))
    operands += list(deps)
    in_specs += [ANY] * len(deps)
    return pl.pallas_call(
        functools.partial(moe_kernel, rows, part, first, last, len(deps)),
        grid=(part, steps),
        out_shape=tuple(outs), in_specs=in_specs, out_specs=tuple(out_specs),
        compiler_params=pltpu.CompilerParams(vmem_limit_bytes=58 << 20),
        cost_estimate=cost("moe"),
        name="moe",
    )(*operands)


def expert_grad_kernel(steps, at_ref, mine, other, *refs):
    gin, gout, mark = refs[-3:]
    mark[...] = jnp.zeros_like(mark)

    def put(a, b):
        both = [jnp.concatenate([r[n, 0, flip] for r in (a, b) for flip in range(4)], axis=0) for n in range(4)]
        for ref, left, right in ((gin, both[0], both[3]), (gout, both[2], both[1])):
            if steps == 1:
                ref[0] = dot(left, right, TN)
            else:
                part = dot(left, right, TN)
                ref[0] = jnp.where(pl.program_id(1) == 0, part, ref[0] + part)

    pl.when(at_ref[1] == 0)(lambda: put(mine, other))
    pl.when(at_ref[1] == 1)(lambda: put(other, mine))


def expert_grad(at, first, start, part, local, mine, other, before, deps):
    four, all_rows, width = mine.shape[2:]
    rows = 128 if all_rows % 128 == 0 else all_rows
    steps = all_rows // rows
    spec = pl.BlockSpec((4, 1, 4, rows, width), lambda e, j: (0, start + e, 0, j, 0))
    in_specs = [SM, spec, spec]
    operands = [at, mine, other]
    alias = {}
    if before:
        alias = {3: 0, 4: 1}
        operands += list(before)
        in_specs += [ANY] * 2
    operands += list(deps)
    in_specs += [ANY] * len(deps)
    out = pl.BlockSpec((1, width, width), lambda e, j: (first + start + e, 0, 0))
    return pl.pallas_call(
        functools.partial(expert_grad_kernel, steps),
        grid=(part, steps),
        out_shape=(sd((local, width, width), f32),) * 2 + (sd((8, 128), f32),), in_specs=in_specs,
        out_specs=(out, out, pl.BlockSpec((8, 128), lambda e, j: (0, 0))),
        input_output_aliases=alias,
        compiler_params=pltpu.CompilerParams(vmem_limit_bytes=56 << 20),
        cost_estimate=cost("expert_grad"),
        name="expert_grad",
    )(*operands)


def back_kernel(size, chunks, idx_ref, cot_ref, h_ref, xn_ref, probs_ref, gate_ref, router_ref, gains_ref, *refs):
    blocks = refs[:chunks * size]
    dh_ref, dhb_ref, small_ref, ds = refs[chunks * size:]
    experts = router_ref.shape[1]
    local = experts // size
    rows_of = local // chunks * CAP
    lanes = lanes_of(size)
    for n, block in enumerate(blocks):
        ds[n * rows_of:(n + 1) * rows_of, :] = block[0:rows_of, :]
    last = blocks[(chunks - 1) * size:]
    held = jnp.concatenate([last[k][rows_of:rows_of + local, 0:lanes].astype(f32) for k in range(size)], axis=0).astype(bf16)
    spread = as_bf16(onehot(idx_ref[:, 1:2], experts * CAP)) + as_bf16(onehot(idx_ref[:, 5:6], experts * CAP))
    dxn = dot(spread, ds[...])
    probs = probs_ref[...]
    gates, dgates, chosen = [], [], []
    for j in (0, 1):
        got = dot(as_bf16(onehot(idx_ref[:, 4 * j + 2:4 * j + 3], experts)), held)
        dgates.append(jnp.sum(jnp.where(onehot(idx_ref[:, 4 * j + 3:4 * j + 4], lanes), got, 0.0), axis=-1, keepdims=True))
        gates.append(gate_ref[:, j:j + 1])
        chosen.append(onehot(idx_ref[:, 4 * j:4 * j + 1], experts))
    mean = gates[0] * dgates[0] + gates[1] * dgates[1]
    scale = 1.0 / gate_ref[:, 2:3]
    dprobs = jnp.where(chosen[0], (dgates[0] - mean) * scale, 0.0) + jnp.where(chosen[1], (dgates[1] - mean) * scale, 0.0)
    dlogits = (probs * (dprobs - jnp.sum(probs * dprobs, axis=-1, keepdims=True))).astype(bf16)
    small_ref[...] = jnp.zeros_like(small_ref)
    small_ref[:, 0:experts] = dot(xn_ref[...], dlogits, TN).astype(bf16)
    dxn = dxn + dot(dlogits, router_ref[...], NT)
    h = h_ref[...]
    r = lax.rsqrt(jnp.mean(h * h, axis=-1, keepdims=True) + epsilon)
    gain_row = jnp.sum(dxn * h * r, axis=0, keepdims=True)
    small_ref[:, experts:experts + 1] = column_of(gain_row).astype(bf16)
    scaled = dxn * gains_ref[1:2, :]
    dh = cot_ref[...].astype(f32) + r * scaled - h * (r * r * r) * jnp.mean(h * scaled, axis=-1, keepdims=True)
    dh_ref[...] = dh
    dhb_ref[...] = dh.astype(bf16)


def back(idx, cot, h, xn, probs, gate, router, gains, blocks, size, chunks, deps):
    count, width = h.shape
    experts = router.shape[1]
    outs = [sd((count, width), f32), sd((count, width), bf16), sd((width, 128), bf16)]
    return call(functools.partial(back_kernel, size, chunks), "back", outs, (idx, cot, h, xn, probs, gate, router, gains, *blocks),
                scratch=[pltpu.VMEM((experts * CAP, width), bf16)], deps=deps)


def mix_kernel(count, chunks, idx_ref, h_ref, gate_ref, *refs):
    blocks, out_ref, ys = refs[:count], refs[count], refs[count + 1]
    rows_of = blocks[0].shape[0]
    part = rows_of // chunks
    for k, block in enumerate(blocks):
        for c in range(chunks):
            ys[(c * count + k) * part:(c * count + k + 1) * part, :] = block[c * part:(c + 1) * part, :]
    out = h_ref[...]
    for j in (0, 1):
        out = out + gate_ref[:, j:j + 1] * dot(as_bf16(onehot(idx_ref[:, 4 * j + 1:4 * j + 2], rows_of * count)), ys[...])
    out_ref[...] = out.astype(bf16)


def mix(idx, h, gate, blocks, size, chunks, deps):
    count, width = h.shape
    return call(functools.partial(mix_kernel, len(blocks), chunks), "mix", [sd((count, width), bf16)], (idx, h, gate, *blocks),
                scratch=[pltpu.VMEM((len(blocks) * blocks[0].shape[0], width), bf16)], deps=deps)[0]


def last_kernel(tokens_ref, dh_ref, own, rx, ry, rd, gains_ref, out_ref):
    x = tokens_ref[...].astype(f32)
    r = lax.rsqrt(jnp.mean(x * x, axis=-1, keepdims=True) + epsilon)
    scaled = add_terms((own, rx, ry, rd)) * gains_ref[0:1, :]
    out_ref[...] = dh_ref[...] + r * scaled - x * (r * r * r) * jnp.mean(x * scaled, axis=-1, keepdims=True)


def merge_kernel(size, at_ref, keep_ref, got_ref, *outs):
    me = at_ref[0]
    for k in range(size):
        to = (me + k) & (size - 1)
        outs[k][...] = (keep_ref[to].astype(f32) + got_ref[to].astype(f32)).astype(bf16)


def total_kernel(size, at_ref, q_ref, k_ref, v_ref, *refs):
    blocks, out_ref, few_ref = refs[:size], refs[size], refs[size + 1]
    total = sum(b[...].astype(f32) for b in blocks)
    out_ref[...] = total
    half = total.shape[0]
    width = q_ref.shape[1]
    few = total[:, 4 * width:]
    lane = lax.broadcasted_iota(i32, few.shape, 1)
    for r in (0, 1):
        @pl.when(at_ref[1] == r)
        def _():
            product = sum(total[:, n * width:(n + 1) * width] * ref[r * half:(r + 1) * half, :].astype(f32) for n, ref in enumerate((q_ref, k_ref, v_ref)))
            few_ref[...] = jnp.where(lane == TABLE - 1, jnp.sum(product, axis=1, keepdims=True), few)


def finish_kernel(at_ref, mine_ref, other_ref, few_mine, few_other, gain_ref, q_ref, k_ref, v_ref, o_ref, router_ref, table_ref, ga_ref, gm_ref, few):
    half = mine_ref.shape[0]
    width = q_ref.shape[1]
    experts = router_ref.shape[0]
    rows = table_ref.shape[1]

    def put(first, second, few_first, few_second):
        for n, ref in enumerate((q_ref, k_ref, v_ref, o_ref)):
            ref[0:half, :] = first[:, n * width:(n + 1) * width]
            ref[half:, :] = second[:, n * width:(n + 1) * width]
        few[0:half, :] = few_first[...]
        few[half:, :] = few_second[...]
        table_ref[...] = first[:, 4 * width:].T[TABLE + 1:TABLE + 1 + table_ref.shape[0], 0:rows]

    pl.when(at_ref[1] == 0)(lambda: put(mine_ref, other_ref, few_mine, few_other))
    pl.when(at_ref[1] == 1)(lambda: put(other_ref, mine_ref, few_other, few_mine))
    turned = few[...].T
    router_ref[...] = turned[0:experts, :]
    ga_ref[...] = turned[TABLE - 1:TABLE, :] / gain_ref[...].astype(f32)
    gm_ref[...] = turned[TABLE - 2:TABLE - 1, :]


def on_device(size, tokens, segments, routes, capacity, cotangent, rel_table, w_query, w_key, w_value, w_attn_out, gain_attn, gain_moe, w_router, w_in, w_out):
    z = lax.axis_index("expert").astype(i32)
    rep = lax.axis_index("rep").astype(i32)
    pos = lax.axis_index("tensor").astype(i32)
    at = jnp.stack([z, rep, pos])
    tok = tokens[0]
    cot = cotangent[0]
    count, width = tok.shape
    local = w_in.shape[0]
    experts = w_router.shape[1]
    chunks = 2 if local >= 4 else 1
    part = local // chunks
    rows_dev = w_query.shape[0]
    half = rows_dev // 2
    buckets = rel_table.shape[0] * size
    part_rows = part * CAP
    half_rows = part_rows * size // 2
    matrix = order_matrix(size, part, part_rows, 0, 0)

    packed, rest = call(pack_kernel, "pack", [sd((half, 896), bf16)] * 2,
                        (at, w_query, w_key, w_value, w_router.T, w_attn_out, gain_attn, gain_moe, rel_table.T),
                        scratch=[pltpu.VMEM((rows_dev, 896), f32)], smem=1)
    pieces = gather_pieces(tok, count // 2)
    idx = call(functools.partial(prepare_kernel, size, chunks), "prepare", [sd((count, 8), i32)], (z[None], routes[0].T, capacity[None]),
               smem=1, deps=(packed,))[0]

    g_blocks = spread(idx, cot, 0, size, local * CAP, (), "spread_g", chunks)
    mine = [after(to_expert(packed, k, size), g_blocks[0]) for k in range(1, size)]
    other = [to_core(m) for m in mine]
    g_blocks = [g_blocks[0]] + [after(b, *mine) for b in g_blocks[1:]]
    g_arrived = shifted(g_blocks)
    qkv_w, wo, router, gains, table = unpack(at, [packed, *mine], [rest, *other], buckets, pieces[1:3])

    xn, qkv = project(at, pieces, qkv_w, gains, tuple(g_blocks[1:]))
    o, lse, *parts = attn_fwd(at, table, qkv, segments, wo, ())
    g_ordered = call(functools.partial(reorder_all_kernel, size), "order_g", [sd((local * CAP * size, width), bf16)], (matrix, *g_arrived), deps=(o,))[0]
    terms = scatter_direct(parts[0], after(parts[1], g_ordered), parts[2], parts[3])
    terms = (*terms[:2], after(terms[2], gains), after(terms[3], gains))
    h, xn2, probs, gate, *blocks = route(idx, tok, terms, router, gains, size, chunks, ())
    g_pieces = gather_pieces(after(g_ordered, xn2), half_rows * chunks)

    arrived = shifted(blocks)
    ordered = [reorder(order_matrix(size, part, part_rows + 16, 16, 16), arrived, "order")]
    got = [gather_pieces(ordered[0], half_rows)]
    if chunks == 2:
        blocks = spread(idx, xn2, 1, size, part_rows, (ordered[0], *g_pieces[1:3]), "spread", 1)
        ordered.append(reorder(matrix, shifted(blocks), "order"))
        got.append(gather_direct(ordered[1]))
    extras = (*got[0][:3], got[0][4])
    ready = ordered[1:]

    step = max(part // 4, 1)
    pending = [(c, start) for c in range(chunks) for start in range(0, part, step)]
    grads = ()

    def expert_grads(many, *ready):
        nonlocal grads
        mark = ready[0]
        for c, start in pending[:many]:
            *grads, mark = expert_grad(at, c * part, start, step, local, acts[c], other_acts[c], grads, ready)
        del pending[:many]
        return mark

    acts, sums, ys = [], [], []
    dg_full = jnp.zeros((4, lanes_of(size) // 128, 16, 128), f32)
    for c in range(chunks):
        *outs, dg_full, act = moe(at, size, chunks, c, got[c], extras, g_pieces, w_in, w_out, dg_full, () if c else ready)
        sums.append(scatter_direct(*outs[:4]) if c < chunks - 1 else outs[:4])
        ys.append(outs[4:])
        acts.append(act)
    other_acts = [to_core(acts[0])]


    def give(c, extra, deps):
        given = call(functools.partial(give_back_kernel, size, extra), "give_back", [sd((part_rows + 16 * extra, width), bf16)] * size,
                     (matrix, *sums[c]), deps=deps)
        return given[0], [given[0]] + [to_expert(given[k], size - k, size) for k in range(1, size)]

    outs = list(sums[-1])
    if chunks == 2:
        outs = [*outs[:1], *[after(piece, *sums[0][1:]) for piece in outs[1:4]]]
    sums[-1] = scatter_direct(*outs)
    back_blocks = []
    mark = outs[0]
    if chunks == 2:
        mark, back_blocks = give(0, False, (mark,))
    mark = expert_grads(1, mark)
    mark = expert_grads(1, mark, *back_blocks[1:])
    ready, blocks = give(chunks - 1, True, (mark,))
    if chunks == 2:
        y_packs = [after(ys[c][1], mark, *sums[-1][1:]) for c in (0, 1)]
        y_got = [to_tensor(pack, flip) for flip, pack in zip((1, 2), y_packs)]
    else:
        y_terms = scatter_direct(*ys[0])
    ready = (expert_grads(1, ready), *y_packs) if chunks == 2 else (ready,)
    dh, dhb, small = back(idx, cot, h, xn2, probs, gate, router, gains, back_blocks + blocks, size, chunks, ready)
    dh_pieces = gather_direct(dhb)
    mark = expert_grads(1, dhb)
    if chunks == 2:
        acts[1] = after(acts[1], mark)
        other_acts.append(to_core(acts[1]))
    if chunks == 2:
        y_parts, sent = scatter_end(*y_got, ys[1][2], ys[0][2], (mark,))
        mark = sent[0]

    y_late = (y_parts[1], y_parts[3]) if chunks == 2 else ()
    gtab, dqkv = attn_bwd(at, size, table, dh_pieces, segments, wo, qkv, lse, (mark,))
    keep, send, own, *parts = attn_grad(at, size, dqkv, qkv_w, xn, dh_pieces, o, small, gtab, y_late)
    terms = scatter_direct(own, *parts)
    got = to_core(send)
    out_blocks = call(functools.partial(merge_kernel, size), "merge", [sd((half, packed.shape[1]), bf16)] * size,
                      (at, keep, got), smem=1, deps=other_acts[1:])
    outs = [sd((local * CAP, width), bf16)] * size
    if chunks == 2:
        given = call(functools.partial(give_back_halves_kernel, size), "give_back_y", outs, (matrix, ys[0][0], ys[1][0], *y_parts), deps=(out_blocks[0],))
    else:
        given = call(functools.partial(give_back_kernel, size, False), "give_back_y", outs, (matrix, *y_terms), deps=(out_blocks[0],))
    y_blocks = [given[0]] + [to_expert(given[k], size - k, size) for k in range(1, size)]
    grad_tokens = call(last_kernel, "last", [sd((count, width), f32)], (tok, dh, *terms, gains))[0]
    mark = expert_grads(1, out_blocks[0], given[0])
    mark = expert_grads(max(len(pending) - 2, 0), mark, *terms[1:])
    total, gain = call(functools.partial(total_kernel, size), "total", [sd(out_blocks[0].shape, f32), sd((half, 128), f32)],
                       (at, w_query, w_key, w_value, *shifted(out_blocks)), smem=1, deps=(mark, *terms[1:]))
    mark = expert_grads(1, total)
    gain = gain + to_tensor(gain, 1)
    mark = expert_grads(len(pending), mark, gain)
    gain = gain + to_tensor(gain, 2)
    output = mix(idx, h, gate, y_blocks, size, chunks, (mark,))
    lw = w_query.shape[1]
    outs = [sd((rows_dev, lw), f32)] * 4 + [sd((experts, rows_dev), f32), sd(rel_table.T.shape, f32)] + [sd((1, rows_dev), f32)] * 2
    grad_q, grad_k, grad_v, grad_o, grad_router, grad_table, grad_ga, grad_gm = call(
        finish_kernel, "finish", outs, (at, total, to_core(total), gain, to_core(gain), gain_attn[None]), smem=1, scratch=[pltpu.VMEM((rows_dev, 128), f32)], deps=(output, mark))
    return (output[None], grad_tokens[None], grad_table.T, grad_q, grad_k, grad_v, grad_o, grad_ga[0], grad_gm[0], grad_router.T, *grads)


def solution(mesh):
    by_token = P(("expert", "rep"), "tensor", None)
    both = P("expert", "tensor")
    return jax.shard_map(
        functools.partial(on_device, mesh.shape["expert"]),
        mesh=mesh,
        in_specs=(by_token, P(("expert", "rep"), None), by_token, P(), by_token, both, both, both, both, both, P("expert"), P("expert"),
                  P("expert", None), P("expert", None, "tensor"), P("expert", "tensor", None)),
        out_specs=(by_token, by_token, both, both, both, both, both, P("expert"), P("expert"), P("expert", None),
                   P("expert", None, "tensor"), P("expert", "tensor", None)),
        check_vma=False,
    )
```

```python
import functools
import math

import jax
import jax.numpy as jnp
from jax import lax
from jax.experimental import pallas as pl
from jax.experimental.pallas import tpu as pltpu
from jax.sharding import PartitionSpec as P

HEAD = 64
CAP = 12
QB = 128
TABLE = 66
epsilon = 1e-06
masked_value = -1e30
thresholds = (16, 19, 21, 24, 27, 31, 35, 40, 46, 52, 59, 67, 77, 87, 99, 113)
lowest = tuple(range(16)) + thresholds
f32 = jnp.float32
bf16 = jnp.bfloat16
i32 = jnp.int32
NN = (((1,), (0,)), ((), ()))
NT = (((1,), (1,)), ((), ()))
TN = (((0,), (0,)), ((), ()))
VM = pl.BlockSpec(memory_space=pltpu.VMEM)
SM = pl.BlockSpec(memory_space=pltpu.SMEM)
sd = jax.ShapeDtypeStruct


def dot(a, b, dims=NN):
    return lax.dot_general(a, b, dims, preferred_element_type=f32)


ANY = pl.BlockSpec(memory_space=pl.ANY)
TIMES = {"attn_fwd": 13, "attn_bwd": 400, "attn_grad": 9, "project": 5, "moe": 400, "expert_grad": 1, "back": 5, "route": 4}


def cost(name):
    return pl.CostEstimate(flops=int(TIMES.get(name, 0.5) * 1_150_000_000), bytes_accessed=1000, transcendentals=0)


def call(kernel, name, outs, operands, scratch=(), smem=0, flops=0, moved=4_000_000, deps=()):
    given = len(operands)

    def body(*refs):
        kernel(*refs[:given], *refs[given + len(deps):])

    return pl.pallas_call(
        body,
        out_shape=tuple(outs),
        in_specs=[SM] * smem + [VM] * (given - smem) + [ANY] * len(deps),
        out_specs=tuple(VM for _ in outs),
        scratch_shapes=list(scratch),
        compiler_params=pltpu.CompilerParams(vmem_limit_bytes=56 << 20),
        cost_estimate=cost(name),
        name=name,
    )(*operands, *deps)


def after(value, *deps):
    return pl.pallas_call(
        lambda *refs: None,
        out_shape=sd(value.shape, value.dtype),
        in_specs=[ANY] * (1 + len(deps)),
        out_specs=ANY,
        input_output_aliases={0: 0},
        name="after",
    )(value, *deps)


def to_tensor(a, flip):
    return lax.ppermute(a, "tensor", [(i, i ^ flip) for i in range(4)])


def to_expert(a, shift, size):
    return lax.ppermute(a, "expert", [(i, (i + shift) % size) for i in range(size)])


def to_core(a):
    return lax.ppermute(a, "rep", [(0, 1), (1, 0)])


def shifted(blocks):
    size = len(blocks)
    return [blocks[0]] + [to_expert(blocks[k], k, size) for k in range(1, size)]


def gather_pieces(own, half):
    px = to_tensor(own, 1)
    py = to_tensor(own, 2)
    d0 = to_tensor(px[:half], 2)
    d1 = to_tensor(py[half:], 1)
    return own, px, py, d0, d1


def gather_direct(own):
    return (own, *[to_tensor(own, flip) for flip in (1, 2, 3)])


def late_kernel(x_late, y_late, got_x, got_y, sum_x, sum_y):
    sum_x[...] = (x_late[...].astype(f32) + got_y[0].astype(f32)).astype(bf16)
    sum_y[...] = (y_late[...].astype(f32) + got_x[0].astype(f32)).astype(bf16)


def scatter_end(got_x, got_y, x_late, y_late, deps):
    shape = sd(x_late.shape, bf16)
    sent = call(late_kernel, "late", [shape, shape], (x_late, y_late, got_x, got_y), deps=deps)
    return (got_x, to_tensor(sent[1], 2), got_y, to_tensor(sent[0], 1)), sent


def scatter_direct(own, *pieces):
    return (own, *[to_tensor(piece, flip) for flip, piece in zip((1, 2, 3), pieces)])


def add_terms(refs):
    return sum(r[...].astype(f32) for r in refs)


def onehot(index, width):
    return lax.broadcasted_iota(i32, (index.shape[0], width), 1) == index


def as_bf16(mask):
    return jnp.where(mask, 1.0, 0.0).astype(bf16)


def prepare_kernel(size, chunks, me_ref, routes_ref, capacity_ref, idx_ref):
    count = routes_ref.shape[1]
    experts = capacity_ref.shape[1]
    local = experts // size
    part = local // chunks
    me = me_ref[0]
    first, second = (jnp.broadcast_to(routes_ref[j:j + 1, :], (8, count)).T[:, 0:1] for j in (0, 1))
    both = as_bf16(onehot(first, experts)) + as_bf16(onehot(second, experts))
    rows = lax.broadcasted_iota(i32, (count, count), 0)
    cols = lax.broadcasted_iota(i32, (count, count), 1)
    before = dot(as_bf16(cols < rows), both)
    capacity = capacity_ref[...].astype(f32)
    shift = int(math.log2(local))
    columns = []
    for route in (first, second):
        mine = onehot(route, experts)
        position = jnp.sum(jnp.where(mine, before, 0.0), axis=1, keepdims=True)
        limit = jnp.sum(jnp.where(mine, jnp.broadcast_to(capacity, mine.shape), 0.0), axis=1, keepdims=True)
        keep = position < limit
        position = position.astype(i32)
        owner = lax.shift_right_logical(route, jnp.full_like(route, shift))
        inner = route & (local - 1)
        away = (owner - me + size) & (size - 1)
        chunk = lax.shift_right_logical(inner, jnp.full_like(route, int(math.log2(part))))
        slot = ((chunk * size + away) * part + (inner & (part - 1))) * CAP + position
        columns += [route, jnp.where(keep, slot, -1), jnp.where(keep, away * local + inner, -1), away * CAP + position]
    for n, column in enumerate(columns):
        idx_ref[:, n:n + 1] = column


def spread_kernel(first, chunks, idx_ref, rows_ref, *outs):
    count = len(outs)
    block = outs[0].shape[0] // chunks
    width = block * chunks * count
    spread = as_bf16(onehot(idx_ref[:, 1:2] - first, width)) + as_bf16(onehot(idx_ref[:, 5:6] - first, width))
    slots = dot(spread, rows_ref[...], TN).astype(bf16)
    for c in range(chunks):
        for k, ref in enumerate(outs):
            ref[c * block:(c + 1) * block, :] = slots[(c * count + k) * block:(c * count + k + 1) * block]


def spread(idx, rows, chunk, count, block, deps, name, chunks):
    return call(functools.partial(spread_kernel, chunk * count * block, chunks), name, [sd((block, rows.shape[1]), bf16)] * count, (idx, rows), deps=deps)


def order_matrix(size, part, block, extra, out_extra):
    rows = part * size * CAP
    m = [[0.0] * (size * block) for _ in range(rows + out_extra)]
    for e in range(part):
        for k in range(size):
            for c in range(CAP):
                m[(e * size + k) * CAP + c][k * block + e * CAP + c] = 1.0
    for r in range(extra):
        for k in range(size):
            m[rows + r][k * block + part * CAP + r] = 1.0
    return jnp.array(m, dtype=bf16)


def reorder_kernel(count, m_ref, *refs):
    blocks, out_ref = refs[:count], refs[count]
    out_ref[...] = dot(m_ref[...], jnp.concatenate([b[...] for b in blocks], axis=0)).astype(bf16)


def reorder_all_kernel(count, m_ref, *refs):
    blocks, out_ref = refs[:count], refs[count]
    block = m_ref.shape[1] // count
    rows = m_ref.shape[0]
    for c in range(out_ref.shape[0] // rows):
        chosen = jnp.concatenate([b[c * block:(c + 1) * block, :] for b in blocks], axis=0)
        out_ref[c * rows:(c + 1) * rows, :] = dot(m_ref[...], chosen).astype(bf16)


def reorder(matrix, blocks, name, deps=()):
    rows = matrix.shape[0]
    width = blocks[0].shape[1]
    return call(functools.partial(reorder_kernel, len(blocks)), name, [sd((rows, width), bf16)], (matrix, *blocks),
                flops=2 * matrix.size * width, moved=2 * rows * width * 2, deps=deps)[0]


def give_back_kernel(count, extra, m_ref, *refs):
    outs = refs[4:]
    total = add_terms(refs[:4]).astype(bf16)
    rows = m_ref.shape[0]
    back = dot(m_ref[...], total[0:rows], TN).astype(bf16)
    block = back.shape[0] // count
    for k in range(count):
        outs[k][0:block, :] = back[k * block:(k + 1) * block]
        if extra:
            outs[k][block:, :] = total[rows:]


def give_back_halves_kernel(count, m_ref, own_a, own_b, got_x, late_y, got_y, late_x, *outs):
    halves = (own_a[...].astype(f32) + got_x[1].astype(f32) + late_y[...].astype(f32), own_b[...].astype(f32) + got_y[1].astype(f32) + late_x[...].astype(f32))
    for n, total in enumerate(halves):
        back = dot(m_ref[...], total.astype(bf16), TN).astype(bf16)
        block = back.shape[0] // count
        for k in range(count):
            outs[k][n * block:(n + 1) * block, :] = back[k * block:(k + 1) * block]


def pack_kernel(at_ref, q_ref, k_ref, v_ref, r_ref, o_ref, ga_ref, gm_ref, t_ref, out_ref, rest_ref, full):
    rows, width = q_ref.shape
    full[...] = jnp.zeros_like(full)
    place = 0
    for ref in (q_ref, k_ref, v_ref, r_ref, o_ref):
        value = ref[...].astype(f32)
        value = value.T if ref is r_ref else value
        full[:, place:place + value.shape[1]] = value
        place += value.shape[1]
    for ref in (ga_ref, gm_ref):
        full[:, place:place + 1] = column_of(ref[...].astype(f32)[None, :])
        place += 1
    full[0:t_ref.shape[1], place:place + t_ref.shape[0]] = t_ref[...].astype(f32).T
    half = rows // 2
    for r in (0, 1):
        @pl.when(at_ref[1] == r)
        def _():
            out_ref[...] = full[r * half:(r + 1) * half, :].astype(bf16)
            rest_ref[...] = full[(1 - r) * half:(2 - r) * half, :].astype(bf16)


def unpack_kernel(size, at_ref, *refs):
    mine, other = refs[:size], refs[size:2 * size]
    full, qkv_ref, wo_ref, router_ref, gains_ref, table_ref = refs[2 * size:]
    me, rep = at_ref[0], at_ref[1]
    half = mine[0].shape[0]
    for k in range(size):
        z = (me - k + size) & (size - 1)
        full[2 * z + rep] = mine[k][...].astype(f32)
        full[2 * z + 1 - rep] = other[k][...].astype(f32)
    full = jnp.concatenate([full[n] for n in range(2 * size)], axis=0)
    qkv_ref[...] = full[:, 0:576].astype(bf16)
    router_ref[...] = full[:, 576:640].astype(bf16)
    wo_ref[...] = full[:, 640:832].astype(bf16)
    tail = full[:, 768:896]
    turned = tail.T
    gains_ref[...] = turned[64:72, :]
    rows = table_ref.shape[0] // size
    for z in range(size):
        table_ref[z * rows:(z + 1) * rows, :] = tail[z * 2 * half: z * 2 * half + rows, :]


def unpack(at, mine, other, buckets, deps):
    size = len(mine)
    half, cols = mine[0].shape
    width = 2 * half * size

    def kernel(at_ref, *refs):
        unpack_kernel(size, at_ref, *refs[:2 * size], refs[-1], *refs[2 * size:-1])

    outs = [sd((width, 576), bf16), sd((width, 192), bf16), sd((width, 64), bf16), sd((8, width), f32), sd((buckets, 128), f32)]
    return call(kernel, "unpack", outs, (at, *mine, *other), scratch=[pltpu.VMEM((2 * size, half, cols), f32)], smem=1, deps=deps)


def piece_shapes(rows, width):
    return [sd((rows, width), bf16)] * 4


def near_offset():
    rows = lax.broadcasted_iota(jnp.int32, (QB, 2 * QB), 0)
    cols = lax.broadcasted_iota(jnp.int32, (QB, 2 * QB), 1)
    return QB + rows - cols


def near_bias(table_ref, head, buckets):
    off = near_offset()
    bias = jnp.where(off < 0, masked_value, table_ref[0, TABLE + head])
    for b in range(1, buckets):
        bias = jnp.where(off >= lowest[b], table_ref[b, TABLE + head], bias)
    return bias


def scores_of(q, k_ref, head, i, near, far, seg_col, seg_row_ref):
    lo = max(i - 1, 0) * QB
    hi = (i + 1) * QB
    s = dot(q, k_ref[head, 0:hi], NT)
    bias = near[:, QB:] if i == 0 else near
    same_near = seg_col == seg_row_ref[:, lo:hi]
    s_near = jnp.where(same_near, s[:, lo:hi] + bias, masked_value)
    if lo == 0:
        return s_near
    same_far = seg_col == seg_row_ref[:, 0:lo]
    s_far = jnp.where(same_far, s[:, 0:lo] + far, masked_value)
    return jnp.concatenate([s_far, s_near], axis=1)


def project_kernel(at_ref, own_ref, px_ref, py_ref, pd0_ref, pd1_ref, w_ref, gain_ref, xn_ref, qkv_ref):
    pos = at_ref[2]
    tok = own_ref.shape[0]
    half = tok // 2
    gain = gain_ref[0:1, :]

    def put(rows, flip, start=0):
        x = rows.astype(f32)
        r = lax.rsqrt(jnp.mean(x * x, axis=-1, keepdims=True) + epsilon)
        xn = (x * r * gain).astype(bf16)
        at = pl.ds(pl.multiple_of((pos ^ flip) * tok + start, half), rows.shape[0])
        xn_ref[at, :] = xn
        qkv_ref[at, :] = dot(xn, w_ref[...]).astype(bf16)

    put(own_ref[...], 0)
    put(px_ref[...], 1)
    put(py_ref[...], 2)
    put(pd0_ref[...], 3)
    put(pd1_ref[...], 3, half)


def column_of(row):
    return jnp.broadcast_to(row, (8, row.shape[1])).T[:, 0:1]


def attn_fwd_kernel(heads, at_ref, table_ref, qkv_ref, segr_ref, wo_ref, o_ref, lse_ref, out_own, out_x, out_y, out_d, qs, ks, vs, seg):
    pos = at_ref[2]
    tok = out_own.shape[0]
    half = tok // 2
    buckets = table_ref.shape[0]
    seg[...] = column_of(segr_ref[...])

    def at(flip, start=0, size=tok):
        return pl.ds(pl.multiple_of((pos ^ flip) * tok + start, half), size)

    width = heads * HEAD
    qkv = qkv_ref[...]
    for h in range(heads):
        qs[h] = qkv[:, h * HEAD:(h + 1) * HEAD] * bf16(0.125)
        ks[h] = qkv[:, width + h * HEAD: width + (h + 1) * HEAD]
        vs[h] = qkv[:, 2 * width + h * HEAD: 2 * width + (h + 1) * HEAD]
    blocks = qkv_ref.shape[0] // QB
    for h in range(heads):
        near = near_bias(table_ref, h, buckets)
        far = table_ref[buckets - 1, TABLE + h]
        for i in range(blocks):
            rows = slice(i * QB, (i + 1) * QB)
            s = scores_of(qs[h, rows], ks, h, i, near, far, seg[rows, :], segr_ref)
            top = jnp.max(s, axis=-1, keepdims=True)
            e = jnp.exp(s - top)
            total = jnp.sum(e, axis=-1, keepdims=True)
            p = (e * (1.0 / total)).astype(bf16)
            o_ref[rows, h * HEAD:(h + 1) * HEAD] = dot(p, vs[h, 0:(i + 1) * QB]).astype(bf16)
            lse_ref[rows, h:h + 1] = top + jnp.log(total)
    wo = wo_ref[...]
    for flip, ref in enumerate((out_own, out_x, out_y, out_d)):
        ref[...] = dot(o_ref[at(flip), :], wo, NT).astype(bf16)


def attn_bwd_kernel(heads, size, at_ref, table_ref, own_ref, px_ref, py_ref, pd_ref, segr_ref, wo_ref, qkv_ref, lse_ref,
                    gtab_ref, dqkv, dh, qs, ks, vs, do, dk, dv, acc, seg):
    pos = at_ref[2]
    tok = own_ref.shape[0]
    half = tok // 2
    buckets = table_ref.shape[0]
    width = heads * HEAD

    def at(flip, start=0, size=tok):
        return pl.ds(pl.multiple_of((pos ^ flip) * tok + start, half), size)

    seg[...] = column_of(segr_ref[...])
    dh[at(0), :] = own_ref[...]
    dh[at(1), :] = px_ref[...]
    dh[at(2), :] = py_ref[...]
    dh[at(3), :] = pd_ref[...]
    dall = dot(dh[...], wo_ref[...]).astype(bf16)
    for h in range(heads):
        do[h] = dall[:, h * HEAD:(h + 1) * HEAD]
        qs[h] = qkv_ref[:, h * HEAD:(h + 1) * HEAD] * bf16(0.125)
        ks[h] = qkv_ref[:, width + h * HEAD: width + (h + 1) * HEAD]
        vs[h] = qkv_ref[:, 2 * width + h * HEAD: 2 * width + (h + 1) * HEAD]
    blocks = qkv_ref.shape[0] // QB
    off = near_offset()
    per = gtab_ref.shape[1]
    gtab_ref[...] = jnp.zeros_like(gtab_ref)
    for h in range(heads):
        near = near_bias(table_ref, h, buckets)
        far = table_ref[buckets - 1, TABLE + h]
        acc[...] = jnp.zeros_like(acc)
        dk[...] = jnp.zeros_like(dk)
        dv[...] = jnp.zeros_like(dv)
        far_sum = jnp.zeros((QB, 1), f32)
        for i in range(blocks):
            rows = slice(i * QB, (i + 1) * QB)
            lo = max(i - 1, 0) * QB
            hi = (i + 1) * QB
            q = qs[h, rows]
            s = scores_of(q, ks, h, i, near, far, seg[rows, :], segr_ref)
            p = jnp.exp(s - lse_ref[rows, h:h + 1])
            g = do[h, rows]
            dv[0:hi] += dot(p.astype(bf16), g, TN)
            dp = dot(g, vs[h, 0:hi], NT)
            pd = p * dp
            ds = (pd - p * jnp.sum(pd, axis=-1, keepdims=True)).astype(bf16)
            dq = dot(ds, ks[h, 0:hi]) * 0.125
            dqkv[rows, h * HEAD:(h + 1) * HEAD] = dq.astype(bf16)
            dk[0:hi] += dot(ds, q, TN)
            dsf = ds.astype(f32)
            if i == 0:
                acc[:, QB:] += dsf
            else:
                acc[...] += dsf[:, lo:hi]
            if lo > 0:
                far_sum = far_sum + jnp.sum(dsf[:, 0:lo], axis=-1, keepdims=True)
        dqkv[:, width + h * HEAD: width + (h + 1) * HEAD] = dk[...].astype(bf16)
        dqkv[:, 2 * width + h * HEAD: 2 * width + (h + 1) * HEAD] = dv[...].astype(bf16)
        total = acc[...]
        rest = jnp.sum(far_sum, axis=0, keepdims=True)
        for b in range(buckets):
            if b == buckets - 1:
                inside = off >= lowest[b]
            else:
                inside = (off >= lowest[b]) & (off < lowest[b + 1])
            part = jnp.sum(jnp.where(inside, total, 0.0), axis=0, keepdims=True)
            one = jnp.sum(part, axis=1, keepdims=True)
            gtab_ref[b // per, b % per:b % per + 1, TABLE + 1 + h:TABLE + 2 + h] = one + rest if b == buckets - 1 else one


def attn_grad_kernel(size, at_ref, dqkv, w_ref, xn_ref, own_ref, px_ref, py_ref, pd_ref, o_ref, small_ref, gtab_ref, keep_ref, send_ref,
                     out_own, out_x, out_y, out_d, dh, full):
    pos, rep = at_ref[2], at_ref[1]
    tok = out_own.shape[0]
    half = tok // 2
    width = o_ref.shape[1]

    def at(flip, start=0, size=tok):
        return pl.ds(pl.multiple_of((pos ^ flip) * tok + start, half), size)

    dh[at(0), :] = own_ref[...]
    dh[at(1), :] = px_ref[...]
    dh[at(2), :] = py_ref[...]
    dh[at(3), :] = pd_ref[...]
    w = w_ref[...]
    for flip, ref in enumerate((out_own, out_x, out_y, out_d)):
        ref[...] = dot(dqkv[at(flip), :], w, NT).astype(bf16)
    grad = dot(xn_ref[...], dqkv[...], TN)
    grad_out = dot(dh[...], o_ref[...], TN)
    part_rows = keep_ref.shape[1]
    for n in range(2 * size):
        full[n, :, 0:3 * width] = grad[n * part_rows:(n + 1) * part_rows].astype(bf16)
        full[n, :, 3 * width:4 * width] = grad_out[n * part_rows:(n + 1) * part_rows].astype(bf16)
        few = small_ref[n * part_rows:(n + 1) * part_rows, :]
        full[n, :, 4 * width:] = few
        if n % 2 == 0:
            rows = gtab_ref.shape[1]
            full[n, 0:rows, 4 * width:] = (few[0:rows].astype(f32) + gtab_ref[n // 2]).astype(bf16)
    for z in range(size):
        keep_ref[z] = full[2 * z + rep]
        send_ref[z] = full[2 * z + 1 - rep]


def project(at, pieces, w, gains, deps):
    tok, width = pieces[0].shape
    return call(project_kernel, "project", [sd((4 * tok, width), bf16), sd((4 * tok, w.shape[1]), bf16)], (at, *pieces, w, gains),
                smem=1, deps=deps)


def attn_fwd(at, table, qkv, segr, wo, deps):
    width = wo.shape[0]
    length = qkv.shape[0]
    heads = wo.shape[1] // HEAD
    outs = [sd((length, heads * HEAD), bf16), sd((length, heads), f32)]
    return call(functools.partial(attn_fwd_kernel, heads), "attn_fwd", outs + piece_shapes(length // 4, width),
                (at, table, qkv, segr, wo),
                scratch=[pltpu.VMEM((heads, length, HEAD), bf16)] * 3 + [pltpu.VMEM((length, 1), i32)], smem=2,
                flops=8_000_000_000, moved=5_000_000, deps=deps)


def attn_bwd(at, size, table, pieces, segr, wo, qkv, lse, deps):
    tok, width = pieces[0].shape
    length = qkv.shape[0]
    heads = wo.shape[1] // HEAD
    outs = [sd((size, table.shape[0] // size, 128), f32), sd(qkv.shape, bf16)]
    scratch = [pltpu.VMEM((length, width), bf16)] + [pltpu.VMEM((heads, length, HEAD), bf16)] * 4 + [pltpu.VMEM((length, HEAD), f32)] * 2
    scratch += [pltpu.VMEM((QB, 2 * QB), f32), pltpu.VMEM((length, 1), i32)]
    return call(functools.partial(attn_bwd_kernel, heads, size), "attn_bwd", outs, (at, table, *pieces, segr, wo, qkv, lse),
                scratch=scratch, smem=2, flops=12_000_000_000, moved=8_000_000, deps=deps)


def attn_grad(at, size, dqkv, w, xn, pieces, o, small, gtab, deps):
    tok, width = pieces[0].shape
    cols = w.shape[1] + o.shape[1] + small.shape[1]
    rows = width // (2 * size)
    outs = [sd((size, rows, cols), bf16)] * 2 + piece_shapes(tok, width)
    return call(functools.partial(attn_grad_kernel, size), "attn_grad", outs, (at, dqkv, w, xn, *pieces, o, small, gtab),
                scratch=[pltpu.VMEM((4 * tok, width), bf16), pltpu.VMEM((2 * size, rows, cols), bf16)], smem=1,
                flops=4_000_000_000, moved=9_000_000, deps=deps)


def route_kernel(size, chunks, idx_ref, tokens_ref, own, rx, ry, rd, router_ref, gains_ref, h_ref, xn_ref, probs_ref, gate_ref, *blocks):
    count, width = tokens_ref.shape
    experts = router_ref.shape[1]
    local = experts // size
    rows_of = local // chunks * CAP
    lanes = lanes_of(size)
    h = tokens_ref[...].astype(f32) + add_terms((own, rx, ry, rd))
    r = lax.rsqrt(jnp.mean(h * h, axis=-1, keepdims=True) + epsilon)
    xn = (h * r * gains_ref[1:2, :]).astype(bf16)
    h_ref[...] = h
    xn_ref[...] = xn
    logits = dot(xn, router_ref[...])
    e = jnp.exp(logits - jnp.max(logits, axis=-1, keepdims=True))
    probs = e / jnp.sum(e, axis=-1, keepdims=True)
    probs_ref[...] = probs
    picked = [jnp.sum(jnp.where(onehot(idx_ref[:, 4 * j:4 * j + 1], experts), probs, 0.0), axis=-1, keepdims=True) for j in (0, 1)]
    total = picked[0] + picked[1]
    gates = [p / total for p in picked]
    gate_ref[:, 0:1], gate_ref[:, 1:2], gate_ref[:, 2:3] = gates[0], gates[1], total
    spread = as_bf16(onehot(idx_ref[:, 1:2], size * rows_of)) + as_bf16(onehot(idx_ref[:, 5:6], size * rows_of))
    slots = dot(spread, xn, TN).astype(bf16)
    held = jnp.zeros((experts, lanes), f32)
    for j in (0, 1):
        to = as_bf16(onehot(idx_ref[:, 4 * j + 2:4 * j + 3], experts))
        at = jnp.where(onehot(idx_ref[:, 4 * j + 3:4 * j + 4], lanes), gates[j], 0.0).astype(bf16)
        held = held + dot(to, at, TN)
    for k, ref in enumerate(blocks):
        ref[0:rows_of, :] = slots[k * rows_of:(k + 1) * rows_of]
        ref[rows_of:, :] = jnp.zeros((16, width), bf16)
        ref[rows_of:rows_of + local, 0:lanes] = held[k * local:(k + 1) * local].astype(bf16)


def lanes_of(size):
    return -(-size * CAP // 128) * 128


def route(idx, tokens, parts, router, gains, size, chunks, deps):
    count, width = tokens.shape
    experts = router.shape[1]
    rows_of = experts // size // chunks * CAP
    outs = [sd((count, width), f32), sd((count, width), bf16), sd((count, experts), f32), sd((count, 8), f32)]
    outs += [sd((rows_of + 16, width), bf16)] * size
    return call(functools.partial(route_kernel, size, chunks), "route", outs, (idx, tokens, *parts, router, gains),
                flops=400_000_000, moved=5_000_000, deps=deps)


def moe_kernel(rows, part, offset, last, skip, at_ref, own, px, py, d0, d1, e_own, e_px, e_py, e_d, g_own, g_px, g_py, g_far, win_ref, wout_ref,
               dg_in, *refs):
    outs, y_outs, dg_ref, acts = refs[skip:skip + 4], refs[skip + 4:-2], refs[-2], refs[-1]
    e, j = pl.program_id(0), pl.program_id(1)
    steps = pl.num_programs(1)

    @pl.when((e == 0) & (j == 0))
    def _():
        dg_ref[...] = dg_in[...]

    wide = e_own.shape[1]
    pick = lax.broadcasted_iota(i32, (16, wide), 0) == e + offset
    square = lax.broadcasted_iota(i32, (rows, wide), 0) + j * rows == lax.broadcasted_iota(i32, (rows, wide), 1)

    def gate_of(ref):
        row = jnp.sum(jnp.where(pick, ref[...].astype(f32), 0.0), axis=0, keepdims=True)
        return jnp.sum(jnp.where(square, jnp.broadcast_to(row, square.shape), 0.0), axis=1, keepdims=True)

    def keep(n, value):
        for flip in range(4):
            acts[n, 0, flip] = value[flip * rows:(flip + 1) * rows]

    def put(value, outs):
        at = pl.ds(pl.multiple_of((e * steps + j) * rows, 16), rows)
        for flip, ref in enumerate(outs):
            ref[at, :] = value[flip * rows:(flip + 1) * rows]

    gate = jnp.concatenate([gate_of(r) for r in (e_own, e_px, e_py, e_d)], axis=0)
    far = jnp.where(e < part // 2, d0[...].astype(f32), d1[...].astype(f32)).astype(bf16)
    s = jnp.concatenate([own[...], px[...], py[...], far], axis=0)
    g = jnp.concatenate([g_own[...], g_px[...], g_py[...], g_far[...]], axis=0).astype(f32)
    keep(0, s)
    win, wout = win_ref[0], wout_ref[0]
    dy = (g * gate).astype(bf16)
    keep(1, dy)
    a = dot(s, win)
    dhid = dot(dy, wout, NT)
    c = math.sqrt(2.0 / math.pi)
    t = jnp.tanh(a * (c + (c * 0.044715) * (a * a)))
    up = 0.5 + 0.5 * t
    hid = (a * up).astype(bf16)
    slope = up + (0.5 * a) * (1.0 - t * t) * (c + (3 * c * 0.044715) * (a * a))
    da = (dhid * slope).astype(bf16)
    keep(2, hid)
    keep(3, da)
    put(dot(da, win, NT).astype(bf16), outs)
    y = dot(hid, wout)
    ones = jnp.ones((8, y.shape[1]), bf16)
    sums = dot(ones, (y * g).astype(bf16), NT)
    if len(y_outs) == 4:
        put(y.astype(bf16), y_outs)
    else:
        near = 1 if offset == 0 else 2
        own_ref, pack, once = y_outs
        put(y.astype(bf16), [own_ref] + ([pack.at[1], once] if near == 1 else [once, pack.at[1]]) + [pack.at[0]])
    for flip in range(4):
        row = sums[0:1, flip * rows:(flip + 1) * rows]
        dg_ref[flip, j, pl.ds(e + offset, 1), 0:rows] = row

    if last:
        @pl.when((e == part - 1) & (j == steps - 1))
        def _():
            for flip, ref in enumerate(outs):
                ref[-16:, :] = jnp.zeros((16, ref.shape[1]), bf16)
                for n in range(wide // 128):
                    ref[-16:, n * 128:(n + 1) * 128] = dg_ref[flip, n].astype(bf16)


def moe(at, size, chunks, chunk, pieces, extras, g, w_in, w_out, dg, deps):
    all_rows = size * CAP
    rows = 128 if all_rows % 128 == 0 else all_rows
    steps = all_rows // rows
    local, width, hidden = w_in.shape
    part = local // chunks
    lanes = -(-all_rows // 128) * 128
    first = chunk * part
    whole = lambda e, j: (e * steps + j, 0)
    flat = pl.BlockSpec((rows, width), whole)
    of_all = pl.BlockSpec((rows, width), lambda e, j: ((first + e) * steps + j, 0))
    half = part // 2
    low = pl.BlockSpec((rows, width), lambda e, j: (jnp.where(e < half, e * steps + j, half * steps - 1), 0))
    high = pl.BlockSpec((rows, width), lambda e, j: (jnp.where(e < half, 0, (e - half) * steps + j), 0))
    ext = lambda start: pl.BlockSpec((16, lanes), lambda e, j: (start // 16, 0))
    two_steps = len(pieces) == 5
    in_specs = [SM] + [flat] * 3 + ([low, high] if two_steps else [flat, flat])
    in_specs += [ext(part * all_rows)] * 3 + [ext(half * all_rows)] + [of_all] * 3 + [flat]
    in_specs += [pl.BlockSpec((1, width, hidden), lambda e, j: (first + e, 0, 0)), pl.BlockSpec((1, hidden, width), lambda e, j: (first + e, 0, 0))]
    operands = [at, *pieces, *([] if two_steps else pieces[3:]), *extras, *g[:3], g[3 + chunk], w_in, w_out]
    last = chunk == chunks - 1
    shape = (part * all_rows + 16 * last, width)
    total = part * all_rows
    y_shapes = [(total, width), (2, total, width), (total, width)] if chunks == 2 else [(total, width)] * 4
    outs = [sd(shape, bf16)] * 4 + [sd(y, bf16) for y in y_shapes] + [sd(dg.shape, f32), sd((4, part, 4, all_rows, width), bf16)]
    every = lambda dims: pl.BlockSpec(dims, lambda e, j: (0,) * len(dims))
    out_specs = [every(shape)] * 4 + [every(y) for y in y_shapes]
    out_specs += [every(dg.shape), pl.BlockSpec((4, 1, 4, rows, width), lambda e, j: (0, e, 0, j, 0))]
    operands.append(dg)
    in_specs.append(every(dg.shape))
    operands += list(deps)
    in_specs += [ANY] * len(deps)
    return pl.pallas_call(
        functools.partial(moe_kernel, rows, part, first, last, len(deps)),
        grid=(part, steps),
        out_shape=tuple(outs), in_specs=in_specs, out_specs=tuple(out_specs),
        compiler_params=pltpu.CompilerParams(vmem_limit_bytes=58 << 20),
        cost_estimate=cost("moe"),
        name="moe",
    )(*operands)


def expert_grad_kernel(steps, at_ref, mine, other, *refs):
    gin, gout, mark = refs[-3:]
    mark[...] = jnp.zeros_like(mark)

    def put(a, b):
        both = [jnp.concatenate([r[n, 0, flip] for r in (a, b) for flip in range(4)], axis=0) for n in range(4)]
        for ref, left, right in ((gin, both[0], both[3]), (gout, both[2], both[1])):
            if steps == 1:
                ref[0] = dot(left, right, TN)
            else:
                part = dot(left, right, TN)
                ref[0] = jnp.where(pl.program_id(1) == 0, part, ref[0] + part)

    pl.when(at_ref[1] == 0)(lambda: put(mine, other))
    pl.when(at_ref[1] == 1)(lambda: put(other, mine))


def expert_grad(at, first, start, part, local, mine, other, before, deps):
    four, all_rows, width = mine.shape[2:]
    rows = 128 if all_rows % 128 == 0 else all_rows
    steps = all_rows // rows
    spec = pl.BlockSpec((4, 1, 4, rows, width), lambda e, j: (0, start + e, 0, j, 0))
    in_specs = [SM, spec, spec]
    operands = [at, mine, other]
    alias = {}
    if before:
        alias = {3: 0, 4: 1}
        operands += list(before)
        in_specs += [ANY] * 2
    operands += list(deps)
    in_specs += [ANY] * len(deps)
    out = pl.BlockSpec((1, width, width), lambda e, j: (first + start + e, 0, 0))
    return pl.pallas_call(
        functools.partial(expert_grad_kernel, steps),
        grid=(part, steps),
        out_shape=(sd((local, width, width), f32),) * 2 + (sd((8, 128), f32),), in_specs=in_specs,
        out_specs=(out, out, pl.BlockSpec((8, 128), lambda e, j: (0, 0))),
        input_output_aliases=alias,
        compiler_params=pltpu.CompilerParams(vmem_limit_bytes=56 << 20),
        cost_estimate=cost("expert_grad"),
        name="expert_grad",
    )(*operands)


def back_kernel(size, chunks, idx_ref, cot_ref, h_ref, xn_ref, probs_ref, gate_ref, router_ref, gains_ref, *refs):
    blocks = refs[:chunks * size]
    dh_ref, dhb_ref, small_ref, ds = refs[chunks * size:]
    experts = router_ref.shape[1]
    local = experts // size
    rows_of = local // chunks * CAP
    lanes = lanes_of(size)
    for n, block in enumerate(blocks):
        ds[n * rows_of:(n + 1) * rows_of, :] = block[0:rows_of, :]
    last = blocks[(chunks - 1) * size:]
    held = jnp.concatenate([last[k][rows_of:rows_of + local, 0:lanes].astype(f32) for k in range(size)], axis=0).astype(bf16)
    spread = as_bf16(onehot(idx_ref[:, 1:2], experts * CAP)) + as_bf16(onehot(idx_ref[:, 5:6], experts * CAP))
    dxn = dot(spread, ds[...])
    probs = probs_ref[...]
    gates, dgates, chosen = [], [], []
    for j in (0, 1):
        got = dot(as_bf16(onehot(idx_ref[:, 4 * j + 2:4 * j + 3], experts)), held)
        dgates.append(jnp.sum(jnp.where(onehot(idx_ref[:, 4 * j + 3:4 * j + 4], lanes), got, 0.0), axis=-1, keepdims=True))
        gates.append(gate_ref[:, j:j + 1])
        chosen.append(onehot(idx_ref[:, 4 * j:4 * j + 1], experts))
    mean = gates[0] * dgates[0] + gates[1] * dgates[1]
    scale = 1.0 / gate_ref[:, 2:3]
    dprobs = jnp.where(chosen[0], (dgates[0] - mean) * scale, 0.0) + jnp.where(chosen[1], (dgates[1] - mean) * scale, 0.0)
    dlogits = (probs * (dprobs - jnp.sum(probs * dprobs, axis=-1, keepdims=True))).astype(bf16)
    small_ref[...] = jnp.zeros_like(small_ref)
    small_ref[:, 0:experts] = dot(xn_ref[...], dlogits, TN).astype(bf16)
    dxn = dxn + dot(dlogits, router_ref[...], NT)
    h = h_ref[...]
    r = lax.rsqrt(jnp.mean(h * h, axis=-1, keepdims=True) + epsilon)
    gain_row = jnp.sum(dxn * h * r, axis=0, keepdims=True)
    small_ref[:, experts:experts + 1] = column_of(gain_row).astype(bf16)
    scaled = dxn * gains_ref[1:2, :]
    dh = cot_ref[...].astype(f32) + r * scaled - h * (r * r * r) * jnp.mean(h * scaled, axis=-1, keepdims=True)
    dh_ref[...] = dh
    dhb_ref[...] = dh.astype(bf16)


def back(idx, cot, h, xn, probs, gate, router, gains, blocks, size, chunks, deps):
    count, width = h.shape
    experts = router.shape[1]
    outs = [sd((count, width), f32), sd((count, width), bf16), sd((width, 128), bf16)]
    return call(functools.partial(back_kernel, size, chunks), "back", outs, (idx, cot, h, xn, probs, gate, router, gains, *blocks),
                scratch=[pltpu.VMEM((experts * CAP, width), bf16)], deps=deps)


def mix_kernel(count, chunks, idx_ref, h_ref, gate_ref, *refs):
    blocks, out_ref, ys = refs[:count], refs[count], refs[count + 1]
    rows_of = blocks[0].shape[0]
    part = rows_of // chunks
    for k, block in enumerate(blocks):
        for c in range(chunks):
            ys[(c * count + k) * part:(c * count + k + 1) * part, :] = block[c * part:(c + 1) * part, :]
    out = h_ref[...]
    for j in (0, 1):
        out = out + gate_ref[:, j:j + 1] * dot(as_bf16(onehot(idx_ref[:, 4 * j + 1:4 * j + 2], rows_of * count)), ys[...])
    out_ref[...] = out.astype(bf16)


def mix(idx, h, gate, blocks, size, chunks, deps):
    count, width = h.shape
    return call(functools.partial(mix_kernel, len(blocks), chunks), "mix", [sd((count, width), bf16)], (idx, h, gate, *blocks),
                scratch=[pltpu.VMEM((len(blocks) * blocks[0].shape[0], width), bf16)], deps=deps)[0]


def last_kernel(tokens_ref, dh_ref, own, rx, ry, rd, gains_ref, out_ref):
    x = tokens_ref[...].astype(f32)
    r = lax.rsqrt(jnp.mean(x * x, axis=-1, keepdims=True) + epsilon)
    scaled = add_terms((own, rx, ry, rd)) * gains_ref[0:1, :]
    out_ref[...] = dh_ref[...] + r * scaled - x * (r * r * r) * jnp.mean(x * scaled, axis=-1, keepdims=True)


def merge_kernel(size, at_ref, keep_ref, got_ref, *outs):
    me = at_ref[0]
    for k in range(size):
        to = (me + k) & (size - 1)
        outs[k][...] = (keep_ref[to].astype(f32) + got_ref[to].astype(f32)).astype(bf16)


def total_kernel(size, at_ref, q_ref, k_ref, v_ref, *refs):
    blocks, out_ref, few_ref = refs[:size], refs[size], refs[size + 1]
    total = sum(b[...].astype(f32) for b in blocks)
    out_ref[...] = total
    half = total.shape[0]
    width = q_ref.shape[1]
    few = total[:, 4 * width:]
    lane = lax.broadcasted_iota(i32, few.shape, 1)
    for r in (0, 1):
        @pl.when(at_ref[1] == r)
        def _():
            product = sum(total[:, n * width:(n + 1) * width] * ref[r * half:(r + 1) * half, :].astype(f32) for n, ref in enumerate((q_ref, k_ref, v_ref)))
            few_ref[...] = jnp.where(lane == TABLE - 1, jnp.sum(product, axis=1, keepdims=True), few)


def finish_kernel(at_ref, mine_ref, other_ref, few_mine, few_other, gain_ref, q_ref, k_ref, v_ref, o_ref, router_ref, table_ref, ga_ref, gm_ref, few):
    half = mine_ref.shape[0]
    width = q_ref.shape[1]
    experts = router_ref.shape[0]
    rows = table_ref.shape[1]

    def put(first, second, few_first, few_second):
        for n, ref in enumerate((q_ref, k_ref, v_ref, o_ref)):
            ref[0:half, :] = first[:, n * width:(n + 1) * width]
            ref[half:, :] = second[:, n * width:(n + 1) * width]
        few[0:half, :] = few_first[...]
        few[half:, :] = few_second[...]
        table_ref[...] = first[:, 4 * width:].T[TABLE + 1:TABLE + 1 + table_ref.shape[0], 0:rows]

    pl.when(at_ref[1] == 0)(lambda: put(mine_ref, other_ref, few_mine, few_other))
    pl.when(at_ref[1] == 1)(lambda: put(other_ref, mine_ref, few_other, few_mine))
    turned = few[...].T
    router_ref[...] = turned[0:experts, :]
    ga_ref[...] = turned[TABLE - 1:TABLE, :] / gain_ref[...].astype(f32)
    gm_ref[...] = turned[TABLE - 2:TABLE - 1, :]


def on_device(size, tokens, segments, routes, capacity, cotangent, rel_table, w_query, w_key, w_value, w_attn_out, gain_attn, gain_moe, w_router, w_in, w_out):
    z = lax.axis_index("expert").astype(i32)
    rep = lax.axis_index("rep").astype(i32)
    pos = lax.axis_index("tensor").astype(i32)
    at = jnp.stack([z, rep, pos])
    tok = tokens[0]
    cot = cotangent[0]
    count, width = tok.shape
    local = w_in.shape[0]
    experts = w_router.shape[1]
    chunks = 2 if local >= 4 else 1
    part = local // chunks
    rows_dev = w_query.shape[0]
    half = rows_dev // 2
    buckets = rel_table.shape[0] * size
    part_rows = part * CAP
    half_rows = part_rows * size // 2
    matrix = order_matrix(size, part, part_rows, 0, 0)

    packed, rest = call(pack_kernel, "pack", [sd((half, 896), bf16)] * 2,
                        (at, w_query, w_key, w_value, w_router.T, w_attn_out, gain_attn, gain_moe, rel_table.T),
                        scratch=[pltpu.VMEM((rows_dev, 896), f32)], smem=1)
    pieces = gather_pieces(tok, count // 2)
    idx = call(functools.partial(prepare_kernel, size, chunks), "prepare", [sd((count, 8), i32)], (z[None], routes[0].T, capacity[None]),
               smem=1, deps=(packed,))[0]

    g_blocks = spread(idx, cot, 0, size, local * CAP, (), "spread_g", chunks)
    mine = [after(to_expert(packed, k, size), g_blocks[0]) for k in range(1, size)]
    other = [to_core(m) for m in mine]
    g_blocks = [g_blocks[0]] + [after(b, *mine) for b in g_blocks[1:]]
    g_arrived = shifted(g_blocks)
    qkv_w, wo, router, gains, table = unpack(at, [packed, *mine], [rest, *other], buckets, pieces[1:3])

    xn, qkv = project(at, pieces, qkv_w, gains, tuple(g_blocks[1:]))
    o, lse, *parts = attn_fwd(at, table, qkv, segments, wo, ())
    g_ordered = call(functools.partial(reorder_all_kernel, size), "order_g", [sd((local * CAP * size, width), bf16)], (matrix, *g_arrived), deps=(o,))[0]
    terms = scatter_direct(parts[0], after(parts[1], g_ordered), parts[2], parts[3])
    terms = (*terms[:2], after(terms[2], gains), after(terms[3], gains))
    h, xn2, probs, gate, *blocks = route(idx, tok, terms, router, gains, size, chunks, ())
    g_pieces = gather_pieces(after(g_ordered, xn2), half_rows * chunks)

    arrived = shifted(blocks)
    ordered = [reorder(order_matrix(size, part, part_rows + 16, 16, 16), arrived, "order")]
    got = [gather_pieces(ordered[0], half_rows)]
    if chunks == 2:
        blocks = spread(idx, xn2, 1, size, part_rows, (ordered[0], *g_pieces[1:3]), "spread", 1)
        ordered.append(reorder(matrix, shifted(blocks), "order"))
        got.append(gather_direct(ordered[1]))
    extras = (*got[0][:3], got[0][4])
    ready = ordered[1:]

    step = max(part // 4, 1)
    pending = [(c, start) for c in range(chunks) for start in range(0, part, step)]
    grads = ()

    def expert_grads(many, *ready):
        nonlocal grads
        mark = ready[0]
        for c, start in pending[:many]:
            *grads, mark = expert_grad(at, c * part, start, step, local, acts[c], other_acts[c], grads, ready)
        del pending[:many]
        return mark

    acts, sums, ys = [], [], []
    dg_full = jnp.zeros((4, lanes_of(size) // 128, 16, 128), f32)
    for c in range(chunks):
        *outs, dg_full, act = moe(at, size, chunks, c, got[c], extras, g_pieces, w_in, w_out, dg_full, () if c else ready)
        sums.append(scatter_direct(*outs[:4]) if c < chunks - 1 else outs[:4])
        ys.append(outs[4:])
        acts.append(act)
    other_acts = [to_core(acts[0])]


    def give(c, extra, deps):
        given = call(functools.partial(give_back_kernel, size, extra), "give_back", [sd((part_rows + 16 * extra, width), bf16)] * size,
                     (matrix, *sums[c]), deps=deps)
        return given[0], [given[0]] + [to_expert(given[k], size - k, size) for k in range(1, size)]

    outs = list(sums[-1])
    if chunks == 2:
        outs = [*outs[:1], *[after(piece, *sums[0][1:]) for piece in outs[1:4]]]
    sums[-1] = scatter_direct(*outs)
    back_blocks = []
    mark = outs[0]
    if chunks == 2:
        mark, back_blocks = give(0, False, (mark, other_acts[0]))
    mark = expert_grads(1, mark)
    mark = expert_grads(1, mark, *back_blocks[1:])
    ready, blocks = give(chunks - 1, True, (mark,))
    if chunks == 2:
        y_packs = [after(ys[c][1], mark, *sums[-1][1:]) for c in (0, 1)]
        y_got = [to_tensor(pack, flip) for flip, pack in zip((1, 2), y_packs)]
    else:
        y_terms = scatter_direct(*ys[0])
    ready = (expert_grads(1, ready), *y_packs) if chunks == 2 else (ready,)
    dh, dhb, small = back(idx, cot, h, xn2, probs, gate, router, gains, back_blocks + blocks, size, chunks, ready)
    dh_pieces = gather_direct(dhb)
    mark = expert_grads(1, dhb)
    if chunks == 2:
        acts[1] = after(acts[1], mark)
        other_acts.append(to_core(acts[1]))
    if chunks == 2:
        y_parts, sent = scatter_end(*y_got, ys[1][2], ys[0][2], (mark,))
        mark = sent[0]

    y_late = (y_parts[1], y_parts[3]) if chunks == 2 else ()
    gtab, dqkv = attn_bwd(at, size, table, dh_pieces, segments, wo, qkv, lse, (mark,))
    keep, send, own, *parts = attn_grad(at, size, dqkv, qkv_w, xn, dh_pieces, o, small, gtab, y_late)
    terms = scatter_direct(own, *parts)
    got = to_core(send)
    out_blocks = call(functools.partial(merge_kernel, size), "merge", [sd((half, packed.shape[1]), bf16)] * size,
                      (at, keep, got), smem=1, deps=other_acts[1:])
    outs = [sd((local * CAP, width), bf16)] * size
    if chunks == 2:
        given = call(functools.partial(give_back_halves_kernel, size), "give_back_y", outs, (matrix, ys[0][0], ys[1][0], *y_parts), deps=(out_blocks[0],))
    else:
        given = call(functools.partial(give_back_kernel, size, False), "give_back_y", outs, (matrix, *y_terms), deps=(out_blocks[0],))
    y_blocks = [given[0]] + [to_expert(given[k], size - k, size) for k in range(1, size)]
    mark = expert_grads(1, out_blocks[0], given[0])
    mark = expert_grads(max(len(pending) - 2, 0), mark, *terms[1:])
    total, gain = call(functools.partial(total_kernel, size), "total", [sd(out_blocks[0].shape, f32), sd((half, 128), f32)],
                       (at, w_query, w_key, w_value, *shifted(out_blocks)), smem=1, deps=(mark, *terms[1:]))
    mark = expert_grads(1, total)
    grad_tokens = call(last_kernel, "last", [sd((count, width), f32)], (tok, dh, *terms, gains), deps=(mark,))[0]
    gain = gain + to_tensor(gain, 1)
    mark = expert_grads(len(pending), mark, gain)
    gain = gain + to_tensor(gain, 2)
    output = mix(idx, h, gate, y_blocks, size, chunks, (mark,))
    lw = w_query.shape[1]
    outs = [sd((rows_dev, lw), f32)] * 4 + [sd((experts, rows_dev), f32), sd(rel_table.T.shape, f32)] + [sd((1, rows_dev), f32)] * 2
    grad_q, grad_k, grad_v, grad_o, grad_router, grad_table, grad_ga, grad_gm = call(
        finish_kernel, "finish", outs, (at, total, to_core(total), gain, to_core(gain), gain_attn[None]), smem=1, scratch=[pltpu.VMEM((rows_dev, 128), f32)], deps=(output, mark))
    return (output[None], grad_tokens[None], grad_table.T, grad_q, grad_k, grad_v, grad_o, grad_ga[0], grad_gm[0], grad_router.T, *grads)


def solution(mesh):
    by_token = P(("expert", "rep"), "tensor", None)
    both = P("expert", "tensor")
    return jax.shard_map(
        functools.partial(on_device, mesh.shape["expert"]),
        mesh=mesh,
        in_specs=(by_token, P(("expert", "rep"), None), by_token, P(), by_token, both, both, both, both, both, P("expert"), P("expert"),
                  P("expert", None), P("expert", None, "tensor"), P("expert", "tensor", None)),
        out_specs=(by_token, by_token, both, both, both, both, both, P("expert"), P("expert"), P("expert", None),
                   P("expert", None, "tensor"), P("expert", "tensor", None)),
        check_vma=False,
    )
```

```python
import functools
import math

import jax
import jax.numpy as jnp
from jax import lax
from jax.experimental import pallas as pl
from jax.experimental.pallas import tpu as pltpu
from jax.sharding import PartitionSpec as P

HEAD = 64
CAP = 12
QB = 128
TABLE = 66
epsilon = 1e-06
masked_value = -1e30
thresholds = (16, 19, 21, 24, 27, 31, 35, 40, 46, 52, 59, 67, 77, 87, 99, 113)
lowest = tuple(range(16)) + thresholds
f32 = jnp.float32
bf16 = jnp.bfloat16
i32 = jnp.int32
NN = (((1,), (0,)), ((), ()))
NT = (((1,), (1,)), ((), ()))
TN = (((0,), (0,)), ((), ()))
VM = pl.BlockSpec(memory_space=pltpu.VMEM)
SM = pl.BlockSpec(memory_space=pltpu.SMEM)
sd = jax.ShapeDtypeStruct


def dot(a, b, dims=NN):
    return lax.dot_general(a, b, dims, preferred_element_type=f32)


ANY = pl.BlockSpec(memory_space=pl.ANY)
TIMES = {"attn_fwd": 13, "prepare": 30, "attn_bwd": 400, "attn_grad": 9, "project": 5, "moe": 300, "expert_grad": 1, "back": 5, "route": 4}


def cost(name):
    return pl.CostEstimate(flops=int(TIMES.get(name, 0.5) * 1_150_000_000), bytes_accessed=1000, transcendentals=0)


def call(kernel, name, outs, operands, scratch=(), smem=0, flops=0, moved=4_000_000, deps=()):
    given = len(operands)

    def body(*refs):
        kernel(*refs[:given], *refs[given + len(deps):])

    return pl.pallas_call(
        body,
        out_shape=tuple(outs),
        in_specs=[SM] * smem + [VM] * (given - smem) + [ANY] * len(deps),
        out_specs=tuple(VM for _ in outs),
        scratch_shapes=list(scratch),
        compiler_params=pltpu.CompilerParams(vmem_limit_bytes=56 << 20),
        cost_estimate=cost(name),
        name=name,
    )(*operands, *deps)


def after(value, *deps):
    return pl.pallas_call(
        lambda *refs: None,
        out_shape=sd(value.shape, value.dtype),
        in_specs=[ANY] * (1 + len(deps)),
        out_specs=ANY,
        input_output_aliases={0: 0},
        name="after",
    )(value, *deps)


def to_tensor(a, flip):
    return lax.ppermute(a, "tensor", [(i, i ^ flip) for i in range(4)])


def to_expert(a, shift, size):
    return lax.ppermute(a, "expert", [(i, (i + shift) % size) for i in range(size)])


def to_core(a):
    return lax.ppermute(a, "rep", [(0, 1), (1, 0)])


def shifted(blocks):
    size = len(blocks)
    return [blocks[0]] + [to_expert(blocks[k], k, size) for k in range(1, size)]


def gather_pieces(own, half):
    px = to_tensor(own, 1)
    py = to_tensor(own, 2)
    d0 = to_tensor(px[:half], 2)
    d1 = to_tensor(py[half:], 1)
    return own, px, py, d0, d1


def gather_direct(own):
    return (own, *[to_tensor(own, flip) for flip in (1, 2, 3)])


def late_kernel(x_late, y_late, got_x, got_y, sum_x, sum_y):
    sum_x[...] = (x_late[...].astype(f32) + got_y[0].astype(f32)).astype(bf16)
    sum_y[...] = (y_late[...].astype(f32) + got_x[0].astype(f32)).astype(bf16)


def scatter_end(got_x, got_y, x_late, y_late, deps):
    shape = sd(x_late.shape, bf16)
    sent = call(late_kernel, "late", [shape, shape], (x_late, y_late, got_x, got_y), deps=deps)
    return (got_x, to_tensor(sent[1], 2), got_y, to_tensor(sent[0], 1)), sent


def scatter_direct(own, *pieces):
    return (own, *[to_tensor(piece, flip) for flip, piece in zip((1, 2, 3), pieces)])


def add_terms(refs):
    return sum(r[...].astype(f32) for r in refs)


def onehot(index, width):
    return lax.broadcasted_iota(i32, (index.shape[0], width), 1) == index


def as_bf16(mask):
    return jnp.where(mask, 1.0, 0.0).astype(bf16)


def prepare_kernel(size, chunks, me_ref, routes_ref, capacity_ref, idx_ref):
    count = routes_ref.shape[1]
    experts = capacity_ref.shape[1]
    local = experts // size
    part = local // chunks
    me = me_ref[0]
    first, second = (jnp.broadcast_to(routes_ref[j:j + 1, :], (8, count)).T[:, 0:1] for j in (0, 1))
    both = as_bf16(onehot(first, experts)) + as_bf16(onehot(second, experts))
    rows = lax.broadcasted_iota(i32, (count, count), 0)
    cols = lax.broadcasted_iota(i32, (count, count), 1)
    before = dot(as_bf16(cols < rows), both)
    capacity = capacity_ref[...].astype(f32)
    shift = int(math.log2(local))
    columns = []
    for route in (first, second):
        mine = onehot(route, experts)
        position = jnp.sum(jnp.where(mine, before, 0.0), axis=1, keepdims=True)
        limit = jnp.sum(jnp.where(mine, jnp.broadcast_to(capacity, mine.shape), 0.0), axis=1, keepdims=True)
        keep = position < limit
        position = position.astype(i32)
        owner = lax.shift_right_logical(route, jnp.full_like(route, shift))
        inner = route & (local - 1)
        away = (owner - me + size) & (size - 1)
        chunk = lax.shift_right_logical(inner, jnp.full_like(route, int(math.log2(part))))
        slot = ((chunk * size + away) * part + (inner & (part - 1))) * CAP + position
        columns += [route, jnp.where(keep, slot, -1), jnp.where(keep, away * local + inner, -1), away * CAP + position]
    for n, column in enumerate(columns):
        idx_ref[:, n:n + 1] = column


def spread_kernel(first, chunks, idx_ref, rows_ref, *outs):
    count = len(outs)
    block = outs[0].shape[0] // chunks
    width = block * chunks * count
    spread = as_bf16(onehot(idx_ref[:, 1:2] - first, width)) + as_bf16(onehot(idx_ref[:, 5:6] - first, width))
    slots = dot(spread, rows_ref[...], TN).astype(bf16)
    for c in range(chunks):
        for k, ref in enumerate(outs):
            ref[c * block:(c + 1) * block, :] = slots[(c * count + k) * block:(c * count + k + 1) * block]


def spread(idx, rows, chunk, count, block, deps, name, chunks):
    return call(functools.partial(spread_kernel, chunk * count * block, chunks), name, [sd((block, rows.shape[1]), bf16)] * count, (idx, rows), deps=deps)


def order_matrix(size, part, block, extra, out_extra):
    rows = part * size * CAP
    m = [[0.0] * (size * block) for _ in range(rows + out_extra)]
    for e in range(part):
        for k in range(size):
            for c in range(CAP):
                m[(e * size + k) * CAP + c][k * block + e * CAP + c] = 1.0
    for r in range(extra):
        for k in range(size):
            m[rows + r][k * block + part * CAP + r] = 1.0
    return jnp.array(m, dtype=bf16)


def reorder_kernel(count, m_ref, *refs):
    blocks, out_ref = refs[:count], refs[count]
    out_ref[...] = dot(m_ref[...], jnp.concatenate([b[...] for b in blocks], axis=0)).astype(bf16)


def reorder_all_kernel(count, m_ref, *refs):
    blocks, out_ref = refs[:count], refs[count]
    block = m_ref.shape[1] // count
    rows = m_ref.shape[0]
    for c in range(out_ref.shape[0] // rows):
        chosen = jnp.concatenate([b[c * block:(c + 1) * block, :] for b in blocks], axis=0)
        out_ref[c * rows:(c + 1) * rows, :] = dot(m_ref[...], chosen).astype(bf16)


def reorder(matrix, blocks, name, deps=()):
    rows = matrix.shape[0]
    width = blocks[0].shape[1]
    return call(functools.partial(reorder_kernel, len(blocks)), name, [sd((rows, width), bf16)], (matrix, *blocks),
                flops=2 * matrix.size * width, moved=2 * rows * width * 2, deps=deps)[0]


def give_back_kernel(count, extra, m_ref, *refs):
    outs = refs[4:]
    total = add_terms(refs[:4]).astype(bf16)
    rows = m_ref.shape[0]
    back = dot(m_ref[...], total[0:rows], TN).astype(bf16)
    block = back.shape[0] // count
    for k in range(count):
        outs[k][0:block, :] = back[k * block:(k + 1) * block]
        if extra:
            outs[k][block:, :] = total[rows:]


def give_back_halves_kernel(count, m_ref, own_a, own_b, got_x, late_y, got_y, late_x, *outs):
    halves = (own_a[...].astype(f32) + got_x[1].astype(f32) + late_y[...].astype(f32), own_b[...].astype(f32) + got_y[1].astype(f32) + late_x[...].astype(f32))
    for n, total in enumerate(halves):
        back = dot(m_ref[...], total.astype(bf16), TN).astype(bf16)
        block = back.shape[0] // count
        for k in range(count):
            outs[k][n * block:(n + 1) * block, :] = back[k * block:(k + 1) * block]


def pack_kernel(at_ref, q_ref, k_ref, v_ref, r_ref, o_ref, ga_ref, gm_ref, t_ref, out_ref, rest_ref, full):
    rows, width = q_ref.shape
    full[...] = jnp.zeros_like(full)
    place = 0
    for ref in (q_ref, k_ref, v_ref, r_ref, o_ref):
        value = ref[...].astype(f32)
        value = value.T if ref is r_ref else value
        full[:, place:place + value.shape[1]] = value
        place += value.shape[1]
    for ref in (ga_ref, gm_ref):
        full[:, place:place + 1] = column_of(ref[...].astype(f32)[None, :])
        place += 1
    full[0:t_ref.shape[1], place:place + t_ref.shape[0]] = t_ref[...].astype(f32).T
    half = rows // 2
    for r in (0, 1):
        @pl.when(at_ref[1] == r)
        def _():
            out_ref[...] = full[r * half:(r + 1) * half, :].astype(bf16)
            rest_ref[...] = full[(1 - r) * half:(2 - r) * half, :].astype(bf16)


def unpack_kernel(size, at_ref, *refs):
    mine, other = refs[:size], refs[size:2 * size]
    full, qkv_ref, wo_ref, router_ref, gains_ref, table_ref = refs[2 * size:]
    me, rep = at_ref[0], at_ref[1]
    half = mine[0].shape[0]
    for k in range(size):
        z = (me - k + size) & (size - 1)
        full[2 * z + rep] = mine[k][...].astype(f32)
        full[2 * z + 1 - rep] = other[k][...].astype(f32)
    full = jnp.concatenate([full[n] for n in range(2 * size)], axis=0)
    qkv_ref[...] = full[:, 0:576].astype(bf16)
    router_ref[...] = full[:, 576:640].astype(bf16)
    wo_ref[...] = full[:, 640:832].astype(bf16)
    tail = full[:, 768:896]
    turned = tail.T
    gains_ref[...] = turned[64:72, :]
    rows = table_ref.shape[0] // size
    for z in range(size):
        table_ref[z * rows:(z + 1) * rows, :] = tail[z * 2 * half: z * 2 * half + rows, :]


def unpack(at, mine, other, buckets, deps):
    size = len(mine)
    half, cols = mine[0].shape
    width = 2 * half * size

    def kernel(at_ref, *refs):
        unpack_kernel(size, at_ref, *refs[:2 * size], refs[-1], *refs[2 * size:-1])

    outs = [sd((width, 576), bf16), sd((width, 192), bf16), sd((width, 64), bf16), sd((8, width), f32), sd((buckets, 128), f32)]
    return call(kernel, "unpack", outs, (at, *mine, *other), scratch=[pltpu.VMEM((2 * size, half, cols), f32)], smem=1, deps=deps)


def piece_shapes(rows, width):
    return [sd((rows, width), bf16)] * 4


def near_offset():
    rows = lax.broadcasted_iota(jnp.int32, (QB, 2 * QB), 0)
    cols = lax.broadcasted_iota(jnp.int32, (QB, 2 * QB), 1)
    return QB + rows - cols


def near_bias(table_ref, head, buckets):
    off = near_offset()
    bias = jnp.where(off < 0, masked_value, table_ref[0, TABLE + head])
    for b in range(1, buckets):
        bias = jnp.where(off >= lowest[b], table_ref[b, TABLE + head], bias)
    return bias


def scores_of(q, k_ref, head, i, near, far, seg_col, seg_row_ref):
    lo = max(i - 1, 0) * QB
    hi = (i + 1) * QB
    s = dot(q, k_ref[head, 0:hi], NT)
    bias = near[:, QB:] if i == 0 else near
    same_near = seg_col == seg_row_ref[:, lo:hi]
    s_near = jnp.where(same_near, s[:, lo:hi] + bias, masked_value)
    if lo == 0:
        return s_near
    same_far = seg_col == seg_row_ref[:, 0:lo]
    s_far = jnp.where(same_far, s[:, 0:lo] + far, masked_value)
    return jnp.concatenate([s_far, s_near], axis=1)


def project_kernel(at_ref, own_ref, px_ref, py_ref, pd0_ref, pd1_ref, w_ref, gain_ref, xn_ref, qkv_ref):
    pos = at_ref[2]
    tok = own_ref.shape[0]
    half = tok // 2
    gain = gain_ref[0:1, :]

    def put(rows, flip, start=0):
        x = rows.astype(f32)
        r = lax.rsqrt(jnp.mean(x * x, axis=-1, keepdims=True) + epsilon)
        xn = (x * r * gain).astype(bf16)
        at = pl.ds(pl.multiple_of((pos ^ flip) * tok + start, half), rows.shape[0])
        xn_ref[at, :] = xn
        qkv_ref[at, :] = dot(xn, w_ref[...]).astype(bf16)

    put(own_ref[...], 0)
    put(px_ref[...], 1)
    put(py_ref[...], 2)
    put(pd0_ref[...], 3)
    put(pd1_ref[...], 3, half)


def column_of(row):
    return jnp.broadcast_to(row, (8, row.shape[1])).T[:, 0:1]


def attn_fwd_kernel(heads, at_ref, table_ref, qkv_ref, segr_ref, wo_ref, o_ref, lse_ref, out_own, out_x, out_y, out_d, qs, ks, vs, seg):
    pos = at_ref[2]
    tok = out_own.shape[0]
    half = tok // 2
    buckets = table_ref.shape[0]
    seg[...] = column_of(segr_ref[...])

    def at(flip, start=0, size=tok):
        return pl.ds(pl.multiple_of((pos ^ flip) * tok + start, half), size)

    width = heads * HEAD
    qkv = qkv_ref[...]
    for h in range(heads):
        qs[h] = qkv[:, h * HEAD:(h + 1) * HEAD] * bf16(0.125)
        ks[h] = qkv[:, width + h * HEAD: width + (h + 1) * HEAD]
        vs[h] = qkv[:, 2 * width + h * HEAD: 2 * width + (h + 1) * HEAD]
    blocks = qkv_ref.shape[0] // QB
    for h in range(heads):
        near = near_bias(table_ref, h, buckets)
        far = table_ref[buckets - 1, TABLE + h]
        for i in range(blocks):
            rows = slice(i * QB, (i + 1) * QB)
            s = scores_of(qs[h, rows], ks, h, i, near, far, seg[rows, :], segr_ref)
            top = jnp.max(s, axis=-1, keepdims=True)
            e = jnp.exp(s - top)
            total = jnp.sum(e, axis=-1, keepdims=True)
            p = (e * (1.0 / total)).astype(bf16)
            o_ref[rows, h * HEAD:(h + 1) * HEAD] = dot(p, vs[h, 0:(i + 1) * QB]).astype(bf16)
            lse_ref[rows, h:h + 1] = top + jnp.log(total)
    wo = wo_ref[...]
    for flip, ref in enumerate((out_own, out_x, out_y, out_d)):
        ref[...] = dot(o_ref[at(flip), :], wo, NT).astype(bf16)


def attn_bwd_kernel(heads, size, at_ref, table_ref, own_ref, px_ref, py_ref, pd_ref, segr_ref, wo_ref, qkv_ref, lse_ref,
                    gtab_ref, dqkv, dh, qs, ks, vs, do, dk, dv, acc, seg):
    pos = at_ref[2]
    tok = own_ref.shape[0]
    half = tok // 2
    buckets = table_ref.shape[0]
    width = heads * HEAD

    def at(flip, start=0, size=tok):
        return pl.ds(pl.multiple_of((pos ^ flip) * tok + start, half), size)

    seg[...] = column_of(segr_ref[...])
    dh[at(0), :] = own_ref[...]
    dh[at(1), :] = px_ref[...]
    dh[at(2), :] = py_ref[...]
    dh[at(3), :] = pd_ref[...]
    dall = dot(dh[...], wo_ref[...]).astype(bf16)
    for h in range(heads):
        do[h] = dall[:, h * HEAD:(h + 1) * HEAD]
        qs[h] = qkv_ref[:, h * HEAD:(h + 1) * HEAD] * bf16(0.125)
        ks[h] = qkv_ref[:, width + h * HEAD: width + (h + 1) * HEAD]
        vs[h] = qkv_ref[:, 2 * width + h * HEAD: 2 * width + (h + 1) * HEAD]
    blocks = qkv_ref.shape[0] // QB
    off = near_offset()
    per = gtab_ref.shape[1]
    gtab_ref[...] = jnp.zeros_like(gtab_ref)
    for h in range(heads):
        near = near_bias(table_ref, h, buckets)
        far = table_ref[buckets - 1, TABLE + h]
        acc[...] = jnp.zeros_like(acc)
        dk[...] = jnp.zeros_like(dk)
        dv[...] = jnp.zeros_like(dv)
        far_sum = jnp.zeros((QB, 1), f32)
        for i in range(blocks):
            rows = slice(i * QB, (i + 1) * QB)
            lo = max(i - 1, 0) * QB
            hi = (i + 1) * QB
            q = qs[h, rows]
            s = scores_of(q, ks, h, i, near, far, seg[rows, :], segr_ref)
            p = jnp.exp(s - lse_ref[rows, h:h + 1])
            g = do[h, rows]
            dv[0:hi] += dot(p.astype(bf16), g, TN)
            dp = dot(g, vs[h, 0:hi], NT)
            pd = p * dp
            ds = (pd - p * jnp.sum(pd, axis=-1, keepdims=True)).astype(bf16)
            dq = dot(ds, ks[h, 0:hi]) * 0.125
            dqkv[rows, h * HEAD:(h + 1) * HEAD] = dq.astype(bf16)
            dk[0:hi] += dot(ds, q, TN)
            dsf = ds.astype(f32)
            if i == 0:
                acc[:, QB:] += dsf
            else:
                acc[...] += dsf[:, lo:hi]
            if lo > 0:
                far_sum = far_sum + jnp.sum(dsf[:, 0:lo], axis=-1, keepdims=True)
        dqkv[:, width + h * HEAD: width + (h + 1) * HEAD] = dk[...].astype(bf16)
        dqkv[:, 2 * width + h * HEAD: 2 * width + (h + 1) * HEAD] = dv[...].astype(bf16)
        total = acc[...]
        rest = jnp.sum(far_sum, axis=0, keepdims=True)
        for b in range(buckets):
            if b == buckets - 1:
                inside = off >= lowest[b]
            else:
                inside = (off >= lowest[b]) & (off < lowest[b + 1])
            part = jnp.sum(jnp.where(inside, total, 0.0), axis=0, keepdims=True)
            one = jnp.sum(part, axis=1, keepdims=True)
            gtab_ref[b // per, b % per:b % per + 1, TABLE + 1 + h:TABLE + 2 + h] = one + rest if b == buckets - 1 else one


def attn_grad_kernel(size, at_ref, dqkv, w_ref, xn_ref, own_ref, px_ref, py_ref, pd_ref, o_ref, small_ref, gtab_ref, keep_ref, send_ref,
                     out_own, out_x, out_y, out_d, dh, full):
    pos, rep = at_ref[2], at_ref[1]
    tok = out_own.shape[0]
    half = tok // 2
    width = o_ref.shape[1]

    def at(flip, start=0, size=tok):
        return pl.ds(pl.multiple_of((pos ^ flip) * tok + start, half), size)

    dh[at(0), :] = own_ref[...]
    dh[at(1), :] = px_ref[...]
    dh[at(2), :] = py_ref[...]
    dh[at(3), :] = pd_ref[...]
    w = w_ref[...]
    for flip, ref in enumerate((out_own, out_x, out_y, out_d)):
        ref[...] = dot(dqkv[at(flip), :], w, NT).astype(bf16)
    grad = dot(xn_ref[...], dqkv[...], TN)
    grad_out = dot(dh[...], o_ref[...], TN)
    part_rows = keep_ref.shape[1]
    for n in range(2 * size):
        full[n, :, 0:3 * width] = grad[n * part_rows:(n + 1) * part_rows].astype(bf16)
        full[n, :, 3 * width:4 * width] = grad_out[n * part_rows:(n + 1) * part_rows].astype(bf16)
        few = small_ref[n * part_rows:(n + 1) * part_rows, :]
        full[n, :, 4 * width:] = few
        if n % 2 == 0:
            rows = gtab_ref.shape[1]
            full[n, 0:rows, 4 * width:] = (few[0:rows].astype(f32) + gtab_ref[n // 2]).astype(bf16)
    for z in range(size):
        keep_ref[z] = full[2 * z + rep]
        send_ref[z] = full[2 * z + 1 - rep]


def project(at, pieces, w, gains, deps):
    tok, width = pieces[0].shape
    return call(project_kernel, "project", [sd((4 * tok, width), bf16), sd((4 * tok, w.shape[1]), bf16)], (at, *pieces, w, gains),
                smem=1, deps=deps)


def attn_fwd(at, table, qkv, segr, wo, deps):
    width = wo.shape[0]
    length = qkv.shape[0]
    heads = wo.shape[1] // HEAD
    outs = [sd((length, heads * HEAD), bf16), sd((length, heads), f32)]
    return call(functools.partial(attn_fwd_kernel, heads), "attn_fwd", outs + piece_shapes(length // 4, width),
                (at, table, qkv, segr, wo),
                scratch=[pltpu.VMEM((heads, length, HEAD), bf16)] * 3 + [pltpu.VMEM((length, 1), i32)], smem=2,
                flops=8_000_000_000, moved=5_000_000, deps=deps)


def attn_bwd(at, size, table, pieces, segr, wo, qkv, lse, deps):
    tok, width = pieces[0].shape
    length = qkv.shape[0]
    heads = wo.shape[1] // HEAD
    outs = [sd((size, table.shape[0] // size, 128), f32), sd(qkv.shape, bf16)]
    scratch = [pltpu.VMEM((length, width), bf16)] + [pltpu.VMEM((heads, length, HEAD), bf16)] * 4 + [pltpu.VMEM((length, HEAD), f32)] * 2
    scratch += [pltpu.VMEM((QB, 2 * QB), f32), pltpu.VMEM((length, 1), i32)]
    return call(functools.partial(attn_bwd_kernel, heads, size), "attn_bwd", outs, (at, table, *pieces, segr, wo, qkv, lse),
                scratch=scratch, smem=2, flops=12_000_000_000, moved=8_000_000, deps=deps)


def attn_grad(at, size, dqkv, w, xn, pieces, o, small, gtab, deps):
    tok, width = pieces[0].shape
    cols = w.shape[1] + o.shape[1] + small.shape[1]
    rows = width // (2 * size)
    outs = [sd((size, rows, cols), bf16)] * 2 + piece_shapes(tok, width)
    return call(functools.partial(attn_grad_kernel, size), "attn_grad", outs, (at, dqkv, w, xn, *pieces, o, small, gtab),
                scratch=[pltpu.VMEM((4 * tok, width), bf16), pltpu.VMEM((2 * size, rows, cols), bf16)], smem=1,
                flops=4_000_000_000, moved=9_000_000, deps=deps)


def route_kernel(size, chunks, idx_ref, tokens_ref, own, rx, ry, rd, router_ref, gains_ref, h_ref, xn_ref, probs_ref, gate_ref, *blocks):
    count, width = tokens_ref.shape
    experts = router_ref.shape[1]
    local = experts // size
    rows_of = local // chunks * CAP
    lanes = lanes_of(size)
    h = tokens_ref[...].astype(f32) + add_terms((own, rx, ry, rd))
    r = lax.rsqrt(jnp.mean(h * h, axis=-1, keepdims=True) + epsilon)
    xn = (h * r * gains_ref[1:2, :]).astype(bf16)
    h_ref[...] = h
    xn_ref[...] = xn
    logits = dot(xn, router_ref[...])
    e = jnp.exp(logits - jnp.max(logits, axis=-1, keepdims=True))
    probs = e / jnp.sum(e, axis=-1, keepdims=True)
    probs_ref[...] = probs
    picked = [jnp.sum(jnp.where(onehot(idx_ref[:, 4 * j:4 * j + 1], experts), probs, 0.0), axis=-1, keepdims=True) for j in (0, 1)]
    total = picked[0] + picked[1]
    gates = [p / total for p in picked]
    gate_ref[:, 0:1], gate_ref[:, 1:2], gate_ref[:, 2:3] = gates[0], gates[1], total
    spread = as_bf16(onehot(idx_ref[:, 1:2], size * rows_of)) + as_bf16(onehot(idx_ref[:, 5:6], size * rows_of))
    slots = dot(spread, xn, TN).astype(bf16)
    held = jnp.zeros((experts, lanes), f32)
    for j in (0, 1):
        to = as_bf16(onehot(idx_ref[:, 4 * j + 2:4 * j + 3], experts))
        at = jnp.where(onehot(idx_ref[:, 4 * j + 3:4 * j + 4], lanes), gates[j], 0.0).astype(bf16)
        held = held + dot(to, at, TN)
    for k, ref in enumerate(blocks):
        ref[0:rows_of, :] = slots[k * rows_of:(k + 1) * rows_of]
        ref[rows_of:, :] = jnp.zeros((16, width), bf16)
        ref[rows_of:rows_of + local, 0:lanes] = held[k * local:(k + 1) * local].astype(bf16)


def lanes_of(size):
    return -(-size * CAP // 128) * 128


def route(idx, tokens, parts, router, gains, size, chunks, deps):
    count, width = tokens.shape
    experts = router.shape[1]
    rows_of = experts // size // chunks * CAP
    outs = [sd((count, width), f32), sd((count, width), bf16), sd((count, experts), f32), sd((count, 8), f32)]
    outs += [sd((rows_of + 16, width), bf16)] * size
    return call(functools.partial(route_kernel, size, chunks), "route", outs, (idx, tokens, *parts, router, gains),
                flops=400_000_000, moved=5_000_000, deps=deps)


def moe_kernel(rows, part, offset, last, skip, at_ref, own, px, py, d0, d1, e_own, e_px, e_py, e_d, g_own, g_px, g_py, g_far, win_ref, wout_ref,
               dg_in, *refs):
    outs, y_outs, dg_ref, acts = refs[skip:skip + 4], refs[skip + 4:-2], refs[-2], refs[-1]
    e, j = pl.program_id(0), pl.program_id(1)
    steps = pl.num_programs(1)

    @pl.when((e == 0) & (j == 0))
    def _():
        dg_ref[...] = dg_in[...]

    wide = e_own.shape[1]
    pick = lax.broadcasted_iota(i32, (16, wide), 0) == e + offset
    square = lax.broadcasted_iota(i32, (rows, wide), 0) + j * rows == lax.broadcasted_iota(i32, (rows, wide), 1)

    def gate_of(ref):
        row = jnp.sum(jnp.where(pick, ref[...].astype(f32), 0.0), axis=0, keepdims=True)
        return jnp.sum(jnp.where(square, jnp.broadcast_to(row, square.shape), 0.0), axis=1, keepdims=True)

    def keep(n, value):
        for flip in range(4):
            acts[n, 0, flip] = value[flip * rows:(flip + 1) * rows]

    def put(value, outs):
        at = pl.ds(pl.multiple_of((e * steps + j) * rows, 16), rows)
        for flip, ref in enumerate(outs):
            ref[at, :] = value[flip * rows:(flip + 1) * rows]

    gate = jnp.concatenate([gate_of(r) for r in (e_own, e_px, e_py, e_d)], axis=0)
    far = jnp.where(e < part // 2, d0[...].astype(f32), d1[...].astype(f32)).astype(bf16)
    s = jnp.concatenate([own[...], px[...], py[...], far], axis=0)
    g = jnp.concatenate([g_own[...], g_px[...], g_py[...], g_far[...]], axis=0).astype(f32)
    keep(0, s)
    win, wout = win_ref[0], wout_ref[0]
    dy = (g * gate).astype(bf16)
    keep(1, dy)
    a = dot(s, win)
    dhid = dot(dy, wout, NT)
    c = math.sqrt(2.0 / math.pi)
    t = jnp.tanh(a * (c + (c * 0.044715) * (a * a)))
    up = 0.5 + 0.5 * t
    hid = (a * up).astype(bf16)
    slope = up + (0.5 * a) * (1.0 - t * t) * (c + (3 * c * 0.044715) * (a * a))
    da = (dhid * slope).astype(bf16)
    keep(2, hid)
    keep(3, da)
    put(dot(da, win, NT).astype(bf16), outs)
    y = dot(hid, wout)
    ones = jnp.ones((8, y.shape[1]), bf16)
    sums = dot(ones, (y * g).astype(bf16), NT)
    if len(y_outs) == 4:
        put(y.astype(bf16), y_outs)
    else:
        near = 1 if offset == 0 else 2
        own_ref, pack, once = y_outs
        put(y.astype(bf16), [own_ref] + ([pack.at[1], once] if near == 1 else [once, pack.at[1]]) + [pack.at[0]])
    for flip in range(4):
        row = sums[0:1, flip * rows:(flip + 1) * rows]
        dg_ref[flip, j, pl.ds(e + offset, 1), 0:rows] = row

    if last:
        @pl.when((e == part - 1) & (j == steps - 1))
        def _():
            for flip, ref in enumerate(outs):
                ref[-16:, :] = jnp.zeros((16, ref.shape[1]), bf16)
                for n in range(wide // 128):
                    ref[-16:, n * 128:(n + 1) * 128] = dg_ref[flip, n].astype(bf16)


def moe(at, size, chunks, chunk, pieces, extras, g, w_in, w_out, dg, deps):
    all_rows = size * CAP
    rows = 128 if all_rows % 128 == 0 else all_rows
    steps = all_rows // rows
    local, width, hidden = w_in.shape
    part = local // chunks
    lanes = -(-all_rows // 128) * 128
    first = chunk * part
    whole = lambda e, j: (e * steps + j, 0)
    flat = pl.BlockSpec((rows, width), whole)
    of_all = pl.BlockSpec((rows, width), lambda e, j: ((first + e) * steps + j, 0))
    half = part // 2
    low = pl.BlockSpec((rows, width), lambda e, j: (jnp.where(e < half, e * steps + j, half * steps - 1), 0))
    high = pl.BlockSpec((rows, width), lambda e, j: (jnp.where(e < half, 0, (e - half) * steps + j), 0))
    ext = lambda start: pl.BlockSpec((16, lanes), lambda e, j: (start // 16, 0))
    two_steps = len(pieces) == 5
    in_specs = [SM] + [flat] * 3 + ([low, high] if two_steps else [flat, flat])
    in_specs += [ext(part * all_rows)] * 3 + [ext(half * all_rows)] + [of_all] * 3 + [flat]
    in_specs += [pl.BlockSpec((1, width, hidden), lambda e, j: (first + e, 0, 0)), pl.BlockSpec((1, hidden, width), lambda e, j: (first + e, 0, 0))]
    operands = [at, *pieces, *([] if two_steps else pieces[3:]), *extras, *g[:3], g[3 + chunk], w_in, w_out]
    last = chunk == chunks - 1
    shape = (part * all_rows + 16 * last, width)
    total = part * all_rows
    y_shapes = [(total, width), (2, total, width), (total, width)] if chunks == 2 else [(total, width)] * 4
    outs = [sd(shape, bf16)] * 4 + [sd(y, bf16) for y in y_shapes] + [sd(dg.shape, f32), sd((4, part, 4, all_rows, width), bf16)]
    every = lambda dims: pl.BlockSpec(dims, lambda e, j: (0,) * len(dims))
    out_specs = [every(shape)] * 4 + [every(y) for y in y_shapes]
    out_specs += [every(dg.shape), pl.BlockSpec((4, 1, 4, rows, width), lambda e, j: (0, e, 0, j, 0))]
    operands.append(dg)
    in_specs.append(every(dg.shape))
    operands += list(deps)
    in_specs += [ANY] * len(deps)
    return pl.pallas_call(
        functools.partial(moe_kernel, rows, part, first, last, len(deps)),
        grid=(part, steps),
        out_shape=tuple(outs), in_specs=in_specs, out_specs=tuple(out_specs),
        compiler_params=pltpu.CompilerParams(vmem_limit_bytes=58 << 20),
        cost_estimate=cost("moe"),
        name="moe",
    )(*operands)


def expert_grad_kernel(steps, at_ref, mine, other, *refs):
    gin, gout, mark = refs[-3:]
    mark[...] = jnp.zeros_like(mark)

    def put(a, b):
        both = [jnp.concatenate([r[n, 0, flip] for r in (a, b) for flip in range(4)], axis=0) for n in range(4)]
        for ref, left, right in ((gin, both[0], both[3]), (gout, both[2], both[1])):
            if steps == 1:
                ref[0] = dot(left, right, TN)
            else:
                part = dot(left, right, TN)
                ref[0] = jnp.where(pl.program_id(1) == 0, part, ref[0] + part)

    pl.when(at_ref[1] == 0)(lambda: put(mine, other))
    pl.when(at_ref[1] == 1)(lambda: put(other, mine))


def expert_grad(at, first, start, part, local, mine, other, before, deps):
    four, all_rows, width = mine.shape[2:]
    rows = 128 if all_rows % 128 == 0 else all_rows
    steps = all_rows // rows
    spec = pl.BlockSpec((4, 1, 4, rows, width), lambda e, j: (0, start + e, 0, j, 0))
    in_specs = [SM, spec, spec]
    operands = [at, mine, other]
    alias = {}
    if before:
        alias = {3: 0, 4: 1}
        operands += list(before)
        in_specs += [ANY] * 2
    operands += list(deps)
    in_specs += [ANY] * len(deps)
    out = pl.BlockSpec((1, width, width), lambda e, j: (first + start + e, 0, 0))
    return pl.pallas_call(
        functools.partial(expert_grad_kernel, steps),
        grid=(part, steps),
        out_shape=(sd((local, width, width), f32),) * 2 + (sd((8, 128), f32),), in_specs=in_specs,
        out_specs=(out, out, pl.BlockSpec((8, 128), lambda e, j: (0, 0))),
        input_output_aliases=alias,
        compiler_params=pltpu.CompilerParams(vmem_limit_bytes=56 << 20),
        cost_estimate=cost("expert_grad"),
        name="expert_grad",
    )(*operands)


def back_kernel(size, chunks, idx_ref, cot_ref, h_ref, xn_ref, probs_ref, gate_ref, router_ref, gains_ref, *refs):
    blocks = refs[:chunks * size]
    dh_ref, dhb_ref, small_ref, ds = refs[chunks * size:]
    experts = router_ref.shape[1]
    local = experts // size
    rows_of = local // chunks * CAP
    lanes = lanes_of(size)
    for n, block in enumerate(blocks):
        ds[n * rows_of:(n + 1) * rows_of, :] = block[0:rows_of, :]
    last = blocks[(chunks - 1) * size:]
    held = jnp.concatenate([last[k][rows_of:rows_of + local, 0:lanes].astype(f32) for k in range(size)], axis=0).astype(bf16)
    spread = as_bf16(onehot(idx_ref[:, 1:2], experts * CAP)) + as_bf16(onehot(idx_ref[:, 5:6], experts * CAP))
    dxn = dot(spread, ds[...])
    probs = probs_ref[...]
    gates, dgates, chosen = [], [], []
    for j in (0, 1):
        got = dot(as_bf16(onehot(idx_ref[:, 4 * j + 2:4 * j + 3], experts)), held)
        dgates.append(jnp.sum(jnp.where(onehot(idx_ref[:, 4 * j + 3:4 * j + 4], lanes), got, 0.0), axis=-1, keepdims=True))
        gates.append(gate_ref[:, j:j + 1])
        chosen.append(onehot(idx_ref[:, 4 * j:4 * j + 1], experts))
    mean = gates[0] * dgates[0] + gates[1] * dgates[1]
    scale = 1.0 / gate_ref[:, 2:3]
    dprobs = jnp.where(chosen[0], (dgates[0] - mean) * scale, 0.0) + jnp.where(chosen[1], (dgates[1] - mean) * scale, 0.0)
    dlogits = (probs * (dprobs - jnp.sum(probs * dprobs, axis=-1, keepdims=True))).astype(bf16)
    small_ref[...] = jnp.zeros_like(small_ref)
    small_ref[:, 0:experts] = dot(xn_ref[...], dlogits, TN).astype(bf16)
    dxn = dxn + dot(dlogits, router_ref[...], NT)
    h = h_ref[...]
    r = lax.rsqrt(jnp.mean(h * h, axis=-1, keepdims=True) + epsilon)
    gain_row = jnp.sum(dxn * h * r, axis=0, keepdims=True)
    small_ref[:, experts:experts + 1] = column_of(gain_row).astype(bf16)
    scaled = dxn * gains_ref[1:2, :]
    dh = cot_ref[...].astype(f32) + r * scaled - h * (r * r * r) * jnp.mean(h * scaled, axis=-1, keepdims=True)
    dh_ref[...] = dh
    dhb_ref[...] = dh.astype(bf16)


def back(idx, cot, h, xn, probs, gate, router, gains, blocks, size, chunks, deps):
    count, width = h.shape
    experts = router.shape[1]
    outs = [sd((count, width), f32), sd((count, width), bf16), sd((width, 128), bf16)]
    return call(functools.partial(back_kernel, size, chunks), "back", outs, (idx, cot, h, xn, probs, gate, router, gains, *blocks),
                scratch=[pltpu.VMEM((experts * CAP, width), bf16)], deps=deps)


def mix_kernel(count, chunks, idx_ref, h_ref, gate_ref, *refs):
    blocks, out_ref, ys = refs[:count], refs[count], refs[count + 1]
    rows_of = blocks[0].shape[0]
    part = rows_of // chunks
    for k, block in enumerate(blocks):
        for c in range(chunks):
            ys[(c * count + k) * part:(c * count + k + 1) * part, :] = block[c * part:(c + 1) * part, :]
    out = h_ref[...]
    for j in (0, 1):
        out = out + gate_ref[:, j:j + 1] * dot(as_bf16(onehot(idx_ref[:, 4 * j + 1:4 * j + 2], rows_of * count)), ys[...])
    out_ref[...] = out.astype(bf16)


def mix(idx, h, gate, blocks, size, chunks, deps):
    count, width = h.shape
    return call(functools.partial(mix_kernel, len(blocks), chunks), "mix", [sd((count, width), bf16)], (idx, h, gate, *blocks),
                scratch=[pltpu.VMEM((len(blocks) * blocks[0].shape[0], width), bf16)], deps=deps)[0]


def last_kernel(tokens_ref, dh_ref, own, rx, ry, rd, gains_ref, out_ref):
    x = tokens_ref[...].astype(f32)
    r = lax.rsqrt(jnp.mean(x * x, axis=-1, keepdims=True) + epsilon)
    scaled = add_terms((own, rx, ry, rd)) * gains_ref[0:1, :]
    out_ref[...] = dh_ref[...] + r * scaled - x * (r * r * r) * jnp.mean(x * scaled, axis=-1, keepdims=True)


def merge_kernel(size, at_ref, keep_ref, got_ref, *outs):
    me = at_ref[0]
    for k in range(size):
        to = (me + k) & (size - 1)
        outs[k][...] = (keep_ref[to].astype(f32) + got_ref[to].astype(f32)).astype(bf16)


def total_kernel(size, at_ref, q_ref, k_ref, v_ref, *refs):
    blocks, out_ref, few_ref = refs[:size], refs[size], refs[size + 1]
    total = sum(b[...].astype(f32) for b in blocks)
    out_ref[...] = total
    half = total.shape[0]
    width = q_ref.shape[1]
    few = total[:, 4 * width:]
    lane = lax.broadcasted_iota(i32, few.shape, 1)
    for r in (0, 1):
        @pl.when(at_ref[1] == r)
        def _():
            product = sum(total[:, n * width:(n + 1) * width] * ref[r * half:(r + 1) * half, :].astype(f32) for n, ref in enumerate((q_ref, k_ref, v_ref)))
            few_ref[...] = jnp.where(lane == TABLE - 1, jnp.sum(product, axis=1, keepdims=True), few)


def finish_kernel(at_ref, mine_ref, other_ref, few_mine, few_other, gain_ref, q_ref, k_ref, v_ref, o_ref, router_ref, table_ref, ga_ref, gm_ref, few):
    half = mine_ref.shape[0]
    width = q_ref.shape[1]
    experts = router_ref.shape[0]
    rows = table_ref.shape[1]

    def put(first, second, few_first, few_second):
        for n, ref in enumerate((q_ref, k_ref, v_ref, o_ref)):
            ref[0:half, :] = first[:, n * width:(n + 1) * width]
            ref[half:, :] = second[:, n * width:(n + 1) * width]
        few[0:half, :] = few_first[...]
        few[half:, :] = few_second[...]
        table_ref[...] = first[:, 4 * width:].T[TABLE + 1:TABLE + 1 + table_ref.shape[0], 0:rows]

    pl.when(at_ref[1] == 0)(lambda: put(mine_ref, other_ref, few_mine, few_other))
    pl.when(at_ref[1] == 1)(lambda: put(other_ref, mine_ref, few_other, few_mine))
    turned = few[...].T
    router_ref[...] = turned[0:experts, :]
    ga_ref[...] = turned[TABLE - 1:TABLE, :] / gain_ref[...].astype(f32)
    gm_ref[...] = turned[TABLE - 2:TABLE - 1, :]


def on_device(size, tokens, segments, routes, capacity, cotangent, rel_table, w_query, w_key, w_value, w_attn_out, gain_attn, gain_moe, w_router, w_in, w_out):
    z = lax.axis_index("expert").astype(i32)
    rep = lax.axis_index("rep").astype(i32)
    pos = lax.axis_index("tensor").astype(i32)
    at = jnp.stack([z, rep, pos])
    tok = tokens[0]
    cot = cotangent[0]
    count, width = tok.shape
    local = w_in.shape[0]
    experts = w_router.shape[1]
    chunks = 2 if local >= 4 else 1
    part = local // chunks
    rows_dev = w_query.shape[0]
    half = rows_dev // 2
    buckets = rel_table.shape[0] * size
    part_rows = part * CAP
    half_rows = part_rows * size // 2
    matrix = order_matrix(size, part, part_rows, 0, 0)

    packed, rest = call(pack_kernel, "pack", [sd((half, 896), bf16)] * 2,
                        (at, w_query, w_key, w_value, w_router.T, w_attn_out, gain_attn, gain_moe, rel_table.T),
                        scratch=[pltpu.VMEM((rows_dev, 896), f32)], smem=1)
    pieces = gather_pieces(tok, count // 2)
    idx = call(functools.partial(prepare_kernel, size, chunks), "prepare", [sd((count, 8), i32)], (z[None], routes[0].T, capacity[None]),
               smem=1, deps=(packed,))[0]

    g_blocks = spread(idx, cot, 0, size, local * CAP, (), "spread_g", chunks)
    mine = [after(to_expert(packed, k, size), g_blocks[0]) for k in range(1, size)]
    other = [to_core(m) for m in mine]
    g_blocks = [g_blocks[0]] + [after(b, *mine) for b in g_blocks[1:]]
    g_arrived = shifted(g_blocks)
    qkv_w, wo, router, gains, table = unpack(at, [packed, *mine], [rest, *other], buckets, pieces[1:3])

    xn, qkv = project(at, pieces, qkv_w, gains, tuple(g_blocks[1:]))
    o, lse, *parts = attn_fwd(at, table, qkv, segments, wo, ())
    g_ordered = call(functools.partial(reorder_all_kernel, size), "order_g", [sd((local * CAP * size, width), bf16)], (matrix, *g_arrived), deps=(o,))[0]
    terms = scatter_direct(parts[0], after(parts[1], g_ordered), parts[2], parts[3])
    terms = (*terms[:2], after(terms[2], gains), after(terms[3], gains))
    h, xn2, probs, gate, *blocks = route(idx, tok, terms, router, gains, size, chunks, ())
    g_pieces = gather_pieces(after(g_ordered, xn2), half_rows * chunks)

    arrived = shifted(blocks)
    ordered = [reorder(order_matrix(size, part, part_rows + 16, 16, 16), arrived, "order")]
    got = [gather_pieces(ordered[0], half_rows)]
    if chunks == 2:
        blocks = spread(idx, xn2, 1, size, part_rows, (ordered[0], *g_pieces[1:3]), "spread", 1)
        ordered.append(reorder(matrix, shifted(blocks), "order"))
        got.append(gather_direct(ordered[1]))
    extras = (*got[0][:3], got[0][4])
    ready = ordered[1:]

    step = max(part // 4, 1)
    pending = [(c, start) for c in range(chunks) for start in range(0, part, step)]
    grads = ()

    def expert_grads(many, *ready):
        nonlocal grads
        mark = ready[0]
        for c, start in pending[:many]:
            *grads, mark = expert_grad(at, c * part, start, step, local, acts[c], other_acts[c], grads, ready)
        del pending[:many]
        return mark

    acts, sums, ys = [], [], []
    dg_full = jnp.zeros((4, lanes_of(size) // 128, 16, 128), f32)
    for c in range(chunks):
        *outs, dg_full, act = moe(at, size, chunks, c, got[c], extras, g_pieces, w_in, w_out, dg_full, () if c else ready)
        sums.append(scatter_direct(*outs[:4]) if c < chunks - 1 else outs[:4])
        ys.append(outs[4:])
        acts.append(act)
    other_acts = [to_core(acts[0])]


    def give(c, extra, deps):
        given = call(functools.partial(give_back_kernel, size, extra), "give_back", [sd((part_rows + 16 * extra, width), bf16)] * size,
                     (matrix, *sums[c]), deps=deps)
        return given[0], [given[0]] + [to_expert(given[k], size - k, size) for k in range(1, size)]

    outs = list(sums[-1])
    if chunks == 2:
        outs = [*outs[:1], *[after(piece, *sums[0][1:]) for piece in outs[1:4]]]
    sums[-1] = scatter_direct(*outs)
    back_blocks = []
    mark = outs[0]
    if chunks == 2:
        mark, back_blocks = give(0, False, (mark,))
    mark = expert_grads(1, mark)
    mark = expert_grads(1, mark, *back_blocks[1:])
    ready, blocks = give(chunks - 1, True, (mark,))
    if chunks == 2:
        y_packs = [after(ys[c][1], mark, *sums[-1][1:]) for c in (0, 1)]
        y_got = [to_tensor(pack, flip) for flip, pack in zip((1, 2), y_packs)]
    else:
        y_terms = scatter_direct(*ys[0])
    ready = (expert_grads(1, ready), *y_packs) if chunks == 2 else (ready,)
    dh, dhb, small = back(idx, cot, h, xn2, probs, gate, router, gains, back_blocks + blocks, size, chunks, ready)
    dh_pieces = gather_direct(dhb)
    mark = expert_grads(1, dhb)
    if chunks == 2:
        acts[1] = after(acts[1], mark)
        other_acts.append(to_core(acts[1]))
    if chunks == 2:
        y_parts, sent = scatter_end(*y_got, ys[1][2], ys[0][2], (mark,))
        mark = sent[0]

    y_late = (y_parts[1], y_parts[3]) if chunks == 2 else ()
    gtab, dqkv = attn_bwd(at, size, table, dh_pieces, segments, wo, qkv, lse, (mark,))
    keep, send, own, *parts = attn_grad(at, size, dqkv, qkv_w, xn, dh_pieces, o, small, gtab, y_late)
    terms = scatter_direct(own, *parts)
    got = to_core(send)
    out_blocks = call(functools.partial(merge_kernel, size), "merge", [sd((half, packed.shape[1]), bf16)] * size,
                      (at, keep, got), smem=1, deps=other_acts[1:])
    outs = [sd((local * CAP, width), bf16)] * size
    if chunks == 2:
        given = call(functools.partial(give_back_halves_kernel, size), "give_back_y", outs, (matrix, ys[0][0], ys[1][0], *y_parts), deps=(out_blocks[0],))
    else:
        given = call(functools.partial(give_back_kernel, size, False), "give_back_y", outs, (matrix, *y_terms), deps=(out_blocks[0],))
    y_blocks = [given[0]] + [to_expert(given[k], size - k, size) for k in range(1, size)]
    grad_tokens = call(last_kernel, "last", [sd((count, width), f32)], (tok, dh, *terms, gains))[0]
    mark = expert_grads(1, out_blocks[0], given[0])
    mark = expert_grads(max(len(pending) - 2, 0), mark, *terms[1:])
    total, gain = call(functools.partial(total_kernel, size), "total", [sd(out_blocks[0].shape, f32), sd((half, 128), f32)],
                       (at, w_query, w_key, w_value, *shifted(out_blocks)), smem=1, deps=(mark, *terms[1:]))
    mark = expert_grads(1, total)
    gain = gain + to_tensor(gain, 1)
    mark = expert_grads(len(pending), mark, gain)
    gain = gain + to_tensor(gain, 2)
    output = mix(idx, h, gate, y_blocks, size, chunks, (mark,))
    lw = w_query.shape[1]
    outs = [sd((rows_dev, lw), f32)] * 4 + [sd((experts, rows_dev), f32), sd(rel_table.T.shape, f32)] + [sd((1, rows_dev), f32)] * 2
    grad_q, grad_k, grad_v, grad_o, grad_router, grad_table, grad_ga, grad_gm = call(
        finish_kernel, "finish", outs, (at, total, to_core(total), gain, to_core(gain), gain_attn[None]), smem=1, scratch=[pltpu.VMEM((rows_dev, 128), f32)], deps=(output, mark))
    return (output[None], grad_tokens[None], grad_table.T, grad_q, grad_k, grad_v, grad_o, grad_ga[0], grad_gm[0], grad_router.T, *grads)


def solution(mesh):
    by_token = P(("expert", "rep"), "tensor", None)
    both = P("expert", "tensor")
    return jax.shard_map(
        functools.partial(on_device, mesh.shape["expert"]),
        mesh=mesh,
        in_specs=(by_token, P(("expert", "rep"), None), by_token, P(), by_token, both, both, both, both, both, P("expert"), P("expert"),
                  P("expert", None), P("expert", None, "tensor"), P("expert", "tensor", None)),
        out_specs=(by_token, by_token, both, both, both, both, both, P("expert"), P("expert"), P("expert", None),
                   P("expert", None, "tensor"), P("expert", "tensor", None)),
        check_vma=False,
    )
```
